128 devices in a mesh: blk: 4 (over z), owner: 32 (over x, y, core).
Axes of the slice: x: 4, y: 4, z: 4, core: 2. Of those that a mesh axis runs over, the one named last changes fastest.
Arguments:
- embed: bfloat16 [32768, 4096], P(('blk', 'owner')), may hold values from -8 to 8
- group: int32 [32768, 1], P(('blk', 'owner')), may hold values from 0 to 31; in each aligned block of 256 rows (0 to 255, 256 to 511, ...) at most 24 rows name the same one
- half: int32 [32768], P(('blk', 'owner')), may hold values from 0 to 1
Outputs:
- nearest: float32 [32768], P(('blk', 'owner'))
The draws below stay inside these ranges and needn't reach their ends.
Inputs may be any that keep to these rules, and one draw needn't show every extreme that they name: The 256 documents of one device name one owner group at most 24 times; in every draw some device names some group exactly 24 times. Every cluster, a value of 2 * group + half, holds two or more documents.
All inputs are finite; a program needn't handle non-finite values.
Results may differ from the reference program's by a relative error of at most 0.00046.
Values may be sent and summed in bfloat16 or wider, within the bound.
No kernel may reach another device: no remote copies, remote signals or barrier semaphores. Data moves between devices by JAX's collectives and lax.ppermute only.
A program may use at most 128 MiB of HBM per device.

```python
import math
import jax
import jax.numpy as jnp
import numpy as np
from jax import lax

D = 4096
DOC_DEV = 256
DOCS = 32768
CAP = 24
N_OWNER = 32
DEVICES = 128


def draw_embed(key, part):
    key = jax.random.fold_in(key, 11)
    key_topic = jax.random.fold_in(key, 0)
    key_table = jax.random.fold_in(key, 2)
    key_noise = jax.random.fold_in(key, 3)
    topics = max(DOCS // 64, 1)
    topic = jax.random.randint(key_topic, (DOCS,), 0, topics)
    table = jnp.clip(jax.random.normal(key_table, (topics, D), jnp.float32), -4.0, 4.0)
    noise = jnp.clip(jax.random.normal(key_noise, (DOCS, D), jnp.float32), -4.0, 4.0)
    return (noise + 0.8 * table[topic]).astype(jnp.bfloat16)


def place_ends(array, stream_key, least, top_value):
    spot = [jax.random.randint(jax.random.fold_in(stream_key, axis), (), 0, length) for axis, length in enumerate(array.shape)]
    main_axis = array.shape.index(max(array.shape))
    neighbour = spot[:main_axis] + [(spot[main_axis] + 1) % array.shape[main_axis]] + spot[main_axis + 1:]
    return array.at[tuple(spot)].set(least).at[tuple(neighbour)].set(top_value)


def assign_block(own_key, own, number, rows, number_of, top, most, slope):
    order = jax.random.permutation(own_key, number_of)
    packed, ordinary = load_shares(number_of, rows * top, most, slope, True), load_shares(number_of, rows * top, most, slope, False)
    places = jnp.arange(number_of)

    def named(lengths, rotation):
        used = int((lengths > 0).sum())
        fixed = max(1, used // 4)
        shifted = fixed + (places - fixed + rotation * (used - fixed)) % max(1, number_of - fixed)
        return jnp.zeros((number_of,), jnp.int32).at[order[jnp.where(places < fixed, places, shifted)]].set(jnp.asarray(lengths, jnp.int32))

    lengths = jnp.where(number % 4 == 0, named(packed, number // 4), named(ordinary, number - number // 4 - 1))
    mixed = jax.random.permutation(jax.random.fold_in(own, 3), number_of)
    donor, sink = mixed[0:number_of // 2 * 2:2], mixed[1:number_of // 2 * 2:2]
    margin = jnp.minimum(lengths[donor] - 1, most - lengths[sink]) // 2
    margin = jnp.where((donor == order[0]) | (sink == order[0]) | (lengths[sink] == 0), 0, jnp.maximum(margin, 0))
    shifted = jax.random.randint(jax.random.fold_in(own, 4), (number_of // 2,), 0, 1 << 20) % (margin + 1)
    lengths = lengths.at[donor].add(-shifted).at[sink].add(shifted)
    items = jnp.searchsorted(jnp.cumsum(lengths), jnp.arange(rows * top), side="right").astype(jnp.int32)
    grid = items.reshape(top, rows).T
    grid = grid[jax.random.permutation(jax.random.fold_in(own, 1), rows)]
    rotation = jax.random.randint(jax.random.fold_in(own, 2), (rows, 1), 0, top)
    return jnp.take_along_axis(grid, (jnp.arange(top)[None, :] + rotation) % top, axis=1)


def load_shares(number_of, total, most, skew, full):
    loads = [(1 << 20) // math.isqrt(standing ** skew) + 1 for standing in range(1, number_of + 1)]
    largest = most if full else min(most, max(-(-total // number_of), total * loads[0] // sum(loads)))
    least = 1 if total - largest >= number_of - 1 else 0
    given, surplus = [largest] + [least] * (number_of - 1), total - largest - least * (number_of - 1)
    while surplus > 0:
        movable = [i for i in range(1, number_of) if given[i] < largest] or [i for i in range(1, number_of) if given[i] < most]
        mass, budget = sum([loads[i] for i in movable]), surplus
        for i in movable:
            extra = min(most - given[i], max(1, budget * loads[i] // mass), surplus)
            given[i] = given[i] + extra
            surplus = surplus - extra
    return np.array(given)


def setup_inputs(seed: int = 0) -> dict:
    seeds = jax.random.split(jax.random.key(seed), 4)
    embed = draw_embed(jax.random.fold_in(seeds[3], 71), 0)
    group_keys = jax.random.split(jax.random.fold_in(seeds[1], 1), DOCS // DOC_DEV)
    group_turns = jax.random.permutation(jax.random.fold_in(seeds[1], 3), DOCS // DOC_DEV)
    group = jax.vmap(lambda own, number: assign_block(jax.random.fold_in(seeds[1], 2), own, number, DOC_DEV, N_OWNER, 1, CAP, 1))(group_keys, group_turns).reshape((DOCS, 1))
    half = place_ends(jax.random.randint(seeds[2], (DOCS,), 0, 2), jax.random.fold_in(seeds[2], 1), 0, 1).astype(jnp.int32)
    return {"embed": embed, "group": group, "half": half}


def reference(embed, group, half):
    floats = embed.astype(jnp.float32)
    unit = (floats * lax.rsqrt(lax.optimization_barrier(jnp.sum(floats * floats, axis=1, keepdims=True)) + 1e-06)).astype(jnp.bfloat16)
    target = group[:, 0].astype(jnp.int32)
    order = jnp.argsort(target, stable=True).astype(jnp.int32)
    counts = lax.optimization_barrier(jnp.sum((target[:, None] == jnp.arange(N_OWNER, dtype=jnp.int32)[None, :]).astype(jnp.int32), axis=0)).astype(jnp.int32)
    starts = (jnp.cumsum(counts) - counts).astype(jnp.int32)
    span = CAP * DEVICES
    padded_order = jnp.concatenate([order, jnp.full((span,), DOCS, jnp.int32)]).astype(jnp.int32)
    unit_pad = jnp.concatenate([unit, jnp.zeros((1, D), jnp.bfloat16)], axis=0)
    half_pad = jnp.concatenate([half.astype(jnp.int32), jnp.full((1,), -1, jnp.int32)]).astype(jnp.int32)
    diagonal = jnp.eye(span, dtype=bool)

    def one_group(index):
        members = lax.dynamic_slice_in_dim(padded_order, starts[index], span)
        valid = jnp.arange(span) < counts[index]
        rows = unit_pad[members].astype(jnp.float32)
        labels = jnp.where(valid, half_pad[members], -1)
        scores = jnp.dot(rows, rows.T, precision=lax.Precision.HIGHEST)
        keep = (labels[:, None] == labels[None, :]) & (labels[None, :] >= 0) & ~diagonal
        best = lax.optimization_barrier(jnp.max(jnp.where(keep, scores, -2.0), axis=1))
        return (jnp.where(valid, members, DOCS).astype(jnp.int32), best)
    places, bests = lax.map(one_group, jnp.arange(N_OWNER, dtype=jnp.int32))
    result = jnp.zeros((DOCS + 1,), jnp.float32).at[places.reshape(-1)].set(bests.reshape(-1).astype(jnp.float32))
    return result[:DOCS]
```

```python
import functools

import jax
import jax.numpy as jnp
from jax import lax
from jax.experimental import pallas as pl
from jax.experimental.pallas import tpu as pltpu
from jax.sharding import Mesh, PartitionSpec as P

WIDTH = 4096
HALFW = WIDTH // 2
CHIPS = 64
DOCS = 256
CAP = 24
SIDE = 12
HEAD = 8
ROWS = CHIPS * HEAD
TAIL = CHIPS * (SIDE - HEAD)
META = WIDTH + HALFW
SENT = META + 128
CHIP_AXES = ("z", "xyh", "yl")
ALL_AXES = CHIP_AXES + ("core",)
F32 = jnp.float32
BF16 = jnp.bfloat16
VMEM_LIMIT = 56 * 1024 * 1024


def iota(shape, axis):
    return lax.broadcasted_iota(jnp.int32, shape, axis)


def dot(a, b):
    return jnp.dot(a, b, preferred_element_type=F32)


def dot_t(a, b):
    return lax.dot_general(a, b, (((1,), (1,)), ((), ())), preferred_element_type=F32)


def onehot(mask):
    return jnp.where(mask, 1.0, 0.0).astype(BF16)


def split3(x):
    a = x.astype(BF16)
    rest = x - a.astype(F32)
    b = rest.astype(BF16)
    c = (rest - b.astype(F32)).astype(BF16)
    return a, b, c


def send_kernel(embed_ref, group_ref, half_ref, out_ref, rank_ref, count_ref, unit_ref, slot_ref, meta_ref):
    step = pl.program_id(0)

    @pl.when(step == 0)
    def _():
        floats = embed_ref[...].astype(F32)
        scale = lax.rsqrt(jnp.sum(floats * floats, axis=1, keepdims=True) + 1e-06)
        unit_ref[...] = (floats * scale).astype(BF16)
        cluster = 2 * group_ref[...] + half_ref[...]
        other = cluster + 1 - 2 * half_ref[...]
        member = iota((CHIPS, DOCS), 0) == cluster
        earlier = onehot(iota((DOCS, DOCS), 0) < iota((DOCS, DOCS), 1))
        before = dot(onehot(member), earlier)
        rank = jnp.sum(jnp.where(member, before, 0.0), axis=0, keepdims=True).astype(jnp.int32)
        over = rank >= SIDE
        chip = jnp.where(over, other, cluster)
        row = jnp.where(over, CAP - 1 - rank, rank)
        slot_ref[0:1, :] = jnp.where(row < HEAD, chip * HEAD + row, -1)
        slot_ref[1:2, :] = jnp.where(row >= HEAD, chip * HEAD + row - HEAD, -1)
        slot_ref[2:3, :] = jnp.where(row >= HEAD, chip * HEAD + row - HEAD + 4, -1)
        rank_ref[0:1, :] = rank
        rank_ref[1:2, :] = cluster
        own = jnp.sum(jnp.where(member, 1.0, 0.0), axis=1, keepdims=True)
        oth = jnp.sum(jnp.where(iota((CHIPS, DOCS), 0) == other, 1.0, 0.0), axis=1, keepdims=True)
        lane = iota((CHIPS, 128), 1)
        meta = jnp.where(lane == 0, own, jnp.where(lane == 1, oth, 0.0))
        count_ref[...] = meta
        meta_ref[...] = jnp.broadcast_to(meta[:, None, :], (CHIPS, HEAD, 128)).reshape(ROWS, 128)

    rows = out_ref.shape[0]
    base = step * rows
    here = iota((rows, DOCS), 0) + base
    head = onehot(here == slot_ref[0:1, :])
    left = onehot(here == slot_ref[1:2, :])
    right = onehot(here == slot_ref[2:3, :])
    out_ref[:, :WIDTH] = dot(head, unit_ref[...]).astype(BF16)
    out_ref[:, WIDTH:META] = (dot(left, unit_ref[:, :HALFW]) + dot(right, unit_ref[:, HALFW:])).astype(BF16)
    out_ref[:, META:] = meta_ref[pl.ds(pl.multiple_of(base, rows), rows), :].astype(BF16)


def place_documents(embed, group, half):
    steps = 4
    whole = lambda shape: pl.BlockSpec(shape, lambda i: (0, 0))
    return pl.pallas_call(
        send_kernel,
        grid=(steps,),
        in_specs=[whole((DOCS, WIDTH)), whole((1, DOCS)), whole((1, DOCS))],
        out_specs=[pl.BlockSpec((ROWS // steps, SENT), lambda i: (i, 0)), whole((8, DOCS)), whole((CHIPS, 128))],
        out_shape=[
            jax.ShapeDtypeStruct((ROWS, SENT), BF16),
            jax.ShapeDtypeStruct((8, DOCS), jnp.int32),
            jax.ShapeDtypeStruct((CHIPS, 128), F32),
        ],
        scratch_shapes=[
            pltpu.VMEM((DOCS, WIDTH), BF16),
            pltpu.VMEM((8, DOCS), jnp.int32),
            pltpu.VMEM((ROWS, 128), F32),
        ],
        compiler_params=pltpu.CompilerParams(vmem_limit_bytes=VMEM_LIMIT),
        cost_estimate=pl.CostEstimate(flops=2 * 10**9, bytes_accessed=9 * 2**20, transcendentals=256),
        name="place_documents",
    )(embed, group, half)


def tail_rows(y_ref):
    to = iota((TAIL, ROWS), 0)
    at = iota((TAIL, ROWS), 1)
    want = (to % CHIPS) * HEAD + to // CHIPS
    left = dot(onehot(at == want), y_ref[:, WIDTH:META]).astype(BF16)
    right = dot(onehot(at == want + 4), y_ref[:, WIDTH:META]).astype(BF16)
    return left, right


def lane_counts(y_ref):
    meta = y_ref[:, META:].astype(F32).T[:8, :]
    pick = onehot(iota((ROWS, TAIL), 0) == (iota((ROWS, TAIL), 1) % CHIPS) * HEAD)
    tail = dot(meta.astype(BF16), pick)
    return meta[0:1, :], meta[1:2, :], tail[0:1, :], tail[1:2, :]


def pack_kernel(y_ref, x2_ref, v_ref):
    room = v_ref.shape[0]
    left, right = tail_rows(y_ref)
    x2_ref[:, :HALFW] = left
    x2_ref[:, HALFW:] = right
    _, oth1, _, oth2 = lane_counts(y_ref)
    row1 = iota((1, ROWS), 1) % HEAD
    row2 = iota((1, TAIL), 1) // CHIPS + HEAD
    over1 = row1.astype(F32) >= CAP - oth1
    over2 = row2.astype(F32) >= CAP - oth2
    before1 = onehot(iota((ROWS, ROWS), 0) < iota((ROWS, ROWS), 1))
    before2 = onehot(iota((TAIL, TAIL), 0) < iota((TAIL, TAIL), 1))
    flag1 = jnp.where(over1, 1.0, 0.0)
    flag2 = jnp.where(over2, 1.0, 0.0)
    place1 = dot(jnp.broadcast_to(flag1, (8, ROWS)).astype(BF16), before1)[0:1, :]
    place2 = dot(jnp.broadcast_to(flag2, (8, TAIL)).astype(BF16), before2)[0:1, :]
    place2 = place2 + jnp.sum(flag1, axis=1, keepdims=True)
    take1 = onehot((iota((room, ROWS), 0) == place1.astype(jnp.int32)) & over1)
    take2 = onehot((iota((room, TAIL), 0) == place2.astype(jnp.int32)) & over2)
    v_ref[:, :WIDTH] = (dot(take1, y_ref[:, :WIDTH]) + dot(take2, x2_ref[...])).astype(BF16)

    def about(source, row):
        lane = iota(source.shape, 1)
        rank = CAP - 1 - row
        return jnp.where(lane == 0, source, jnp.where(lane == 1, rank, jnp.where(lane == 2, 1, 0))).astype(F32).astype(BF16)

    at1 = iota((ROWS, 128), 0)
    at2 = iota((TAIL, 128), 0)
    info = dot(take1, about(at1 // HEAD, at1 % HEAD)) + dot(take2, about(at2 % CHIPS, at2 // CHIPS + HEAD))
    v_ref[:, WIDTH:] = info.astype(BF16)


def pack(y, room):
    return pl.pallas_call(
        pack_kernel,
        out_shape=[jax.ShapeDtypeStruct((TAIL, WIDTH), BF16), jax.ShapeDtypeStruct((room, WIDTH + 128), BF16)],
        compiler_params=pltpu.CompilerParams(vmem_limit_bytes=VMEM_LIMIT),
        cost_estimate=pl.CostEstimate(flops=3 * 10**9, bytes_accessed=12 * 2**20, transcendentals=0),
        name="pack_overflow",
    )(y)


def best_to_slots(best, block):
    lane = iota((256, 128), 1)
    at = iota((256, 128), 0)
    if block < 2:
        return jnp.max(jnp.where(lane == at % HEAD, best, -2.0).reshape(32, HEAD, 128), axis=1)
    return jnp.max(jnp.where(lane == at // CHIPS + HEAD, best, -2.0).reshape(4, CHIPS, 128), axis=0)


def own_valid(y_ref):
    own1, _, own2, _ = lane_counts(y_ref)
    ok1 = (iota((1, ROWS), 1) % HEAD).astype(F32) < own1
    ok2 = (iota((1, TAIL), 1) // CHIPS + HEAD).astype(F32) < own2
    return [ok1[:, :256], ok1[:, 256:], ok2]


def row_block(y_ref, x2_ref, block):
    return y_ref[256 * block : 256 * (block + 1), :WIDTH] if block < 2 else x2_ref[...]


def own_kernel(y_ref, x2_ref, best_ref):
    ok = own_valid(y_ref)
    same = iota((256, 256), 0) == iota((256, 256), 1)
    for a in range(3):
        mine = row_block(y_ref, x2_ref, a)
        top = jnp.full((256, 256), -2.0, F32)
        for b in range(3):
            scores = dot_t(mine, row_block(y_ref, x2_ref, b))
            keep = ok[b] & ~same if a == b else ok[b]
            top = jnp.maximum(top, jnp.where(keep, scores, -2.0))
        best_ref[256 * a : 256 * (a + 1), :] = jnp.broadcast_to(jnp.max(top, axis=1, keepdims=True), (256, 128))


def own_pairs(y, x2):
    return pl.pallas_call(
        own_kernel,
        out_shape=jax.ShapeDtypeStruct((ROWS + TAIL, 128), F32),
        compiler_params=pltpu.CompilerParams(vmem_limit_bytes=VMEM_LIMIT),
        cost_estimate=pl.CostEstimate(flops=5 * 10**9, bytes_accessed=9 * 2**20, transcendentals=0),
        name="own_pairs",
    )(y, x2)


def cross_kernel(y_ref, x2_ref, s_ref, so_far_ref, best_ref, s2_ref):
    left, right = tail_rows(s_ref)
    s2_ref[:, :HALFW] = left
    s2_ref[:, HALFW:] = right
    ok = own_valid(s_ref)
    for a in range(3):
        mine = row_block(y_ref, x2_ref, a)
        top = jnp.full((256, 256), -2.0, F32)
        for b in range(3):
            scores = dot_t(mine, row_block(s_ref, s2_ref, b))
            top = jnp.maximum(top, jnp.where(ok[b], scores, -2.0))
        best_ref[256 * a : 256 * (a + 1), :] = jnp.maximum(
            so_far_ref[256 * a : 256 * (a + 1), :], jnp.max(top, axis=1, keepdims=True)
        )


def cross_pairs(y, x2, s, so_far):
    return pl.pallas_call(
        cross_kernel,
        out_shape=[jax.ShapeDtypeStruct((ROWS + TAIL, 128), F32), jax.ShapeDtypeStruct((TAIL, WIDTH), BF16)],
        compiler_params=pltpu.CompilerParams(vmem_limit_bytes=VMEM_LIMIT),
        cost_estimate=pl.CostEstimate(flops=6 * 10**9, bytes_accessed=17 * 2**20, transcendentals=0),
        name="cross_pairs",
    )(y, x2, s, so_far)


def last_kernel(y_ref, x2_ref, s_ref, s2_ref, v_ref, w_ref, so_far_ref, out_ref, over_ref):
    room = v_ref.shape[0]
    tile = min(room, 256)
    about_v = v_ref[:, WIDTH:].astype(F32).T
    about_w = w_ref[:, WIDTH:].astype(F32).T
    ok_v = about_v[2:3, :] > 0.5
    ok_w = about_w[2:3, :] > 0.5
    ok_y = own_valid(y_ref)
    ok_s = own_valid(s_ref)
    result = jnp.full((CHIPS, 128), -2.0, F32)
    parts = []
    for a in range(3):
        mine = row_block(y_ref, x2_ref, a)
        top = so_far_ref[256 * a : 256 * (a + 1), 0:1]
        for start in range(0, room, tile):
            span = slice(start, start + tile)
            for ref, ok in ((v_ref, ok_v), (w_ref, ok_w)):
                scores = jnp.where(ok[:, span], dot_t(mine, ref[span, :WIDTH]), -2.0)
                top = jnp.maximum(top, jnp.max(scores, axis=1, keepdims=True))
        parts.append(best_to_slots(top, a))
    out_ref[...] = jnp.maximum(jnp.concatenate(parts[:2], axis=0), parts[2])
    for start in range(0, room, tile):
        span = slice(start, start + tile)
        mine = v_ref[span, :WIDTH]
        top = jnp.full((tile, 1), -2.0, F32)
        for b in range(3):
            for ref, ref2, ok in ((y_ref, x2_ref, ok_y), (s_ref, s2_ref, ok_s)):
                scores = jnp.where(ok[b], dot_t(mine, row_block(ref, ref2, b)), -2.0)
                top = jnp.maximum(top, jnp.max(scores, axis=1, keepdims=True))
        for other in range(0, room, tile):
            at = slice(other, other + tile)
            keep = ok_v[:, at]
            if other == start:
                keep = keep & (iota((tile, tile), 0) != iota((tile, tile), 1))
            scores = jnp.where(keep, dot_t(mine, v_ref[at, :WIDTH]), -2.0)
            top = jnp.maximum(top, jnp.max(scores, axis=1, keepdims=True))
            scores = jnp.where(ok_w[:, at], dot_t(mine, w_ref[at, :WIDTH]), -2.0)
            top = jnp.maximum(top, jnp.max(scores, axis=1, keepdims=True))
        over_ref[span, :] = jnp.broadcast_to(top, (tile, 128))
    source = onehot((iota((CHIPS, room), 0) == about_v[0:1, :].astype(jnp.int32)) & ok_v)
    info = v_ref[:, WIDTH:].astype(F32)
    rank = (iota((room, 128), 1) == info[:, 1:2].astype(jnp.int32)) & (info[:, 2:3] > 0.5)
    placed = jnp.zeros((CHIPS, 128), F32)
    for piece in split3(jnp.where(rank, over_ref[...], 0.0)):
        placed = placed + dot(source, piece)
    filled = dot(source, onehot(rank))
    out_ref[...] = jnp.where(filled > 0.5, placed, out_ref[...])


def last_pairs(y, x2, s, s2, v, w, so_far):
    room = v.shape[0]
    return pl.pallas_call(
        last_kernel,
        out_shape=jax.ShapeDtypeStruct((CHIPS, 128), F32),
        scratch_shapes=[pltpu.VMEM((room, 128), F32)],
        compiler_params=pltpu.CompilerParams(vmem_limit_bytes=VMEM_LIMIT),
        cost_estimate=pl.CostEstimate(
            flops=2 * WIDTH * room * (2 * 768 + 1536 + 2 * room), bytes_accessed=20 * 2**20, transcendentals=0
        ),
        name="overflow_pairs",
    )(y, x2, s, s2, v, w, so_far)


def owner_side(room, y):
    swap = [(0, 1), (1, 0)]
    s = lax.ppermute(y, "core", swap)
    x2, v = pack(y, room)
    v = lax.ppermute(v, "yl", swap)
    w = lax.ppermute(v, "core", swap)
    best = own_pairs(y, x2)
    best, s2 = cross_pairs(y, x2, s, best)
    return last_pairs(y, x2, s, s2, v, w, best)


def pick_kernel(back_ref, rank_ref, out_ref):
    rank = rank_ref[0:1, :]
    cluster = rank_ref[1:2, :]
    at_rank = onehot(iota((128, DOCS), 0) == rank)
    found = jnp.zeros((CHIPS, DOCS), F32)
    for piece in split3(back_ref[...]):
        found = found + dot(piece, at_rank)
    out_ref[...] = jnp.sum(jnp.where(iota((CHIPS, DOCS), 0) == cluster, found, 0.0), axis=0, keepdims=True)


def pick(back, rank):
    return pl.pallas_call(
        pick_kernel,
        out_shape=jax.ShapeDtypeStruct((1, DOCS), F32),
        compiler_params=pltpu.CompilerParams(vmem_limit_bytes=VMEM_LIMIT),
        name="pick_documents",
    )(back, rank)


def on_device(embed, group, half):
    sent, rank, count = place_documents(embed, group.reshape(1, DOCS), half.reshape(1, DOCS))
    room = 128
    over = jnp.maximum(count[:, 0] - SIDE, 0.0)
    mine = (jnp.arange(2)[:, None] == lax.axis_index("core")).astype(F32)
    totals = lax.psum((mine * over[None, :]).reshape(2 * CHIPS), ALL_AXES)
    y = lax.all_to_all(sent, CHIP_AXES, split_axis=0, concat_axis=0, tiled=True)
    best = lax.cond(
        jnp.max(totals) > room,
        functools.partial(owner_side, ROWS + TAIL),
        functools.partial(owner_side, room),
        y,
    )
    back = lax.all_to_all(best, CHIP_AXES, split_axis=0, concat_axis=0, tiled=True)
    return pick(back, rank).reshape(DOCS)


def solution(mesh):
    devices = mesh.devices.reshape(4, 8, 2, 2)
    fine = Mesh(devices, ALL_AXES)
    return jax.shard_map(
        on_device,
        mesh=fine,
        in_specs=(P(ALL_AXES, None), P(ALL_AXES, None), P(ALL_AXES)),
        out_specs=P(ALL_AXES),
        check_vma=False,
    )
```

```python
import jax
import jax.numpy as jnp
from jax import lax
from jax.experimental import pallas as pl
from jax.experimental.pallas import tpu as pltpu
from jax.sharding import Mesh, PartitionSpec as P

WIDTH = 4096
HALFW = WIDTH // 2
CHIPS = 64
DOCS = 256
CAP = 24
SIDE = 12
HEAD = 8
PARTS = 4
ROWS = CHIPS * HEAD
TAIL = CHIPS * (SIDE - HEAD)
META = WIDTH + HALFW
SENT = META + 128
CHIP_AXES = ("z", "xyh", "yl")
ALL_AXES = CHIP_AXES + ("core",)
F32 = jnp.float32
BF16 = jnp.bfloat16
MIB = 1024 * 1024
ROOM = 64


def iota(shape, axis):
    return lax.broadcasted_iota(jnp.int32, shape, axis)


def dot(a, b):
    return jnp.dot(a, b, preferred_element_type=F32)


def dot_t(a, b):
    return lax.dot_general(a, b, (((1,), (1,)), ((), ())), preferred_element_type=F32)


def onehot(mask):
    return jnp.where(mask, 1.0, 0.0).astype(BF16)


def split3(x):
    a = x.astype(BF16)
    rest = x - a.astype(F32)
    b = rest.astype(BF16)
    c = (rest - b.astype(F32)).astype(BF16)
    return a, b, c


def send_kernel(embed_hbm, group_hbm, half_hbm, out_ref, rank_ref, embed_ref, group_ref, half_ref, unit_ref, slot_ref, meta_ref, sems):
    step = pl.program_id(0)

    @pl.when(step == 0)
    def _():
        names = [pltpu.make_async_copy(group_hbm, group_ref, sems.at[0]), pltpu.make_async_copy(half_hbm, half_ref, sems.at[1])]
        size = DOCS // PARTS
        spans = [pl.ds(size * part, size) for part in range(PARTS)]
        parts = [pltpu.make_async_copy(embed_hbm.at[span, :], embed_ref.at[span, :], sems.at[2 + i]) for i, span in enumerate(spans)]
        for copy in names + parts:
            copy.start()
        for copy in names:
            copy.wait()
        cluster = 2 * group_ref[...] + half_ref[...]
        other = cluster + 1 - 2 * half_ref[...]
        member = iota((CHIPS, DOCS), 0) == cluster
        earlier = onehot(iota((DOCS, DOCS), 0) < iota((DOCS, DOCS), 1))
        before = dot(onehot(member), earlier)
        rank = jnp.sum(jnp.where(member, before, 0.0), axis=0, keepdims=True).astype(jnp.int32)
        over = rank >= SIDE
        chip = jnp.where(over, other, cluster)
        row = jnp.where(over, CAP - 1 - rank, rank)
        slot_ref[0:1, :] = jnp.where(row < HEAD, chip * HEAD + row, -1)
        slot_ref[1:2, :] = jnp.where(row >= HEAD, chip * HEAD + row - HEAD, -1)
        slot_ref[2:3, :] = jnp.where(row >= HEAD, chip * HEAD + row - HEAD + 4, -1)
        rank_ref[0:1, :] = rank
        rank_ref[1:2, :] = cluster
        own = jnp.sum(jnp.where(member, 1.0, 0.0), axis=1, keepdims=True)
        oth = jnp.sum(jnp.where(iota((CHIPS, DOCS), 0) == other, 1.0, 0.0), axis=1, keepdims=True)
        lane = iota((CHIPS, 128), 1)
        meta = jnp.where(lane == 0, own, jnp.where(lane == 1, oth, 0.0))
        meta_ref[...] = jnp.broadcast_to(meta[:, None, :], (CHIPS, HEAD, 128)).reshape(ROWS, 128)
        for copy, span in zip(parts, spans):
            copy.wait()
            floats = embed_ref[span, :].astype(F32)
            scale = lax.rsqrt(jnp.sum(floats * floats, axis=1, keepdims=True) + 1e-06)
            unit_ref[span, :] = (floats * scale).astype(BF16)

    rows = out_ref.shape[0]
    base = step * rows
    here = iota((rows, DOCS), 0) + base
    head = onehot(here == slot_ref[0:1, :])
    left = onehot(here == slot_ref[1:2, :])
    right = onehot(here == slot_ref[2:3, :])
    out_ref[:, :WIDTH] = dot(head, unit_ref[...]).astype(BF16)
    out_ref[:, WIDTH:META] = (dot(left, unit_ref[:, :HALFW]) + dot(right, unit_ref[:, HALFW:])).astype(BF16)
    out_ref[:, META:] = meta_ref[pl.ds(pl.multiple_of(base, rows), rows), :].astype(BF16)


def place_documents(embed, group, half):
    steps = 4
    far = pl.BlockSpec(memory_space=pltpu.HBM)
    operands = [pltpu.with_memory_space_constraint(x, pltpu.HBM) for x in (embed, group, half)]
    return pl.pallas_call(
        send_kernel,
        grid=(steps,),
        in_specs=[far, far, far],
        out_specs=[pl.BlockSpec((ROWS // steps, SENT), lambda i: (i, 0)), pl.BlockSpec((8, DOCS), lambda i: (0, 0))],
        out_shape=[jax.ShapeDtypeStruct((ROWS, SENT), BF16), jax.ShapeDtypeStruct((8, DOCS), jnp.int32)],
        scratch_shapes=[
            pltpu.VMEM((DOCS, WIDTH), BF16),
            pltpu.VMEM((1, DOCS), jnp.int32),
            pltpu.VMEM((1, DOCS), jnp.int32),
            pltpu.VMEM((DOCS, WIDTH), BF16),
            pltpu.VMEM((8, DOCS), jnp.int32),
            pltpu.VMEM((ROWS, 128), F32),
            pltpu.SemaphoreType.DMA((2 + PARTS,)),
        ],
        compiler_params=pltpu.CompilerParams(vmem_limit_bytes=28 * MIB),
        cost_estimate=pl.CostEstimate(flops=2 * 10**9, bytes_accessed=9 * 2**20, transcendentals=256),
        name="place_documents",
    )(*operands)


def tail_rows(y_ref):
    to = iota((TAIL, ROWS), 0)
    at = iota((TAIL, ROWS), 1)
    want = (to % CHIPS) * HEAD + to // CHIPS
    left = dot(onehot(at == want), y_ref[:, WIDTH:META]).astype(BF16)
    right = dot(onehot(at == want + 4), y_ref[:, WIDTH:META]).astype(BF16)
    return left, right


def lane_counts(y_ref):
    meta = y_ref[:, META:].astype(F32).T[:8, :]
    pick = onehot(iota((ROWS, TAIL), 0) == (iota((ROWS, TAIL), 1) % CHIPS) * HEAD)
    tail = dot(meta.astype(BF16), pick)
    return meta[0:1, :], meta[1:2, :], tail[0:1, :], tail[1:2, :]


def pack_kernel(y_ref, v_ref):
    room = v_ref.shape[0]
    counts = y_ref[:, META:].astype(F32).T[:8, :]
    first = CAP - counts[1:2, :]
    row = (iota((1, ROWS), 1) % HEAD).astype(F32)
    low = row < 4
    over = [row >= first, low & (row + HEAD >= first), ~low & (row + HEAD - 4 >= first)]
    flags = [jnp.where(mask, 1.0, 0.0) for mask in over]
    before = onehot(iota((ROWS, ROWS), 0) < iota((ROWS, ROWS), 1))
    place = dot(jnp.concatenate(flags + [jnp.zeros((5, ROWS), F32)], axis=0).astype(BF16), before)
    count = jnp.sum(flags[0], axis=1, keepdims=True)
    full = jnp.where(count + jnp.sum(flags[1], axis=1, keepdims=True) > room, 1.0, 0.0)
    places = [place[0:1, :], place[1:2, :] + count, place[2:3, :] + count]
    take = [onehot((iota((room, ROWS), 0) == at.astype(jnp.int32)) & mask) for at, mask in zip(places, over)]
    tail = y_ref[:, WIDTH:META]
    v_ref[:, :HALFW] = (dot(take[0], y_ref[:, :HALFW]) + dot(take[1], tail)).astype(BF16)
    v_ref[:, HALFW:WIDTH] = (dot(take[0], y_ref[:, HALFW:WIDTH]) + dot(take[2], tail)).astype(BF16)
    lane = iota((ROWS, 128), 1)
    at = iota((ROWS, 128), 0)

    def about(row):
        return jnp.where(lane == 0, at // HEAD, jnp.where(lane == 1, CAP - 1 - row, jnp.where(lane == 2, 1, 0))).astype(F32).astype(BF16)

    info = dot(take[0], about(at % HEAD)) + dot(take[1], about(at % HEAD + HEAD))
    v_ref[:, WIDTH:] = jnp.where(iota((room, 128), 1) == 3, full, info).astype(BF16)


def slots(tops):
    lane = iota((256, 128), 1)
    at = iota((256, 128), 0)
    head = [jnp.max(jnp.where(lane == at % HEAD, top, -2.0).reshape(32, HEAD, 128), axis=1) for top in tops[:2]]
    tail = jnp.max(jnp.where(lane == at // CHIPS + HEAD, tops[2], -2.0).reshape(4, CHIPS, 128), axis=0)
    return jnp.maximum(jnp.concatenate(head, axis=0), tail)


def own_valid(y_ref):
    own1, _, own2, _ = lane_counts(y_ref)
    ok1 = (iota((1, ROWS), 1) % HEAD).astype(F32) < own1
    ok2 = (iota((1, TAIL), 1) // CHIPS + HEAD).astype(F32) < own2
    return [ok1[:, :256], ok1[:, 256:], ok2]


def row_block(y_ref, x2_ref, block):
    return y_ref[256 * block : 256 * (block + 1), :WIDTH] if block < 2 else x2_ref[...]


def row_max(mine, other, keep):
    return jnp.max(jnp.where(keep, dot_t(mine, other), -2.0), axis=1, keepdims=True)


def off_diagonal(n):
    return iota((n, n), 0) != iota((n, n), 1)


def call(kernel, name, out_shape, flops, *args, mib=28, scratch=()):
    return pl.pallas_call(
        kernel,
        out_shape=out_shape,
        scratch_shapes=list(scratch),
        compiler_params=pltpu.CompilerParams(vmem_limit_bytes=mib * MIB),
        cost_estimate=pl.CostEstimate(flops=int(flops), bytes_accessed=2**20, transcendentals=0),
        name=name,
    )(*args)


def own_kernel(y_ref, best_ref, x2_ref):
    left, right = tail_rows(y_ref)
    x2_ref[:, :HALFW] = left
    x2_ref[:, HALFW:] = right
    ok = own_valid(y_ref)
    tops = []
    for a in range(3):
        mine = row_block(y_ref, x2_ref, a)
        top = jnp.full((256, 1), -2.0, F32)
        for b in range(3):
            keep = ok[b] & off_diagonal(256) if a == b else ok[b]
            top = jnp.maximum(top, row_max(mine, row_block(y_ref, x2_ref, b), keep))
        tops.append(top)
    best_ref[...] = slots(tops)


def cross_kernel(y_ref, x2_ref, s_ref, so_far_ref, best_ref, s2_ref):
    left, right = tail_rows(s_ref)
    s2_ref[:, :HALFW] = left
    s2_ref[:, HALFW:] = right
    ok = own_valid(s_ref)
    tops = []
    for a in range(3):
        mine = row_block(y_ref, x2_ref, a)
        top = jnp.full((256, 1), -2.0, F32)
        for b in range(3):
            top = jnp.maximum(top, row_max(mine, row_block(s_ref, s2_ref, b), ok[b]))
        tops.append(top)
    best_ref[...] = jnp.maximum(so_far_ref[...], slots(tops))


def valid_rows(y_ref):
    counts = y_ref[:, META:].astype(F32)
    head = (iota((ROWS, 1), 0) % HEAD).astype(F32) < counts[:, 0:1]
    source = jnp.max(counts.reshape(CHIPS, HEAD, 128), axis=1)
    tail = (iota((TAIL, 1), 0) // CHIPS + HEAD).astype(F32) < jnp.concatenate([source] * 4, axis=0)[:, 0:1]
    return [head[:256], head[256:], tail]


def tiles(room):
    size = min(room, 256)
    return [slice(start, start + size) for start in range(0, room, size)]


def column_max(scores, keep):
    return jnp.max(jnp.where(keep, scores, -2.0), axis=0, keepdims=True)


def received_kernel(s_ref, s2_ref, v_ref, so_far_ref, top_ref):
    ok_s = valid_rows(s_ref)
    used = v_ref[:, WIDTH:].astype(F32)[:, 2:3] > 0.5
    for span in tiles(v_ref.shape[0]):
        mine = v_ref[span, :WIDTH]
        size = mine.shape[0]
        top = jnp.full((1, size), -2.0, F32)
        for b in range(3):
            top = jnp.maximum(top, column_max(dot_t(row_block(s_ref, s2_ref, b), mine), ok_s[b]))
        for at in tiles(v_ref.shape[0]):
            keep = used[at] & off_diagonal(size) if at == span else used[at]
            top = jnp.maximum(top, column_max(dot_t(v_ref[at, :WIDTH], mine), keep))
        top_ref[:, span] = jnp.broadcast_to(top, (8, size))


def sibling_kernel(y_ref, x2_ref, v_ref, w_ref, so_far_ref, so_far_top_ref, out_ref, top_ref):
    room = v_ref.shape[0]
    about_v = v_ref[:, WIDTH:].astype(F32)
    about_w = w_ref[:, WIDTH:].astype(F32)
    lanes = jnp.concatenate([about_v, about_w], axis=0).T[:8, :]
    used = lanes[2:3, :] > 0.5
    ok_y = valid_rows(y_ref)
    tops = [jnp.full((256, 1), -2.0, F32) for _ in range(3)]
    top_ref[...] = so_far_top_ref[...]
    if room <= 128:
        groups = [(jnp.concatenate([v_ref[:, :WIDTH], w_ref[:, :WIDTH]], axis=0), used, slice(0, room))]
    else:
        groups = [(v_ref[span, :WIDTH], used[:, span], span) for span in tiles(room)]
        groups += [(w_ref[span, :WIDTH], used[:, room + span.start : room + span.stop], None) for span in tiles(room)]
    for rows, ok, span in groups:
        for a in range(3):
            scores = dot_t(row_block(y_ref, x2_ref, a), rows)
            tops[a] = jnp.maximum(tops[a], jnp.max(jnp.where(ok, scores, -2.0), axis=1, keepdims=True))
            if span is not None:
                top = column_max(scores, ok_y[a])[:, : span.stop - span.start]
                top_ref[:, span] = jnp.maximum(top_ref[:, span], top)
    best = jnp.maximum(so_far_ref[...], slots(tops))
    for span in tiles(room):
        for at in tiles(room):
            top = column_max(dot_t(w_ref[at, :WIDTH], v_ref[span, :WIDTH]), about_w[at, 2:3] > 0.5)
            top_ref[:, span] = jnp.maximum(top_ref[:, span], top)
    source = lanes[0:1, :room].astype(jnp.int32)
    here = (iota((CHIPS, room), 0) == source) & used[:, :room]
    rank = onehot((iota((room, 128), 1) == about_v[:, 1:2].astype(jnp.int32)) & (about_v[:, 2:3] > 0.5))
    placed = jnp.zeros((CHIPS, 128), F32)
    for piece in split3(jnp.where(here, top_ref[0:1, :], 0.0)):
        placed = placed + dot(piece, rank)
    filled = dot(onehot(here), rank)
    full = jnp.maximum(about_v[0:1, 3:4], about_w[0:1, 3:4])
    out = jnp.where(filled > 0.5, placed, best)
    out_ref[...] = jnp.where(iota((CHIPS, 128), 1) == 127, full, out)


def after_kernel(v_ref, best_ref, out_ref):
    pass


def after(v, best):
    anywhere = pl.BlockSpec(memory_space=pl.ANY)
    return pl.pallas_call(
        after_kernel,
        in_specs=[anywhere, anywhere],
        out_specs=anywhere,
        out_shape=jax.ShapeDtypeStruct(v.shape, v.dtype),
        input_output_aliases={0: 0},
        compiler_params=pltpu.CompilerParams(vmem_limit_bytes=MIB),
        name="overflow_after_own",
    )(v, best)


def owner_side(y, room):
    swap = [(0, 1), (1, 0)]
    mib = 28 if room <= 256 else 52
    slot_shape = jax.ShapeDtypeStruct((CHIPS, 128), F32)
    top_shape = jax.ShapeDtypeStruct((8, room), F32)
    tail_shape = jax.ShapeDtypeStruct((TAIL, WIDTH), BF16)
    packed_shape = jax.ShapeDtypeStruct((room, WIDTH + 128), BF16)
    s = lax.ppermute(y, "core", swap)
    v = call(pack_kernel, "pack_overflow", packed_shape, 3e9, y, mib=mib)
    v = lax.ppermute(v, "yl", swap)
    best, x2 = call(own_kernel, "own_pairs", [slot_shape, tail_shape], 5e9, y)
    best, s2 = call(cross_kernel, "cross_pairs", [slot_shape, tail_shape], 6e9, y, x2, s, best)
    v = after(v, best)
    w = lax.ppermute(v, "core", swap)
    top = call(received_kernel, "received_pairs", top_shape, 3e9, s, s2, v, best, mib=mib)
    scratch = [pltpu.VMEM((8, room), F32)]
    return call(sibling_kernel, "sibling_pairs", slot_shape, 1e9, y, x2, v, w, best, top, mib=mib, scratch=scratch)


def pick_kernel(back_ref, rank_ref, out_ref, full_ref):
    rank = rank_ref[0:1, :]
    cluster = rank_ref[1:2, :]
    at_rank = onehot(iota((128, DOCS), 0) == rank)
    back = back_ref[...]
    found = jnp.zeros((CHIPS, DOCS), F32)
    for piece in split3(back):
        found = found + dot(piece, at_rank)
    out_ref[...] = jnp.sum(jnp.where(iota((CHIPS, DOCS), 0) == cluster, found, 0.0), axis=0, keepdims=True)
    full_ref[0, 0] = jnp.max(back[:, 127:128])


def return_to_source(best, rank):
    back = lax.all_to_all(best, CHIP_AXES, split_axis=0, concat_axis=0, tiled=True)
    return pl.pallas_call(
        pick_kernel,
        out_specs=[pl.BlockSpec(memory_space=pltpu.VMEM), pl.BlockSpec(memory_space=pltpu.SMEM)],
        out_shape=[jax.ShapeDtypeStruct((1, DOCS), F32), jax.ShapeDtypeStruct((1, 1), F32)],
        compiler_params=pltpu.CompilerParams(vmem_limit_bytes=4 * MIB),
        name="pick_documents",
    )(back, rank)


def on_device(embed, group, half):
    sent, rank = place_documents(embed, group.reshape(1, DOCS), half.reshape(1, DOCS))
    y = lax.all_to_all(sent, CHIP_AXES, split_axis=0, concat_axis=0, tiled=True)
    nearest, full = return_to_source(owner_side(y, ROOM), rank)
    nearest = lax.cond(
        full[0, 0] > 0.5,
        lambda y, rank, nearest: return_to_source(owner_side(y, ROWS + TAIL), rank)[0],
        lambda y, rank, nearest: nearest,
        y,
        rank,
        nearest,
    )
    return nearest.reshape(DOCS)


def solution(mesh):
    devices = mesh.devices.reshape(4, 8, 2, 2)
    fine = Mesh(devices, ALL_AXES)
    return jax.shard_map(
        on_device,
        mesh=fine,
        in_specs=(P(ALL_AXES, None), P(ALL_AXES, None), P(ALL_AXES)),
        out_specs=P(ALL_AXES),
        check_vma=False,
    )
```

```python
import jax
import jax.numpy as jnp
from jax import lax
from jax.experimental import pallas as pl
from jax.experimental.pallas import tpu as pltpu
from jax.sharding import Mesh, PartitionSpec as P

WIDTH = 4096
HALFW = WIDTH // 2
CHIPS = 64
DOCS = 256
CAP = 24
SIDE = 12
HEAD = 8
PARTS = 4
ROWS = CHIPS * HEAD
TAIL = CHIPS * (SIDE - HEAD)
META = WIDTH + HALFW
SENT = META + 128
CHIP_AXES = ("z", "x", "y")
SHORT = WIDTH + 128
SLOTS = 10
WAYS = 4
ROOM = 48
OVER = WAYS * ROOM
QUARTER = WIDTH // 4
NOTES = WIDTH + QUARTER
FIRST = NOTES + 128
REST = CHIPS * (SLOTS - HEAD)
OWN = ROWS + REST
ALL_AXES = CHIP_AXES + ("core",)
F32 = jnp.float32
BF16 = jnp.bfloat16
MIB = 1024 * 1024


def iota(shape, axis):
    return lax.broadcasted_iota(jnp.int32, shape, axis)


def dot(a, b):
    return jnp.dot(a, b, preferred_element_type=F32)


def dot_t(a, b):
    return lax.dot_general(a, b, (((1,), (1,)), ((), ())), preferred_element_type=F32)


def onehot(mask):
    return jnp.where(mask, 1.0, 0.0).astype(BF16)


def split3(x):
    a = x.astype(BF16)
    rest = x - a.astype(F32)
    b = rest.astype(BF16)
    c = (rest - b.astype(F32)).astype(BF16)
    return a, b, c


def send_kernel(embed_hbm, group_hbm, half_hbm, out_ref, rank_ref, embed_ref, group_ref, half_ref, unit_ref, slot_ref, meta_ref, sems):
    step = pl.program_id(0)

    @pl.when(step == 0)
    def _():
        names = [pltpu.make_async_copy(group_hbm, group_ref, sems.at[0]), pltpu.make_async_copy(half_hbm, half_ref, sems.at[1])]
        size = DOCS // PARTS
        spans = [pl.ds(size * part, size) for part in range(PARTS)]
        parts = [pltpu.make_async_copy(embed_hbm.at[span, :], embed_ref.at[span, :], sems.at[2 + i]) for i, span in enumerate(spans)]
        for copy in names + parts:
            copy.start()
        for copy in names:
            copy.wait()
        cluster = 2 * group_ref[...] + half_ref[...]
        other = cluster + 1 - 2 * half_ref[...]
        member = iota((CHIPS, DOCS), 0) == cluster
        earlier = onehot(iota((DOCS, DOCS), 0) < iota((DOCS, DOCS), 1))
        before = dot(onehot(member), earlier)
        rank = jnp.sum(jnp.where(member, before, 0.0), axis=0, keepdims=True).astype(jnp.int32)
        over = rank >= SIDE
        chip = jnp.where(over, other, cluster)
        row = jnp.where(over, CAP - 1 - rank, rank)
        slot_ref[0:1, :] = jnp.where(row < HEAD, chip * HEAD + row, -1)
        slot_ref[1:2, :] = jnp.where(row >= HEAD, chip * HEAD + row - HEAD, -1)
        slot_ref[2:3, :] = jnp.where(row >= HEAD, chip * HEAD + row - HEAD + 4, -1)
        rank_ref[0:1, :] = rank
        rank_ref[1:2, :] = cluster
        own = jnp.sum(jnp.where(member, 1.0, 0.0), axis=1, keepdims=True)
        oth = jnp.sum(jnp.where(iota((CHIPS, DOCS), 0) == other, 1.0, 0.0), axis=1, keepdims=True)
        lane = iota((CHIPS, 128), 1)
        meta = jnp.where(lane == 0, own, jnp.where(lane == 1, oth, 0.0))
        meta_ref[...] = jnp.broadcast_to(meta[:, None, :], (CHIPS, HEAD, 128)).reshape(ROWS, 128)
        for copy, span in zip(parts, spans):
            copy.wait()
            floats = embed_ref[span, :].astype(F32)
            scale = lax.rsqrt(jnp.sum(floats * floats, axis=1, keepdims=True) + 1e-06)
            unit_ref[span, :] = (floats * scale).astype(BF16)

    rows = out_ref.shape[0]
    base = step * rows
    here = iota((rows, DOCS), 0) + base
    head = onehot(here == slot_ref[0:1, :])
    left = onehot(here == slot_ref[1:2, :])
    right = onehot(here == slot_ref[2:3, :])
    out_ref[:, :WIDTH] = dot(head, unit_ref[...]).astype(BF16)
    out_ref[:, WIDTH:META] = (dot(left, unit_ref[:, :HALFW]) + dot(right, unit_ref[:, HALFW:])).astype(BF16)
    out_ref[:, META:] = meta_ref[pl.ds(pl.multiple_of(base, rows), rows), :].astype(BF16)


def place_documents(embed, group, half):
    steps = 4
    far = pl.BlockSpec(memory_space=pltpu.HBM)
    operands = [pltpu.with_memory_space_constraint(x, pltpu.HBM) for x in (embed, group, half)]
    return pl.pallas_call(
        send_kernel,
        grid=(steps,),
        in_specs=[far, far, far],
        out_specs=[pl.BlockSpec((ROWS // steps, SENT), lambda i: (i, 0)), pl.BlockSpec((8, DOCS), lambda i: (0, 0))],
        out_shape=[jax.ShapeDtypeStruct((ROWS, SENT), BF16), jax.ShapeDtypeStruct((8, DOCS), jnp.int32)],
        scratch_shapes=[
            pltpu.VMEM((DOCS, WIDTH), BF16),
            pltpu.VMEM((1, DOCS), jnp.int32),
            pltpu.VMEM((1, DOCS), jnp.int32),
            pltpu.VMEM((DOCS, WIDTH), BF16),
            pltpu.VMEM((8, DOCS), jnp.int32),
            pltpu.VMEM((ROWS, 128), F32),
            pltpu.SemaphoreType.DMA((2 + PARTS,)),
        ],
        compiler_params=pltpu.CompilerParams(vmem_limit_bytes=28 * MIB),
        cost_estimate=pl.CostEstimate(flops=2 * 10**9, bytes_accessed=9 * 2**20, transcendentals=256),
        name="place_documents",
    )(*operands)


def tail_rows(y_ref):
    to = iota((TAIL, ROWS), 0)
    at = iota((TAIL, ROWS), 1)
    want = (to % CHIPS) * HEAD + to // CHIPS
    left = dot(onehot(at == want), y_ref[:, WIDTH:META]).astype(BF16)
    right = dot(onehot(at == want + 4), y_ref[:, WIDTH:META]).astype(BF16)
    return left, right


def lane_counts(y_ref):
    meta = y_ref[:, META:].astype(F32).T[:8, :]
    pick = onehot(iota((ROWS, TAIL), 0) == (iota((ROWS, TAIL), 1) % CHIPS) * HEAD)
    tail = dot(meta.astype(BF16), pick)
    return meta[0:1, :], meta[1:2, :], tail[0:1, :], tail[1:2, :]


def pack_kernel(y_ref, v_ref):
    room = v_ref.shape[0]
    counts = y_ref[:, META:].astype(F32).T[:8, :]
    first = CAP - counts[1:2, :]
    row = (iota((1, ROWS), 1) % HEAD).astype(F32)
    low = row < 4
    over = [row >= first, low & (row + HEAD >= first), ~low & (row + HEAD - 4 >= first)]
    flags = [jnp.where(mask, 1.0, 0.0) for mask in over]
    before = onehot(iota((ROWS, ROWS), 0) < iota((ROWS, ROWS), 1))
    place = dot(jnp.concatenate(flags + [jnp.zeros((5, ROWS), F32)], axis=0).astype(BF16), before)
    count = jnp.sum(flags[0], axis=1, keepdims=True)
    full = jnp.where(count + jnp.sum(flags[1], axis=1, keepdims=True) > room, 1.0, 0.0)
    places = [place[0:1, :], place[1:2, :] + count, place[2:3, :] + count]
    take = [onehot((iota((room, ROWS), 0) == at.astype(jnp.int32)) & mask) for at, mask in zip(places, over)]
    tail = y_ref[:, WIDTH:META]
    v_ref[:, :HALFW] = (dot(take[0], y_ref[:, :HALFW]) + dot(take[1], tail)).astype(BF16)
    v_ref[:, HALFW:WIDTH] = (dot(take[0], y_ref[:, HALFW:WIDTH]) + dot(take[2], tail)).astype(BF16)
    lane = iota((ROWS, 128), 1)
    at = iota((ROWS, 128), 0)

    def about(row):
        return jnp.where(lane == 0, at // HEAD, jnp.where(lane == 1, CAP - 1 - row, jnp.where(lane == 2, 1, 0))).astype(F32).astype(BF16)

    info = dot(take[0], about(at % HEAD)) + dot(take[1], about(at % HEAD + HEAD))
    v_ref[:, WIDTH:] = jnp.where(iota((room, 128), 1) == 3, full, info).astype(BF16)


def slots(tops):
    lane = iota((256, 128), 1)
    at = iota((256, 128), 0)
    head = [jnp.max(jnp.where(lane == at % HEAD, top, -2.0).reshape(32, HEAD, 128), axis=1) for top in tops[:2]]
    tail = jnp.max(jnp.where(lane == at // CHIPS + HEAD, tops[2], -2.0).reshape(4, CHIPS, 128), axis=0)
    return jnp.maximum(jnp.concatenate(head, axis=0), tail)


def own_valid(y_ref):
    own1, _, own2, _ = lane_counts(y_ref)
    ok1 = (iota((1, ROWS), 1) % HEAD).astype(F32) < own1
    ok2 = (iota((1, TAIL), 1) // CHIPS + HEAD).astype(F32) < own2
    return [ok1[:, :256], ok1[:, 256:], ok2]


def row_block(y_ref, x2_ref, block):
    return y_ref[256 * block : 256 * (block + 1), :WIDTH] if block < 2 else x2_ref[...]


def row_max(mine, other, keep):
    return jnp.max(jnp.where(keep, dot_t(mine, other), -2.0), axis=1, keepdims=True)


def off_diagonal(n):
    return iota((n, n), 0) != iota((n, n), 1)


def call(kernel, name, out_shape, flops, *args, mib=28, scratch=()):
    return pl.pallas_call(
        kernel,
        out_shape=out_shape,
        scratch_shapes=list(scratch),
        compiler_params=pltpu.CompilerParams(vmem_limit_bytes=mib * MIB),
        cost_estimate=pl.CostEstimate(flops=int(flops), bytes_accessed=2**20, transcendentals=0),
        name=name,
    )(*args)


def own_kernel(y_ref, best_ref, x2_ref):
    left, right = tail_rows(y_ref)
    x2_ref[:, :HALFW] = left
    x2_ref[:, HALFW:] = right
    ok = own_valid(y_ref)
    tops = []
    for a in range(3):
        mine = row_block(y_ref, x2_ref, a)
        top = jnp.full((256, 1), -2.0, F32)
        for b in range(3):
            keep = ok[b] & off_diagonal(256) if a == b else ok[b]
            top = jnp.maximum(top, row_max(mine, row_block(y_ref, x2_ref, b), keep))
        tops.append(top)
    best_ref[...] = slots(tops)


def cross_kernel(y_ref, x2_ref, s_ref, so_far_ref, best_ref, s2_ref):
    left, right = tail_rows(s_ref)
    s2_ref[:, :HALFW] = left
    s2_ref[:, HALFW:] = right
    ok = own_valid(s_ref)
    tops = []
    for a in range(3):
        mine = row_block(y_ref, x2_ref, a)
        top = jnp.full((256, 1), -2.0, F32)
        for b in range(3):
            top = jnp.maximum(top, row_max(mine, row_block(s_ref, s2_ref, b), ok[b]))
        tops.append(top)
    best_ref[...] = jnp.maximum(so_far_ref[...], slots(tops))


def valid_rows(y_ref):
    counts = y_ref[:, META:].astype(F32)
    head = (iota((ROWS, 1), 0) % HEAD).astype(F32) < counts[:, 0:1]
    source = jnp.max(counts.reshape(CHIPS, HEAD, 128), axis=1)
    tail = (iota((TAIL, 1), 0) // CHIPS + HEAD).astype(F32) < jnp.concatenate([source] * 4, axis=0)[:, 0:1]
    return [head[:256], head[256:], tail]


def tiles(room):
    size = min(room, 256)
    return [slice(start, start + size) for start in range(0, room, size)]


def column_max(scores, keep):
    return jnp.max(jnp.where(keep, scores, -2.0), axis=0, keepdims=True)


def received_kernel(s_ref, s2_ref, v_ref, so_far_ref, top_ref):
    ok_s = valid_rows(s_ref)
    used = v_ref[:, WIDTH:].astype(F32)[:, 2:3] > 0.5
    for span in tiles(v_ref.shape[0]):
        mine = v_ref[span, :WIDTH]
        size = mine.shape[0]
        top = jnp.full((1, size), -2.0, F32)
        for b in range(3):
            top = jnp.maximum(top, column_max(dot_t(row_block(s_ref, s2_ref, b), mine), ok_s[b]))
        for at in tiles(v_ref.shape[0]):
            keep = used[at] & off_diagonal(size) if at == span else used[at]
            top = jnp.maximum(top, column_max(dot_t(v_ref[at, :WIDTH], mine), keep))
        top_ref[:, span] = jnp.broadcast_to(top, (8, size))


def sibling_kernel(y_ref, x2_ref, v_ref, w_ref, so_far_ref, so_far_top_ref, out_ref, top_ref):
    room = v_ref.shape[0]
    about_v = v_ref[:, WIDTH:].astype(F32)
    about_w = w_ref[:, WIDTH:].astype(F32)
    lanes = jnp.concatenate([about_v, about_w], axis=0).T[:8, :]
    used = lanes[2:3, :] > 0.5
    ok_y = valid_rows(y_ref)
    tops = [jnp.full((256, 1), -2.0, F32) for _ in range(3)]
    top_ref[...] = so_far_top_ref[...]
    if room <= 128:
        groups = [(jnp.concatenate([v_ref[:, :WIDTH], w_ref[:, :WIDTH]], axis=0), used, slice(0, room))]
    else:
        groups = [(v_ref[span, :WIDTH], used[:, span], span) for span in tiles(room)]
        groups += [(w_ref[span, :WIDTH], used[:, room + span.start : room + span.stop], None) for span in tiles(room)]
    for rows, ok, span in groups:
        for a in range(3):
            scores = dot_t(row_block(y_ref, x2_ref, a), rows)
            tops[a] = jnp.maximum(tops[a], jnp.max(jnp.where(ok, scores, -2.0), axis=1, keepdims=True))
            if span is not None:
                top = column_max(scores, ok_y[a])[:, : span.stop - span.start]
                top_ref[:, span] = jnp.maximum(top_ref[:, span], top)
    best = jnp.maximum(so_far_ref[...], slots(tops))
    for span in tiles(room):
        for at in tiles(room):
            top = column_max(dot_t(w_ref[at, :WIDTH], v_ref[span, :WIDTH]), about_w[at, 2:3] > 0.5)
            top_ref[:, span] = jnp.maximum(top_ref[:, span], top)
    source = lanes[0:1, :room].astype(jnp.int32)
    here = (iota((CHIPS, room), 0) == source) & used[:, :room]
    rank = onehot((iota((room, 128), 1) == about_v[:, 1:2].astype(jnp.int32)) & (about_v[:, 2:3] > 0.5))
    placed = jnp.zeros((CHIPS, 128), F32)
    for piece in split3(jnp.where(here, top_ref[0:1, :], 0.0)):
        placed = placed + dot(piece, rank)
    filled = dot(onehot(here), rank)
    full = jnp.maximum(about_v[0:1, 3:4], about_w[0:1, 3:4])
    out = jnp.where(filled > 0.5, placed, best)
    out_ref[...] = jnp.where(iota((CHIPS, 128), 1) == 127, full, out)


def after_kernel(v_ref, best_ref, out_ref):
    pass


def after(v, best):
    anywhere = pl.BlockSpec(memory_space=pl.ANY)
    return pl.pallas_call(
        after_kernel,
        in_specs=[anywhere, anywhere],
        out_specs=anywhere,
        out_shape=jax.ShapeDtypeStruct(v.shape, v.dtype),
        input_output_aliases={0: 0},
        compiler_params=pltpu.CompilerParams(vmem_limit_bytes=MIB),
        name="overflow_after_own",
    )(v, best)


def owner_side(y, room):
    swap = [(0, 1), (1, 0)]
    mib = 28 if room <= 256 else 52
    slot_shape = jax.ShapeDtypeStruct((CHIPS, 128), F32)
    top_shape = jax.ShapeDtypeStruct((8, room), F32)
    tail_shape = jax.ShapeDtypeStruct((TAIL, WIDTH), BF16)
    packed_shape = jax.ShapeDtypeStruct((room, WIDTH + 128), BF16)
    s = lax.ppermute(y, "core", swap)
    v = call(pack_kernel, "pack_overflow", packed_shape, 3e9, y, mib=mib)
    v = lax.ppermute(v, "y", [(0, 1), (1, 0), (2, 3), (3, 2)])
    best, x2 = call(own_kernel, "own_pairs", [slot_shape, tail_shape], 5e9, y)
    best, s2 = call(cross_kernel, "cross_pairs", [slot_shape, tail_shape], 6e9, y, x2, s, best)
    v = after(v, best)
    w = lax.ppermute(v, "core", swap)
    top = call(received_kernel, "received_pairs", top_shape, 3e9, s, s2, v, best, mib=mib)
    scratch = [pltpu.VMEM((8, room), F32)]
    return call(sibling_kernel, "sibling_pairs", slot_shape, 1e9, y, x2, v, w, best, top, mib=mib, scratch=scratch)


def pick_kernel(back_ref, rank_ref, out_ref, full_ref):
    rank = rank_ref[0:1, :]
    cluster = rank_ref[1:2, :]
    at_rank = onehot(iota((128, DOCS), 0) == rank)
    back = back_ref[...]
    found = jnp.zeros((CHIPS, DOCS), F32)
    for piece in split3(back):
        found = found + dot(piece, at_rank)
    out_ref[...] = jnp.sum(jnp.where(iota((CHIPS, DOCS), 0) == cluster, found, 0.0), axis=0, keepdims=True)
    full_ref[0, 0] = jnp.max(back[:, 127:128])


def return_to_source(best, rank):
    back = lax.all_to_all(best, CHIP_AXES, split_axis=0, concat_axis=0, tiled=True)
    return pl.pallas_call(
        pick_kernel,
        out_specs=[pl.BlockSpec(memory_space=pltpu.VMEM), pl.BlockSpec(memory_space=pltpu.SMEM)],
        out_shape=[jax.ShapeDtypeStruct((1, DOCS), F32), jax.ShapeDtypeStruct((1, 1), F32)],
        compiler_params=pltpu.CompilerParams(vmem_limit_bytes=4 * MIB),
        name="pick_documents",
    )(back, rank)


def next_chip(x, way):
    unit = 1 if way < 2 else 4
    place = (iota(x.shape, 1) // unit) % 4
    roll = lambda shift: pltpu.roll(x, shift % 128, axis=1)
    if way % 2 == 0:
        return jnp.where(place == 3, roll(3 * unit), roll(-unit))
    return jnp.where(place == 0, roll(-3 * unit), roll(unit))


def neighbour(z, x, y, way):
    step = 1 if way % 2 == 0 else 3
    if way < 2:
        y = (y + step) & 3
    else:
        x = (x + step) & 3
    return 16 * z + 4 * x + y


def spread_kernel(embed_hbm, group_hbm, half_hbm, out_ref, rank_ref, embed_ref, group_ref, half_ref, unit_ref, note_ref, slot_ref, sems):
    step = pl.program_id(0)

    @pl.when(step == 0)
    def _():
        names = [pltpu.make_async_copy(group_hbm, group_ref, sems.at[0]), pltpu.make_async_copy(half_hbm, half_ref, sems.at[1])]
        size = DOCS // PARTS
        spans = [pl.ds(size * part, size) for part in range(PARTS)]
        parts = [pltpu.make_async_copy(embed_hbm.at[span, :], embed_ref.at[span, :], sems.at[2 + i]) for i, span in enumerate(spans)]
        for copy in names + parts:
            copy.start()
        for copy in names:
            copy.wait()
        group, half = group_ref[...], half_ref[...]
        z, x, y = ((group >> 4) + 2 * half) & 3, ((group >> 2) + 2 * half) & 3, (group + 2 * half) & 3
        home = 16 * z + 4 * x + y
        member = onehot((iota((2 * CHIPS, DOCS), 0) & (CHIPS - 1)) == home)
        earlier = onehot(iota((DOCS, DOCS), 0) < iota((DOCS, DOCS), 1))
        before = dot(member[:CHIPS], earlier)
        rank = jnp.sum(before * member[:CHIPS].astype(F32), axis=0, keepdims=True)
        counts = dot_t(jnp.ones((8, DOCS), BF16), member)
        left = jnp.maximum(counts - SLOTS, 0.0)
        free = SLOTS - jnp.minimum(counts, float(SLOTS))
        given = [jnp.zeros((8, 2 * CHIPS), F32) for _ in range(WAYS)]
        turn = (lax.axis_index("z") + lax.axis_index("x") + lax.axis_index("y")) & 3
        plan = [(d, jnp.where(d >= turn, 1.0, 0.0)) for d in range(WAYS)]
        plan += [(d, 1.0) for d in range(WAYS)] * 2 + [(d, 24.0) for d in reversed(range(WAYS))]
        for d, most in plan:
            take = jnp.minimum(jnp.minimum(left, next_chip(free, d)), most)
            given[d] = given[d] + take
            left = left - take
            free = free - next_chip(take, d ^ 1)
        ends, offsets = [], []
        total, used = jnp.zeros_like(left), jnp.zeros_like(left)
        for d in range(WAYS):
            total = total + given[d]
            ends.append(total)
            offsets.append(next_chip(used, d))
            used = used + next_chip(given[d], d ^ 1)
        table = jnp.concatenate([row[0:1] for row in ends + offsets] + [jnp.zeros((8, 2 * CHIPS), F32)], axis=0)
        table = jnp.where(iota(table.shape, 1) < CHIPS, table, 0.0)
        found = dot(table.astype(BF16), member)
        beyond = rank - SLOTS
        own = beyond < 0.0
        chip = home
        row = jnp.where(own, rank.astype(jnp.int32), -1)
        came = jnp.zeros((1, DOCS), F32)
        for d in range(WAYS):
            start = found[d - 1 : d] if d else jnp.zeros((1, DOCS), F32)
            this = (beyond >= start) & (beyond < found[d : d + 1])
            offset = found[WAYS + d : WAYS + d + 1]
            row = jnp.where(this, SLOTS - 1 - (offset + beyond - start).astype(jnp.int32), row)
            chip = jnp.where(this, neighbour(z, x, y, d), chip)
            came = jnp.where(this, d + 1.0, came)
        slot_ref[0:1, :] = jnp.where((row >= 0) & (row < HEAD), chip * HEAD + row, -1)
        slot_ref[1:2, :] = jnp.where(row >= HEAD, chip * HEAD + 4 * (row - HEAD), -8)
        rank_ref[0:1, :] = rank.astype(jnp.int32)
        rank_ref[1:2, :] = home
        lost = jnp.max(jnp.where(row < 0, 1.0, 0.0), axis=1, keepdims=True)
        line = iota((128, DOCS), 0)
        for part in range(2):
            at = line - 8 * part
            notes = jnp.where(at == 0, jnp.where(own, 1.0, 0.0), jnp.where(at == 1, came, jnp.where(at == 2, rank, 0.0)))
            note_ref[part] = jnp.where(at == 3, lost, notes).T.astype(BF16)
        for copy, span in zip(parts, spans):
            copy.wait()
            floats = embed_ref[span, :].astype(F32)
            scale = lax.rsqrt(jnp.sum(floats * floats, axis=1, keepdims=True) + 1e-06)
            unit_ref[span, :] = (floats * scale).astype(BF16)

    rows = out_ref.shape[0]
    at = iota((rows, DOCS), 0) + step * rows
    whole = onehot(at == slot_ref[0:1, :])
    out_ref[:, :WIDTH] = dot(whole, unit_ref[...]).astype(BF16)
    quarters = jnp.zeros((rows, QUARTER), F32)
    notes = dot(whole, note_ref[0])
    for q in range(4):
        this = onehot(at == slot_ref[1:2, :] + q)
        quarters = quarters + dot(this, unit_ref[:, QUARTER * q : QUARTER * (q + 1)])
        notes = notes + dot(this, note_ref[1])
    out_ref[:, WIDTH:NOTES] = quarters.astype(BF16)
    out_ref[:, NOTES:] = notes.astype(BF16)


def spread_documents(embed, group, half):
    steps = 4
    far = pl.BlockSpec(memory_space=pltpu.HBM)
    operands = [pltpu.with_memory_space_constraint(x, pltpu.HBM) for x in (embed, group, half)]
    return pl.pallas_call(
        spread_kernel,
        grid=(steps,),
        in_specs=[far, far, far],
        out_specs=[pl.BlockSpec((ROWS // steps, FIRST), lambda i: (i, 0)), pl.BlockSpec((8, DOCS), lambda i: (0, 0))],
        out_shape=[jax.ShapeDtypeStruct((ROWS, FIRST), BF16), jax.ShapeDtypeStruct((8, DOCS), jnp.int32)],
        scratch_shapes=[
            pltpu.VMEM((DOCS, WIDTH), BF16),
            pltpu.VMEM((1, DOCS), jnp.int32),
            pltpu.VMEM((1, DOCS), jnp.int32),
            pltpu.VMEM((DOCS, WIDTH), BF16),
            pltpu.VMEM((2, DOCS, 128), BF16),
            pltpu.VMEM((8, DOCS), jnp.int32),
            pltpu.SemaphoreType.DMA((2 + PARTS,)),
        ],
        compiler_params=pltpu.CompilerParams(vmem_limit_bytes=28 * MIB),
        cost_estimate=pl.CostEstimate(flops=2 * 10**9, bytes_accessed=9 * 2**20, transcendentals=256),
        name="spread_documents",
    )(*operands)


def quarter_rows(y_ref):
    to, at = iota((REST, ROWS), 0), iota((REST, ROWS), 1)
    want = (to % CHIPS) * HEAD + 4 * (to // CHIPS)
    return [dot(onehot(at == want + q), y_ref[:, WIDTH:NOTES]).astype(BF16) for q in range(4)]


def at_home(y_ref):
    notes = y_ref[:, NOTES:].astype(F32).T[:16, :]
    at, to = iota((ROWS, REST), 0), iota((ROWS, REST), 1)
    pick = onehot(at == (to % CHIPS) * HEAD + 4 * (to // CHIPS))
    return notes[0:1, :] > 0.5, dot(notes[8:16, :].astype(BF16), pick)[0:1, :] > 0.5


def sort_kernel(y_ref, *v_refs):
    notes = y_ref[:, NOTES:].astype(F32).T[:16, :]
    quarter = iota((1, ROWS), 1) % 4
    ways = [notes[1:2, :] == d + 1.0 for d in range(WAYS)]
    ways += [(notes[9:10, :] == d + 1.0) & (quarter == q) for q in range(4) for d in range(WAYS)]
    flags = jnp.concatenate([jnp.where(way, 1.0, 0.0) for way in ways] + [jnp.zeros((4, ROWS), F32)], axis=0)
    before = onehot(iota((ROWS, ROWS), 0) < iota((ROWS, ROWS), 1))
    place = dot(flags.astype(BF16), before)
    sums = jnp.sum(flags, axis=1, keepdims=True)
    most = jnp.max(sums[0:WAYS] + sums[WAYS : 2 * WAYS], axis=0, keepdims=True)
    lost = jnp.max(jnp.maximum(notes[3:4, :], notes[11:12, :]), axis=1, keepdims=True)
    full = jnp.where((most > ROOM) | (lost > 0.5), 1.0, 0.0)

    def take(first, shift):
        slot = iota((ROOM, ROWS), 0)
        rows = []
        for d in range(WAYS):
            to = place[first + d : first + d + 1, :] + (sums[d : d + 1, :] if shift else 0.0)
            rows.append(jnp.where((slot == to.astype(jnp.int32)) & ways[first + d], 1.0, 0.0))
        return jnp.concatenate(rows, axis=0).astype(BF16)

    whole = take(0, False)
    lane = iota((ROWS, 128), 1)
    source = (iota((ROWS, 128), 0) // HEAD).astype(F32)
    extra = jnp.where(lane == 4, source, jnp.where(lane == 5, 1.0, 0.0))
    given = y_ref[:, NOTES:].astype(F32)
    info = dot(whole, jnp.where(lane == 2, given, extra).astype(BF16))
    for q in range(4):
        this = take(WAYS * (1 + q), True)
        span = slice(QUARTER * q, QUARTER * (q + 1))
        rows = (dot(whole, y_ref[:, span]) + dot(this, y_ref[:, WIDTH:NOTES])).astype(BF16)
        for d in range(WAYS):
            v_refs[d][:, span] = rows[ROOM * d : ROOM * (d + 1)]
        if q == 0:
            moved = jnp.where(lane == 2, pltpu.roll(given, 128 - 8, axis=1), extra)
            info = info + dot(this, moved.astype(BF16))
    info = jnp.where(iota((OVER, 128), 1) == 3, full, info).astype(BF16)
    for d in range(WAYS):
        v_refs[d][:, WIDTH:] = info[ROOM * d : ROOM * (d + 1)]


def to_slots(top, rest):
    keep = iota((ROWS, 128), 1) == iota((ROWS, 128), 0) % HEAD
    head = jnp.max(jnp.where(keep, top, -2.0).reshape(CHIPS, HEAD, 128), axis=1)
    keep = iota((REST, 128), 1) == iota((REST, 128), 0) // CHIPS + HEAD
    return jnp.maximum(head, jnp.max(jnp.where(keep, rest, -2.0).reshape(2, CHIPS, 128), axis=0))


def home_kernel(y_ref, best_ref, x2_ref):
    for q, rows in enumerate(quarter_rows(y_ref)):
        x2_ref[:, QUARTER * q : QUARTER * (q + 1)] = rows
    ok, ok2 = at_home(y_ref)
    tops = []
    for a in range(2):
        mine = y_ref[256 * a : 256 * (a + 1), :WIDTH]
        keep = ok & (iota((256, ROWS), 0) + 256 * a != iota((256, ROWS), 1))
        tops.append(jnp.maximum(row_max(mine, y_ref[:, :WIDTH], keep), row_max(mine, x2_ref[...], ok2)))
    rest = jnp.maximum(row_max(x2_ref[...], y_ref[:, :WIDTH], ok), row_max(x2_ref[...], x2_ref[...], ok2 & off_diagonal(REST)))
    best_ref[...] = to_slots(jnp.concatenate(tops, axis=0), rest)


def other_core_kernel(y_ref, x2_ref, s_ref, so_far_ref, best_ref, s2_ref):
    for q, rows in enumerate(quarter_rows(s_ref)):
        s2_ref[:, QUARTER * q : QUARTER * (q + 1)] = rows
    ok, ok2 = at_home(s_ref)

    def top(mine):
        return jnp.maximum(row_max(mine, s_ref[:, :WIDTH], ok), row_max(mine, s2_ref[...], ok2))

    tops = [top(y_ref[256 * a : 256 * (a + 1), :WIDTH]) for a in range(2)]
    best_ref[...] = jnp.maximum(so_far_ref[...], to_slots(jnp.concatenate(tops, axis=0), top(x2_ref[...])))


def join_kernel(*refs):
    out_ref = refs[-1]
    for d in range(WAYS):
        out_ref[ROOM * d : ROOM * (d + 1), :] = refs[d][...]


def notes_of(v_ref):
    return v_ref[:, WIDTH:].astype(F32).T[:8, :]


def guests_kernel(y_ref, x2_ref, s_ref, s2_ref, v_ref, so_far_ref, top_ref, own_ref):
    mine = v_ref[:, :WIDTH]
    used = v_ref[:, WIDTH:].astype(F32)[:, 5:6] > 0.5
    ok_v = notes_of(v_ref)[5:6, :] > 0.5
    top = row_max(mine, mine, ok_v & off_diagonal(OVER))
    ok, ok2 = at_home(y_ref)
    for rows, keep, span in ((y_ref[:, :WIDTH], ok, slice(0, ROWS)), (x2_ref[...], ok2, slice(ROWS, OWN))):
        scores = dot_t(mine, rows)
        own_ref[:, span] = jnp.broadcast_to(column_max(scores, used), (8, span.stop - span.start))
        top = jnp.maximum(top, jnp.max(jnp.where(keep, scores, -2.0), axis=1, keepdims=True))
    ok, ok2 = at_home(s_ref)
    top = jnp.maximum(top, row_max(mine, s_ref[:, :WIDTH], ok))
    top = jnp.maximum(top, row_max(mine, s2_ref[...], ok2))
    top_ref[...] = jnp.broadcast_to(top, (OVER, 128))


def finish_kernel(y_ref, x2_ref, v_ref, w_ref, so_far_ref, top_ref, own_ref, out_ref):
    about = v_ref[:, WIDTH:].astype(F32)
    about_w = w_ref[:, WIDTH:].astype(F32)
    lanes = notes_of(v_ref)
    theirs = w_ref[:, :WIDTH]
    used = about_w[:, 5:6] > 0.5
    head = jnp.maximum(own_ref[:, :ROWS], column_max(dot_t(theirs, y_ref[:, :WIDTH]), used))
    rest = jnp.maximum(own_ref[:, ROWS:], column_max(dot_t(theirs, x2_ref[...]), used))
    best = jnp.maximum(so_far_ref[...], to_slots(head.T[:, 0:1], rest.T[:, 0:1]))
    top = row_max(v_ref[:, :WIDTH], theirs, notes_of(w_ref)[5:6, :] > 0.5)
    top = jnp.maximum(top_ref[...], top)
    here = onehot((iota((CHIPS, OVER), 0) == lanes[4:5, :].astype(jnp.int32)) & (lanes[5:6, :] > 0.5))
    rank = (iota((OVER, 128), 1) == about[:, 2:3].astype(jnp.int32)) & (about[:, 5:6] > 0.5)
    placed = jnp.zeros((CHIPS, 128), F32)
    for piece in split3(jnp.where(rank, top, 0.0)):
        placed = placed + dot(here, piece)
    filled = dot(here, onehot(rank))
    full = jnp.maximum(about[0:1, 3:4], about_w[0:1, 3:4])
    out = jnp.where(filled > 0.5, placed, best)
    out_ref[...] = jnp.where(iota((CHIPS, 128), 1) == 127, full, out)


def owner_short(y):
    swap = [(0, 1), (1, 0)]
    slot_shape = jax.ShapeDtypeStruct((CHIPS, 128), F32)
    rest_shape = jax.ShapeDtypeStruct((REST, WIDTH), BF16)
    way_shape = jax.ShapeDtypeStruct((ROOM, SHORT), BF16)
    s = lax.ppermute(y, "core", swap)
    ways = call(sort_kernel, "sort_overflow", [way_shape] * WAYS, 3e9, y, mib=20)
    came = []
    for d, v in enumerate(ways):
        back = 3 if d % 2 == 0 else 1
        came.append(lax.ppermute(v, "yx"[d // 2], [(i, (i + back) % 4) for i in range(4)]))
    best, x2 = call(home_kernel, "home_pairs", [slot_shape, rest_shape], 4e9, y, mib=20)
    best, s2 = call(other_core_kernel, "other_core_pairs", [slot_shape, rest_shape], 4e9, y, x2, s, best, mib=20)
    v = call(join_kernel, "join_overflow", jax.ShapeDtypeStruct((OVER, SHORT), BF16), 1e8, *came, best, mib=8)
    w = lax.ppermute(v, "core", swap)
    shapes = [jax.ShapeDtypeStruct((OVER, 128), F32), jax.ShapeDtypeStruct((8, OWN), F32)]
    top, own = call(guests_kernel, "guest_pairs", shapes, 6e9, y, x2, s, s2, v, best, mib=24)
    return call(finish_kernel, "finish_pairs", slot_shape, 3e9, y, x2, v, w, best, top, own, mib=24)


def wide_form(embed, group, half):
    sent, rank = place_documents(embed, group, half)
    y = lax.all_to_all(sent, CHIP_AXES, split_axis=0, concat_axis=0, tiled=True)
    return return_to_source(owner_side(y, ROWS + TAIL), rank)[0]


def on_device(embed, group, half):
    group, half = group.reshape(1, DOCS), half.reshape(1, DOCS)
    sent, rank = spread_documents(embed, group, half)
    y = lax.all_to_all(sent, CHIP_AXES, split_axis=0, concat_axis=0, tiled=True)
    nearest, full = return_to_source(owner_short(y), rank)
    nearest = lax.cond(
        full[0, 0] > 0.5,
        lambda embed, group, half, nearest: wide_form(embed, group, half),
        lambda embed, group, half, nearest: nearest,
        embed,
        group,
        half,
        nearest,
    )
    return nearest.reshape(DOCS)


def solution(mesh):
    devices = mesh.devices.reshape(4, 4, 4, 2)
    fine = Mesh(devices, ALL_AXES)
    return jax.shard_map(
        on_device,
        mesh=fine,
        in_specs=(P(ALL_AXES, None), P(ALL_AXES, None), P(ALL_AXES)),
        out_specs=P(ALL_AXES),
        check_vma=False,
    )
```

```python
import functools
import itertools

import jax
import jax.numpy as jnp
from jax import lax
from jax.experimental import pallas as pl
from jax.experimental.pallas import tpu as pltpu
from jax.sharding import Mesh, PartitionSpec as P

WIDTH = 4096
HALFW = WIDTH // 2
CHIPS = 64
DOCS = 256
CAP = 24
SIDE = 12
HEAD = 8
PARTS = 4
ROWS = CHIPS * HEAD
TAIL = CHIPS * (SIDE - HEAD)
META = WIDTH + HALFW
SENT = META + 128
CHIP_AXES = ("z", "y", "x")
SHORT = WIDTH + 128
SLOTS = 10
ROOMS = (64, 64, 32, 32)
WAYS = len(ROOMS)
STARTS = (0, 64, 128, 160)
OVER = sum(ROOMS)
QUARTER = WIDTH // 4
NOTES = WIDTH + QUARTER
FIRST = NOTES + 128
REST = CHIPS * (SLOTS - HEAD)
OWN = ROWS + REST
ALL_AXES = ("z", "x", "y", "core")
F32 = jnp.float32
BF16 = jnp.bfloat16
MIB = 1024 * 1024


def iota(shape, axis):
    return lax.broadcasted_iota(jnp.int32, shape, axis)


def dot(a, b):
    return jnp.dot(a, b, preferred_element_type=F32)


def dot_t(a, b):
    return lax.dot_general(a, b, (((1,), (1,)), ((), ())), preferred_element_type=F32)


def onehot(mask):
    return jnp.where(mask, 1.0, 0.0).astype(BF16)


def split3(x):
    a = x.astype(BF16)
    rest = x - a.astype(F32)
    b = rest.astype(BF16)
    c = (rest - b.astype(F32)).astype(BF16)
    return a, b, c


def send_kernel(embed_hbm, group_hbm, half_hbm, out_ref, rank_ref, embed_ref, group_ref, half_ref, unit_ref, slot_ref, meta_ref, sems):
    step = pl.program_id(0)

    @pl.when(step == 0)
    def _():
        names = [pltpu.make_async_copy(group_hbm, group_ref, sems.at[0]), pltpu.make_async_copy(half_hbm, half_ref, sems.at[1])]
        size = DOCS // PARTS
        spans = [pl.ds(size * part, size) for part in range(PARTS)]
        parts = [pltpu.make_async_copy(embed_hbm.at[span, :], embed_ref.at[span, :], sems.at[2 + i]) for i, span in enumerate(spans)]
        for copy in names + parts:
            copy.start()
        for copy in names:
            copy.wait()
        cluster = 2 * group_ref[...] + half_ref[...]
        other = cluster + 1 - 2 * half_ref[...]
        member = iota((CHIPS, DOCS), 0) == cluster
        earlier = onehot(iota((DOCS, DOCS), 0) < iota((DOCS, DOCS), 1))
        before = dot(onehot(member), earlier)
        rank = jnp.sum(jnp.where(member, before, 0.0), axis=0, keepdims=True).astype(jnp.int32)
        over = rank >= SIDE
        chip = jnp.where(over, other, cluster)
        row = jnp.where(over, CAP - 1 - rank, rank)
        slot_ref[0:1, :] = jnp.where(row < HEAD, chip * HEAD + row, -1)
        slot_ref[1:2, :] = jnp.where(row >= HEAD, chip * HEAD + row - HEAD, -1)
        slot_ref[2:3, :] = jnp.where(row >= HEAD, chip * HEAD + row - HEAD + 4, -1)
        rank_ref[0:1, :] = rank
        rank_ref[1:2, :] = cluster
        own = jnp.sum(jnp.where(member, 1.0, 0.0), axis=1, keepdims=True)
        oth = jnp.sum(jnp.where(iota((CHIPS, DOCS), 0) == other, 1.0, 0.0), axis=1, keepdims=True)
        lane = iota((CHIPS, 128), 1)
        meta = jnp.where(lane == 0, own, jnp.where(lane == 1, oth, 0.0))
        meta_ref[...] = jnp.broadcast_to(meta[:, None, :], (CHIPS, HEAD, 128)).reshape(ROWS, 128)
        for copy, span in zip(parts, spans):
            copy.wait()
            floats = embed_ref[span, :].astype(F32)
            scale = lax.rsqrt(jnp.sum(floats * floats, axis=1, keepdims=True) + 1e-06)
            unit_ref[span, :] = (floats * scale).astype(BF16)

    rows = out_ref.shape[0]
    base = step * rows
    here = iota((rows, DOCS), 0) + base
    head = onehot(here == slot_ref[0:1, :])
    left = onehot(here == slot_ref[1:2, :])
    right = onehot(here == slot_ref[2:3, :])
    out_ref[:, :WIDTH] = dot(head, unit_ref[...]).astype(BF16)
    out_ref[:, WIDTH:META] = (dot(left, unit_ref[:, :HALFW]) + dot(right, unit_ref[:, HALFW:])).astype(BF16)
    out_ref[:, META:] = meta_ref[pl.ds(pl.multiple_of(base, rows), rows), :].astype(BF16)


def place_documents(embed, group, half):
    steps = 4
    far = pl.BlockSpec(memory_space=pltpu.HBM)
    operands = [pltpu.with_memory_space_constraint(x, pltpu.HBM) for x in (embed, group, half)]
    return pl.pallas_call(
        send_kernel,
        grid=(steps,),
        in_specs=[far, far, far],
        out_specs=[pl.BlockSpec((ROWS // steps, SENT), lambda i: (i, 0)), pl.BlockSpec((8, DOCS), lambda i: (0, 0))],
        out_shape=[jax.ShapeDtypeStruct((ROWS, SENT), BF16), jax.ShapeDtypeStruct((8, DOCS), jnp.int32)],
        scratch_shapes=[
            pltpu.VMEM((DOCS, WIDTH), BF16),
            pltpu.VMEM((1, DOCS), jnp.int32),
            pltpu.VMEM((1, DOCS), jnp.int32),
            pltpu.VMEM((DOCS, WIDTH), BF16),
            pltpu.VMEM((8, DOCS), jnp.int32),
            pltpu.VMEM((ROWS, 128), F32),
            pltpu.SemaphoreType.DMA((2 + PARTS,)),
        ],
        compiler_params=pltpu.CompilerParams(vmem_limit_bytes=28 * MIB),
        cost_estimate=pl.CostEstimate(flops=2 * 10**9, bytes_accessed=9 * 2**20, transcendentals=256),
        name="place_documents",
    )(*operands)


def tail_rows(y_ref):
    to = iota((TAIL, ROWS), 0)
    at = iota((TAIL, ROWS), 1)
    want = (to % CHIPS) * HEAD + to // CHIPS
    left = dot(onehot(at == want), y_ref[:, WIDTH:META]).astype(BF16)
    right = dot(onehot(at == want + 4), y_ref[:, WIDTH:META]).astype(BF16)
    return left, right


def lane_counts(y_ref):
    meta = y_ref[:, META:].astype(F32).T[:8, :]
    pick = onehot(iota((ROWS, TAIL), 0) == (iota((ROWS, TAIL), 1) % CHIPS) * HEAD)
    tail = dot(meta.astype(BF16), pick)
    return meta[0:1, :], meta[1:2, :], tail[0:1, :], tail[1:2, :]


def pack_kernel(y_ref, v_ref):
    room = v_ref.shape[0]
    counts = y_ref[:, META:].astype(F32).T[:8, :]
    first = CAP - counts[1:2, :]
    row = (iota((1, ROWS), 1) % HEAD).astype(F32)
    low = row < 4
    over = [row >= first, low & (row + HEAD >= first), ~low & (row + HEAD - 4 >= first)]
    flags = [jnp.where(mask, 1.0, 0.0) for mask in over]
    before = onehot(iota((ROWS, ROWS), 0) < iota((ROWS, ROWS), 1))
    place = dot(jnp.concatenate(flags + [jnp.zeros((5, ROWS), F32)], axis=0).astype(BF16), before)
    count = jnp.sum(flags[0], axis=1, keepdims=True)
    full = jnp.where(count + jnp.sum(flags[1], axis=1, keepdims=True) > room, 1.0, 0.0)
    places = [place[0:1, :], place[1:2, :] + count, place[2:3, :] + count]
    take = [onehot((iota((room, ROWS), 0) == at.astype(jnp.int32)) & mask) for at, mask in zip(places, over)]
    tail = y_ref[:, WIDTH:META]
    v_ref[:, :HALFW] = (dot(take[0], y_ref[:, :HALFW]) + dot(take[1], tail)).astype(BF16)
    v_ref[:, HALFW:WIDTH] = (dot(take[0], y_ref[:, HALFW:WIDTH]) + dot(take[2], tail)).astype(BF16)
    lane = iota((ROWS, 128), 1)
    at = iota((ROWS, 128), 0)

    def about(row):
        return jnp.where(lane == 0, at // HEAD, jnp.where(lane == 1, CAP - 1 - row, jnp.where(lane == 2, 1, 0))).astype(F32).astype(BF16)

    info = dot(take[0], about(at % HEAD)) + dot(take[1], about(at % HEAD + HEAD))
    v_ref[:, WIDTH:] = jnp.where(iota((room, 128), 1) == 3, full, info).astype(BF16)


def slots(tops):
    lane = iota((256, 128), 1)
    at = iota((256, 128), 0)
    head = [jnp.max(jnp.where(lane == at % HEAD, top, -2.0).reshape(32, HEAD, 128), axis=1) for top in tops[:2]]
    tail = jnp.max(jnp.where(lane == at // CHIPS + HEAD, tops[2], -2.0).reshape(4, CHIPS, 128), axis=0)
    return jnp.maximum(jnp.concatenate(head, axis=0), tail)


def own_valid(y_ref):
    own1, _, own2, _ = lane_counts(y_ref)
    ok1 = (iota((1, ROWS), 1) % HEAD).astype(F32) < own1
    ok2 = (iota((1, TAIL), 1) // CHIPS + HEAD).astype(F32) < own2
    return [ok1[:, :256], ok1[:, 256:], ok2]


def row_block(y_ref, x2_ref, block):
    return y_ref[256 * block : 256 * (block + 1), :WIDTH] if block < 2 else x2_ref[...]


def row_max(mine, other, keep):
    return jnp.max(jnp.where(keep, dot_t(mine, other), -2.0), axis=1, keepdims=True)


def off_diagonal(n):
    return iota((n, n), 0) != iota((n, n), 1)


def call(kernel, name, out_shape, flops, *args, mib=28, scratch=()):
    return pl.pallas_call(
        kernel,
        out_shape=out_shape,
        scratch_shapes=list(scratch),
        compiler_params=pltpu.CompilerParams(vmem_limit_bytes=mib * MIB),
        cost_estimate=pl.CostEstimate(flops=int(flops), bytes_accessed=2**20, transcendentals=0),
        name=name,
    )(*args)


def own_kernel(y_ref, best_ref, x2_ref):
    left, right = tail_rows(y_ref)
    x2_ref[:, :HALFW] = left
    x2_ref[:, HALFW:] = right
    ok = own_valid(y_ref)
    tops = []
    for a in range(3):
        mine = row_block(y_ref, x2_ref, a)
        top = jnp.full((256, 1), -2.0, F32)
        for b in range(3):
            keep = ok[b] & off_diagonal(256) if a == b else ok[b]
            top = jnp.maximum(top, row_max(mine, row_block(y_ref, x2_ref, b), keep))
        tops.append(top)
    best_ref[...] = slots(tops)


def cross_kernel(y_ref, x2_ref, s_ref, so_far_ref, best_ref, s2_ref):
    left, right = tail_rows(s_ref)
    s2_ref[:, :HALFW] = left
    s2_ref[:, HALFW:] = right
    ok = own_valid(s_ref)
    tops = []
    for a in range(3):
        mine = row_block(y_ref, x2_ref, a)
        top = jnp.full((256, 1), -2.0, F32)
        for b in range(3):
            top = jnp.maximum(top, row_max(mine, row_block(s_ref, s2_ref, b), ok[b]))
        tops.append(top)
    best_ref[...] = jnp.maximum(so_far_ref[...], slots(tops))


def valid_rows(y_ref):
    counts = y_ref[:, META:].astype(F32)
    head = (iota((ROWS, 1), 0) % HEAD).astype(F32) < counts[:, 0:1]
    source = jnp.max(counts.reshape(CHIPS, HEAD, 128), axis=1)
    tail = (iota((TAIL, 1), 0) // CHIPS + HEAD).astype(F32) < jnp.concatenate([source] * 4, axis=0)[:, 0:1]
    return [head[:256], head[256:], tail]


def tiles(room):
    size = min(room, 256)
    return [slice(start, start + size) for start in range(0, room, size)]


def column_max(scores, keep):
    return jnp.max(jnp.where(keep, scores, -2.0), axis=0, keepdims=True)


def received_kernel(s_ref, s2_ref, v_ref, so_far_ref, top_ref):
    ok_s = valid_rows(s_ref)
    used = v_ref[:, WIDTH:].astype(F32)[:, 2:3] > 0.5
    for span in tiles(v_ref.shape[0]):
        mine = v_ref[span, :WIDTH]
        size = mine.shape[0]
        top = jnp.full((1, size), -2.0, F32)
        for b in range(3):
            top = jnp.maximum(top, column_max(dot_t(row_block(s_ref, s2_ref, b), mine), ok_s[b]))
        for at in tiles(v_ref.shape[0]):
            keep = used[at] & off_diagonal(size) if at == span else used[at]
            top = jnp.maximum(top, column_max(dot_t(v_ref[at, :WIDTH], mine), keep))
        top_ref[:, span] = jnp.broadcast_to(top, (8, size))


def sibling_kernel(y_ref, x2_ref, v_ref, w_ref, so_far_ref, so_far_top_ref, out_ref, top_ref):
    room = v_ref.shape[0]
    about_v = v_ref[:, WIDTH:].astype(F32)
    about_w = w_ref[:, WIDTH:].astype(F32)
    lanes = jnp.concatenate([about_v, about_w], axis=0).T[:8, :]
    used = lanes[2:3, :] > 0.5
    ok_y = valid_rows(y_ref)
    tops = [jnp.full((256, 1), -2.0, F32) for _ in range(3)]
    top_ref[...] = so_far_top_ref[...]
    if room <= 128:
        groups = [(jnp.concatenate([v_ref[:, :WIDTH], w_ref[:, :WIDTH]], axis=0), used, slice(0, room))]
    else:
        groups = [(v_ref[span, :WIDTH], used[:, span], span) for span in tiles(room)]
        groups += [(w_ref[span, :WIDTH], used[:, room + span.start : room + span.stop], None) for span in tiles(room)]
    for rows, ok, span in groups:
        for a in range(3):
            scores = dot_t(row_block(y_ref, x2_ref, a), rows)
            tops[a] = jnp.maximum(tops[a], jnp.max(jnp.where(ok, scores, -2.0), axis=1, keepdims=True))
            if span is not None:
                top = column_max(scores, ok_y[a])[:, : span.stop - span.start]
                top_ref[:, span] = jnp.maximum(top_ref[:, span], top)
    best = jnp.maximum(so_far_ref[...], slots(tops))
    for span in tiles(room):
        for at in tiles(room):
            top = column_max(dot_t(w_ref[at, :WIDTH], v_ref[span, :WIDTH]), about_w[at, 2:3] > 0.5)
            top_ref[:, span] = jnp.maximum(top_ref[:, span], top)
    source = lanes[0:1, :room].astype(jnp.int32)
    here = (iota((CHIPS, room), 0) == source) & used[:, :room]
    rank = onehot((iota((room, 128), 1) == about_v[:, 1:2].astype(jnp.int32)) & (about_v[:, 2:3] > 0.5))
    placed = jnp.zeros((CHIPS, 128), F32)
    for piece in split3(jnp.where(here, top_ref[0:1, :], 0.0)):
        placed = placed + dot(piece, rank)
    filled = dot(onehot(here), rank)
    full = jnp.maximum(about_v[0:1, 3:4], about_w[0:1, 3:4])
    out = jnp.where(filled > 0.5, placed, best)
    out_ref[...] = jnp.where(iota((CHIPS, 128), 1) == 127, full, out)


def after_kernel(v_ref, best_ref, out_ref):
    pass


def after(v, best):
    anywhere = pl.BlockSpec(memory_space=pl.ANY)
    return pl.pallas_call(
        after_kernel,
        in_specs=[anywhere, anywhere],
        out_specs=anywhere,
        out_shape=jax.ShapeDtypeStruct(v.shape, v.dtype),
        input_output_aliases={0: 0},
        compiler_params=pltpu.CompilerParams(vmem_limit_bytes=MIB),
        name="overflow_after_own",
    )(v, best)


def owner_side(y, room):
    swap = [(0, 1), (1, 0)]
    mib = 28 if room <= 256 else 52
    slot_shape = jax.ShapeDtypeStruct((CHIPS, 128), F32)
    top_shape = jax.ShapeDtypeStruct((8, room), F32)
    tail_shape = jax.ShapeDtypeStruct((TAIL, WIDTH), BF16)
    packed_shape = jax.ShapeDtypeStruct((room, WIDTH + 128), BF16)
    s = lax.ppermute(y, "core", swap)
    v = call(pack_kernel, "pack_overflow", packed_shape, 3e9, y, mib=mib)
    v = lax.ppermute(v, "x", [(0, 1), (1, 0), (2, 3), (3, 2)])
    best, x2 = call(own_kernel, "own_pairs", [slot_shape, tail_shape], 5e9, y)
    best, s2 = call(cross_kernel, "cross_pairs", [slot_shape, tail_shape], 6e9, y, x2, s, best)
    v = after(v, best)
    w = lax.ppermute(v, "core", swap)
    top = call(received_kernel, "received_pairs", top_shape, 3e9, s, s2, v, best, mib=mib)
    scratch = [pltpu.VMEM((8, room), F32)]
    return call(sibling_kernel, "sibling_pairs", slot_shape, 1e9, y, x2, v, w, best, top, mib=mib, scratch=scratch)


def pick_kernel(back_ref, rank_ref, out_ref, full_ref):
    rank = rank_ref[0:1, :]
    cluster = rank_ref[1:2, :]
    at_rank = onehot(iota((128, DOCS), 0) == rank)
    back = back_ref[...]
    found = jnp.zeros((CHIPS, DOCS), F32)
    for piece in split3(back):
        found = found + dot(piece, at_rank)
    out_ref[...] = jnp.sum(jnp.where(iota((CHIPS, DOCS), 0) == cluster, found, 0.0), axis=0, keepdims=True)
    full_ref[0, 0] = jnp.where(jnp.max(back[:, 127:128]) > 0.5, 1, 0)


def return_to_source(best, rank):
    back = lax.all_to_all(best, CHIP_AXES, split_axis=0, concat_axis=0, tiled=True)
    return pl.pallas_call(
        pick_kernel,
        out_specs=[pl.BlockSpec(memory_space=pltpu.VMEM), pl.BlockSpec(memory_space=pltpu.SMEM)],
        out_shape=[jax.ShapeDtypeStruct((1, DOCS), F32), jax.ShapeDtypeStruct((1, 1), jnp.int32)],
        compiler_params=pltpu.CompilerParams(vmem_limit_bytes=4 * MIB),
        name="pick_documents",
    )(back, rank)


def next_chip(x, way, core):
    bits = 4 * core if way < 2 else 2
    unit = 1 << bits
    place = (iota(x.shape, 1) >> bits) & 3
    if way % 2 == 0:
        return jnp.where(place == 3, pltpu.roll(x, 3 * unit, axis=1), pltpu.roll(x, 128 - unit, axis=1))
    return jnp.where(place == 0, pltpu.roll(x, 128 - 3 * unit, axis=1), pltpu.roll(x, unit, axis=1))


def neighbour(z, y, x, way, core):
    step = 1 if way % 2 == 0 else 3
    if way < 2:
        x, z = jnp.where(core == 0, (x + step) & 3, x), jnp.where(core == 0, z, (z + step) & 3)
    else:
        y = (y + step) & 3
    return 16 * z + 4 * y + x


def spread_kernel(embed_hbm, group_hbm, half_hbm, out_ref, rank_ref, embed_ref, group_ref, half_ref, unit_ref, note_ref, slot_ref, sems):
    names = [pltpu.make_async_copy(group_hbm, group_ref, sems.at[0]), pltpu.make_async_copy(half_hbm, half_ref, sems.at[1])]
    size = DOCS // PARTS
    spans = [pl.ds(size * part, size) for part in range(PARTS)]
    parts = [pltpu.make_async_copy(embed_hbm.at[span, :], embed_ref.at[span, :], sems.at[2 + i]) for i, span in enumerate(spans)]
    for copy in names + parts:
        copy.start()
    for copy in names:
        copy.wait()
    group, half = group_ref[...], half_ref[...]
    z, y, x = ((group >> 4) + 2 * half) & 3, ((group >> 2) + 2 * half) & 3, (group + 2 * half) & 3
    home = 16 * z + 4 * y + x
    member = onehot((iota((2 * CHIPS, DOCS), 0) & (CHIPS - 1)) == home)
    earlier = onehot(iota((DOCS, DOCS), 0) < iota((DOCS, DOCS), 1))
    before = dot(member[:CHIPS], earlier)
    rank = jnp.sum(before * member[:CHIPS].astype(F32), axis=0, keepdims=True)
    counts = dot_t(jnp.ones((8, DOCS), BF16), member)
    left = jnp.maximum(counts - SLOTS, 0.0)
    free = SLOTS - jnp.minimum(counts, float(SLOTS))
    given = [jnp.zeros((8, 2 * CHIPS), F32) for _ in range(WAYS)]
    core = lax.axis_index("core")
    turn = (21 * lax.axis_index("z") + 5 * lax.axis_index("y") + lax.axis_index("x")) % 6
    early = jnp.where(turn < 3, 1.0, 0.0)
    plan = [(0, early), (1, 1.0), (0, 1.0 - early), (2, early), (3, 1.0), (2, 1.0 - early), (0, 1.0), (1, 1.0)]
    plan += [(d, 24.0) for d in range(WAYS)]
    for part, (copy, span) in enumerate(zip(parts, spans)):
        copy.wait()
        floats = embed_ref[span, :].astype(F32)
        scale = lax.rsqrt(jnp.sum(floats * floats, axis=1, keepdims=True) + 1e-06)
        unit_ref[span, :] = (floats * scale).astype(BF16)
        for d, most in plan[3 * part : 3 * part + 3]:
            take = jnp.minimum(jnp.minimum(left, next_chip(free, d, core)), most)
            given[d] = given[d] + take
            left = left - take
            free = free - next_chip(take, d ^ 1, core)
    ends, offsets = [], []
    total, used = jnp.zeros_like(left), jnp.zeros_like(left)
    for d in range(WAYS):
        total = total + given[d]
        ends.append(total)
        offsets.append(next_chip(used, d, core))
        used = used + next_chip(given[d], d ^ 1, core)
    table = jnp.concatenate([row[0:1] for row in ends + offsets] + [jnp.zeros((8, 2 * CHIPS), F32)], axis=0)
    table = jnp.where(iota(table.shape, 1) < CHIPS, table, 0.0)
    found = dot(table.astype(BF16), member)
    beyond = rank - SLOTS
    own = beyond < 0.0
    chip = home
    row = jnp.where(own, rank.astype(jnp.int32), -1)
    came = jnp.zeros((1, DOCS), F32)
    for d in range(WAYS):
        start = found[d - 1 : d] if d else jnp.zeros((1, DOCS), F32)
        this = (beyond >= start) & (beyond < found[d : d + 1])
        offset = found[WAYS + d : WAYS + d + 1]
        row = jnp.where(this, SLOTS - 1 - (offset + beyond - start).astype(jnp.int32), row)
        chip = jnp.where(this, neighbour(z, y, x, d, core), chip)
        came = jnp.where(this, d + 1.0, came)
    slot_ref[0:1, :] = jnp.where((row >= 0) & (row < HEAD), chip * HEAD + row, -1)
    slot_ref[1:2, :] = jnp.where(row >= HEAD, chip * HEAD + 4 * (row - HEAD), -8)
    rank_ref[0:1, :] = rank.astype(jnp.int32)
    rank_ref[1:2, :] = home
    lost = jnp.max(jnp.where(row < 0, 1.0, 0.0), axis=1, keepdims=True)
    line = iota((128, DOCS), 0)
    for part in range(2):
        at = line - 8 * part
        notes = jnp.where(at == 0, jnp.where(own, 1.0, 0.0), jnp.where(at == 1, came, jnp.where(at == 2, rank, 0.0)))
        note_ref[part] = jnp.where(at == 3, lost, notes).T.astype(BF16)

    at = iota((ROWS, DOCS), 0)
    whole = onehot(at == slot_ref[0:1, :])
    quarters = jnp.zeros((ROWS, QUARTER), F32)
    notes = dot(whole, note_ref[0])
    for q in range(4):
        span = slice(QUARTER * q, QUARTER * (q + 1))
        out_ref[:, span] = dot(whole, unit_ref[:, span]).astype(BF16)
        this = onehot(at == slot_ref[1:2, :] + q)
        quarters = quarters + dot(this, unit_ref[:, span])
        notes = notes + dot(this, note_ref[1])
    out_ref[:, WIDTH:NOTES] = quarters.astype(BF16)
    out_ref[:, NOTES:] = notes.astype(BF16)


def spread_documents(embed, group, half):
    far = pl.BlockSpec(memory_space=pltpu.HBM)
    operands = [pltpu.with_memory_space_constraint(x, pltpu.HBM) for x in (embed, group, half)]
    return pl.pallas_call(
        spread_kernel,
        in_specs=[far, far, far],
        out_shape=[jax.ShapeDtypeStruct((ROWS, FIRST), BF16), jax.ShapeDtypeStruct((8, DOCS), jnp.int32)],
        scratch_shapes=[
            pltpu.VMEM((DOCS, WIDTH), BF16),
            pltpu.VMEM((1, DOCS), jnp.int32),
            pltpu.VMEM((1, DOCS), jnp.int32),
            pltpu.VMEM((DOCS, WIDTH), BF16),
            pltpu.VMEM((2, DOCS, 128), BF16),
            pltpu.VMEM((8, DOCS), jnp.int32),
            pltpu.SemaphoreType.DMA((2 + PARTS,)),
        ],
        compiler_params=pltpu.CompilerParams(vmem_limit_bytes=28 * MIB),
        cost_estimate=pl.CostEstimate(flops=2 * 10**9, bytes_accessed=9 * 2**20, transcendentals=256),
        name="spread_documents",
    )(*operands)


def quarter_rows(y_ref, out_ref, first):
    to, at = iota((4 * REST, ROWS), 0), iota((4 * REST, ROWS), 1)
    row = to % REST
    want = (row % CHIPS) * HEAD + 4 * (row // CHIPS) + to // REST
    rows = dot(onehot(at == want), y_ref[:, WIDTH:NOTES]).astype(BF16)
    for q in range(4):
        out_ref[first : first + REST, QUARTER * q : QUARTER * (q + 1)] = rows[REST * q : REST * (q + 1)]


def at_home(y_ref):
    notes = y_ref[:, NOTES:].astype(F32).T[:16, :]
    at, to = iota((ROWS, REST), 0), iota((ROWS, REST), 1)
    pick = onehot(at == (to % CHIPS) * HEAD + 4 * (to // CHIPS))
    return notes[0:1, :] > 0.5, dot(notes[8:16, :].astype(BF16), pick)[0:1, :] > 0.5


def sort_kernel(y_ref, *v_refs):
    notes = y_ref[:, NOTES:].astype(F32).T[:16, :]
    quarter = iota((1, ROWS), 1) % 4
    ways = [notes[1:2, :] == d + 1.0 for d in range(WAYS)]
    ways += [(notes[9:10, :] == d + 1.0) & (quarter == q) for q in range(4) for d in range(WAYS)]
    flags = jnp.concatenate([jnp.where(way, 1.0, 0.0) for way in ways] + [jnp.zeros((4, ROWS), F32)], axis=0)
    before = onehot(iota((ROWS, ROWS), 0) < iota((ROWS, ROWS), 1))
    place = dot(flags.astype(BF16), before)
    sums = jnp.sum(flags, axis=1, keepdims=True)
    loads = [sums[d : d + 1] + sums[WAYS + d : WAYS + d + 1] - ROOMS[d] for d in range(WAYS)]
    most = functools.reduce(jnp.maximum, loads)
    lost = jnp.max(jnp.maximum(notes[3:4, :], notes[11:12, :]), axis=1, keepdims=True)
    full = jnp.where((most > 0.5) | (lost > 0.5), 1.0, 0.0)

    def take(first, shift):
        rows = []
        for d in range(WAYS):
            slot = iota((ROOMS[d], ROWS), 0)
            to = place[first + d : first + d + 1, :] + (sums[d : d + 1, :] if shift else 0.0)
            rows.append(jnp.where((slot == to.astype(jnp.int32)) & ways[first + d], 1.0, 0.0))
        return jnp.concatenate(rows, axis=0).astype(BF16)

    whole = take(0, False)
    lane = iota((ROWS, 128), 1)
    source = (iota((ROWS, 128), 0) // HEAD).astype(F32)
    extra = jnp.where(lane == 4, source, jnp.where(lane == 5, 1.0, 0.0))
    given = y_ref[:, NOTES:].astype(F32)
    info = dot(whole, jnp.where(lane == 2, given, extra).astype(BF16))
    some = jnp.concatenate([take(WAYS * (1 + q), True) for q in range(4)], axis=0)
    quarters = dot(some, y_ref[:, WIDTH:NOTES])
    for q in range(4):
        span = slice(QUARTER * q, QUARTER * (q + 1))
        rows = (dot(whole, y_ref[:, span]) + quarters[OVER * q : OVER * (q + 1)]).astype(BF16)
        for d in range(WAYS):
            v_refs[d][:, span] = rows[STARTS[d] : STARTS[d] + ROOMS[d]]
        if q == 0:
            moved = jnp.where(lane == 2, pltpu.roll(given, 128 - 8, axis=1), extra)
            info = info + dot(some[:OVER], moved.astype(BF16))
    info = jnp.where(iota((OVER, 128), 1) == 3, full, info).astype(BF16)
    for d in range(WAYS):
        v_refs[d][:, WIDTH:] = info[STARTS[d] : STARTS[d] + ROOMS[d]]


def to_slots(top, rest):
    keep = iota((ROWS, 128), 1) == iota((ROWS, 128), 0) % HEAD
    head = jnp.max(jnp.where(keep, top, -2.0).reshape(CHIPS, HEAD, 128), axis=1)
    keep = iota((REST, 128), 1) == iota((REST, 128), 0) // CHIPS + HEAD
    return jnp.maximum(head, jnp.max(jnp.where(keep, rest, -2.0).reshape(2, CHIPS, 128), axis=0))


def upright(line):
    return jnp.broadcast_to(line, (8, line.shape[1])).T[:, 0:1]


def lane_max(scores, keep):
    return jnp.max(jnp.where(keep, scores, -2.0), axis=1, keepdims=True)


def home_kernel(y_ref, best_ref, rest_ref):
    quarter_rows(y_ref, rest_ref, 0)
    ok, _ = at_home(y_ref)
    here = y_ref[:, NOTES:].astype(F32)[:, 0:1] > 0.5
    low, high = y_ref[:256, :WIDTH], y_ref[256:, :WIDTH]
    both = dot_t(low, high)
    top0 = jnp.maximum(row_max(low, low, ok[:, :256] & off_diagonal(256)), lane_max(both, ok[:, 256:]))
    top1 = row_max(high, high, ok[:, 256:] & off_diagonal(256))
    top1 = jnp.maximum(top1, upright(column_max(both, here[:256])))
    best_ref[...] = jnp.broadcast_to(jnp.concatenate([top0, top1], axis=0), (ROWS, 128))


def other_core_kernel(y_ref, s_ref, own_rest_ref, so_far_ref, best_ref, rest_ref):
    rest_ref[:REST] = own_rest_ref[...]
    quarter_rows(s_ref, rest_ref, REST)
    (ok, ok2), (ok_s, ok_s2) = at_home(y_ref), at_home(s_ref)
    theirs = s_ref[:, :WIDTH]
    tops = [row_max(y_ref[256 * a : 256 * (a + 1), :WIDTH], theirs, ok_s) for a in range(2)]
    ok_rest = jnp.concatenate([jnp.where(ok2, 1.0, 0.0), jnp.where(ok_s2, 1.0, 0.0)], axis=1)
    scores = dot_t(rest_ref[...], y_ref[:, :WIDTH])
    beside = column_max(scores, upright(ok_rest) > 0.5)
    top = jnp.maximum(jnp.maximum(jnp.concatenate(tops, axis=0), upright(beside)), so_far_ref[:, 0:1])
    mine = rest_ref[:REST]
    keep = (ok_rest > 0.5) & (iota((REST, 2 * REST), 0) != iota((REST, 2 * REST), 1))
    rest = jnp.maximum(lane_max(scores[:REST], ok), row_max(mine, rest_ref[...], keep))
    best_ref[...] = to_slots(top, jnp.maximum(rest, row_max(mine, theirs, ok_s)))


def join_kernel(*refs):
    out_ref = refs[-1]
    for d in range(WAYS):
        out_ref[STARTS[d] : STARTS[d] + ROOMS[d], :] = refs[d][...]


def notes_of(v_ref):
    return v_ref[:, WIDTH:].astype(F32).T[:8, :]


def guests_kernel(y_ref, s_ref, rest_ref, v_ref, so_far_ref, top_ref, own_ref):
    mine = v_ref[:, :WIDTH]
    used = v_ref[:, WIDTH:].astype(F32)[:, 5:6] > 0.5
    ok_v = notes_of(v_ref)[5:6, :] > 0.5
    top = row_max(mine, mine, ok_v & off_diagonal(OVER))
    (ok, ok2), (ok_s, ok_s2) = at_home(y_ref), at_home(s_ref)
    scores = dot_t(mine, y_ref[:, :WIDTH])
    own_ref[:, :ROWS] = jnp.broadcast_to(column_max(scores, used), (8, ROWS))
    top = jnp.maximum(top, lane_max(scores, ok))
    top = jnp.maximum(top, row_max(mine, s_ref[:, :WIDTH], ok_s))
    scores = dot_t(mine, rest_ref[...])
    own_ref[:, ROWS:] = jnp.broadcast_to(column_max(scores[:, :REST], used), (8, REST))
    top = jnp.maximum(top, jnp.maximum(lane_max(scores[:, :REST], ok2), lane_max(scores[:, REST:], ok_s2)))
    top_ref[...] = jnp.broadcast_to(top, (OVER, 128))


def finish_kernel(y_ref, rest_ref, v_ref, w_ref, so_far_ref, top_ref, own_ref, out_ref):
    about = v_ref[:, WIDTH:].astype(F32)
    about_w = w_ref[:, WIDTH:].astype(F32)
    lanes = notes_of(v_ref)
    theirs = w_ref[:, :WIDTH]
    used = about_w[:, 5:6] > 0.5
    head = jnp.maximum(own_ref[:, :ROWS], column_max(dot_t(theirs, y_ref[:, :WIDTH]), used))
    rest = jnp.maximum(own_ref[:, ROWS:], column_max(dot_t(theirs, rest_ref[:REST]), used))
    best = jnp.maximum(so_far_ref[...], to_slots(head.T[:, 0:1], rest.T[:, 0:1]))
    top = row_max(v_ref[:, :WIDTH], theirs, notes_of(w_ref)[5:6, :] > 0.5)
    top = jnp.maximum(top_ref[...], top)
    here = onehot((iota((CHIPS, OVER), 0) == lanes[4:5, :].astype(jnp.int32)) & (lanes[5:6, :] > 0.5))
    rank = (iota((OVER, 128), 1) == about[:, 2:3].astype(jnp.int32)) & (about[:, 5:6] > 0.5)
    pieces = dot(here, jnp.concatenate([*split3(jnp.where(rank, top, 0.0)), onehot(rank)], axis=1))
    placed = pieces[:, :128] + pieces[:, 128:256] + pieces[:, 256:384]
    filled = pieces[:, 384:]
    full = jnp.maximum(about[0:1, 3:4], about_w[0:1, 3:4])
    out = jnp.where(filled > 0.5, placed, best)
    out_ref[...] = jnp.where(iota((CHIPS, 128), 1) == 127, full, out)


def way_home(way):
    pairs = []
    for z, x, y, core in itertools.product(range(4), range(4), range(4), range(2)):
        to = [z, x, y]
        axis = 2 if way >= 2 else 1 if core == 0 else 0
        to[axis] = (to[axis] + (3 if way % 2 == 0 else 1)) % 4
        pairs.append((32 * z + 8 * x + 2 * y + core, 32 * to[0] + 8 * to[1] + 2 * to[2] + core))
    return pairs


def owner_short(y):
    swap = [(0, 1), (1, 0)]
    slot_shape = jax.ShapeDtypeStruct((CHIPS, 128), F32)
    rest_shape = jax.ShapeDtypeStruct((2 * REST, WIDTH), BF16)
    way_shapes = [jax.ShapeDtypeStruct((room, SHORT), BF16) for room in ROOMS]
    s = lax.ppermute(y, "core", swap)
    ways = call(sort_kernel, "sort_overflow", way_shapes, 3e9, y, mib=20)
    came = []
    for d, v in enumerate(ways):
        came.append(lax.ppermute(v, ALL_AXES, way_home(d)))
    shapes = [jax.ShapeDtypeStruct((ROWS, 128), F32), jax.ShapeDtypeStruct((REST, WIDTH), BF16)]
    best, rest = call(home_kernel, "home_pairs", shapes, 1e10, y, mib=24)
    best, rest = call(other_core_kernel, "other_core_pairs", [slot_shape, rest_shape], 4e10, y, s, rest, best, mib=24)
    v = call(join_kernel, "join_overflow", jax.ShapeDtypeStruct((OVER, SHORT), BF16), 1e8, *came, best, mib=8)
    w = lax.ppermute(v, "core", swap)
    shapes = [jax.ShapeDtypeStruct((OVER, 128), F32), jax.ShapeDtypeStruct((8, OWN), F32)]
    top, own = call(guests_kernel, "guest_pairs", shapes, 6e9, y, s, rest, v, best, mib=24)
    return call(finish_kernel, "finish_pairs", slot_shape, 3e9, y, rest, v, w, best, top, own, mib=24)


def wide_form(embed, group, half):
    sent, rank = place_documents(embed, group, half)
    y = lax.all_to_all(sent, CHIP_AXES, split_axis=0, concat_axis=0, tiled=True)
    return return_to_source(owner_side(y, ROWS + TAIL), rank)[0]


def on_device(embed, group, half):
    group, half = group.reshape(1, DOCS), half.reshape(1, DOCS)
    sent, rank = spread_documents(embed, group, half)
    y = lax.all_to_all(sent, CHIP_AXES, split_axis=0, concat_axis=0, tiled=True)
    nearest, full = return_to_source(owner_short(y), rank)
    nearest = lax.switch(
        full[0, 0],
        [lambda embed, group, half, nearest: nearest, lambda embed, group, half, nearest: wide_form(embed, group, half)],
        embed,
        group,
        half,
        nearest,
    )
    return nearest.reshape(DOCS)


def solution(mesh):
    devices = mesh.devices.reshape(4, 4, 4, 2)
    fine = Mesh(devices, ALL_AXES)
    return jax.shard_map(
        on_device,
        mesh=fine,
        in_specs=(P(ALL_AXES, None), P(ALL_AXES, None), P(ALL_AXES)),
        out_specs=P(ALL_AXES),
        check_vma=False,
    )
```

```python
import functools
import itertools

import jax
import jax.numpy as jnp
from jax import lax
from jax.experimental import pallas as pl
from jax.experimental.pallas import tpu as pltpu
from jax.sharding import Mesh, PartitionSpec as P

WIDTH = 4096
HALFW = WIDTH // 2
CHIPS = 64
DOCS = 256
CAP = 24
SIDE = 12
HEAD = 8
PARTS = 4
ROWS = CHIPS * HEAD
TAIL = CHIPS * (SIDE - HEAD)
META = WIDTH + HALFW
SENT = META + 128
CHIP_AXES = ("z", "x", "y")
SHORT = WIDTH + 128
SLOTS = 10
ROOMS = (64, 64, 32, 32)
WAYS = len(ROOMS)
STARTS = (0, 64, 128, 160)
OVER = sum(ROOMS)
QUARTER = WIDTH // 4
NOTES = WIDTH + QUARTER
FIRST = NOTES + 128
REST = CHIPS * (SLOTS - HEAD)
OWN = ROWS + REST
ALL_AXES = CHIP_AXES + ("core",)
F32 = jnp.float32
BF16 = jnp.bfloat16
MIB = 1024 * 1024


def iota(shape, axis):
    return lax.broadcasted_iota(jnp.int32, shape, axis)


def dot(a, b):
    return jnp.dot(a, b, preferred_element_type=F32)


def dot_t(a, b):
    return lax.dot_general(a, b, (((1,), (1,)), ((), ())), preferred_element_type=F32)


def onehot(mask):
    return jnp.where(mask, 1.0, 0.0).astype(BF16)


def split3(x):
    a = x.astype(BF16)
    rest = x - a.astype(F32)
    b = rest.astype(BF16)
    c = (rest - b.astype(F32)).astype(BF16)
    return a, b, c


def send_kernel(embed_hbm, group_hbm, half_hbm, out_ref, rank_ref, embed_ref, group_ref, half_ref, unit_ref, slot_ref, meta_ref, sems):
    step = pl.program_id(0)

    @pl.when(step == 0)
    def _():
        names = [pltpu.make_async_copy(group_hbm, group_ref, sems.at[0]), pltpu.make_async_copy(half_hbm, half_ref, sems.at[1])]
        size = DOCS // PARTS
        spans = [pl.ds(size * part, size) for part in range(PARTS)]
        parts = [pltpu.make_async_copy(embed_hbm.at[span, :], embed_ref.at[span, :], sems.at[2 + i]) for i, span in enumerate(spans)]
        for copy in names + parts:
            copy.start()
        for copy in names:
            copy.wait()
        cluster = 2 * group_ref[...] + half_ref[...]
        other = cluster + 1 - 2 * half_ref[...]
        member = iota((CHIPS, DOCS), 0) == cluster
        earlier = onehot(iota((DOCS, DOCS), 0) < iota((DOCS, DOCS), 1))
        before = dot(onehot(member), earlier)
        rank = jnp.sum(jnp.where(member, before, 0.0), axis=0, keepdims=True).astype(jnp.int32)
        over = rank >= SIDE
        chip = jnp.where(over, other, cluster)
        row = jnp.where(over, CAP - 1 - rank, rank)
        slot_ref[0:1, :] = jnp.where(row < HEAD, chip * HEAD + row, -1)
        slot_ref[1:2, :] = jnp.where(row >= HEAD, chip * HEAD + row - HEAD, -1)
        slot_ref[2:3, :] = jnp.where(row >= HEAD, chip * HEAD + row - HEAD + 4, -1)
        rank_ref[0:1, :] = rank
        rank_ref[1:2, :] = cluster
        own = jnp.sum(jnp.where(member, 1.0, 0.0), axis=1, keepdims=True)
        oth = jnp.sum(jnp.where(iota((CHIPS, DOCS), 0) == other, 1.0, 0.0), axis=1, keepdims=True)
        lane = iota((CHIPS, 128), 1)
        meta = jnp.where(lane == 0, own, jnp.where(lane == 1, oth, 0.0))
        meta_ref[...] = jnp.broadcast_to(meta[:, None, :], (CHIPS, HEAD, 128)).reshape(ROWS, 128)
        for copy, span in zip(parts, spans):
            copy.wait()
            floats = embed_ref[span, :].astype(F32)
            scale = lax.rsqrt(jnp.sum(floats * floats, axis=1, keepdims=True) + 1e-06)
            unit_ref[span, :] = (floats * scale).astype(BF16)

    rows = out_ref.shape[0]
    base = step * rows
    here = iota((rows, DOCS), 0) + base
    head = onehot(here == slot_ref[0:1, :])
    left = onehot(here == slot_ref[1:2, :])
    right = onehot(here == slot_ref[2:3, :])
    out_ref[:, :WIDTH] = dot(head, unit_ref[...]).astype(BF16)
    out_ref[:, WIDTH:META] = (dot(left, unit_ref[:, :HALFW]) + dot(right, unit_ref[:, HALFW:])).astype(BF16)
    out_ref[:, META:] = meta_ref[pl.ds(pl.multiple_of(base, rows), rows), :].astype(BF16)


def place_documents(embed, group, half):
    steps = 4
    far = pl.BlockSpec(memory_space=pltpu.HBM)
    operands = [pltpu.with_memory_space_constraint(x, pltpu.HBM) for x in (embed, group, half)]
    return pl.pallas_call(
        send_kernel,
        grid=(steps,),
        in_specs=[far, far, far],
        out_specs=[pl.BlockSpec((ROWS // steps, SENT), lambda i: (i, 0)), pl.BlockSpec((8, DOCS), lambda i: (0, 0))],
        out_shape=[jax.ShapeDtypeStruct((ROWS, SENT), BF16), jax.ShapeDtypeStruct((8, DOCS), jnp.int32)],
        scratch_shapes=[
            pltpu.VMEM((DOCS, WIDTH), BF16),
            pltpu.VMEM((1, DOCS), jnp.int32),
            pltpu.VMEM((1, DOCS), jnp.int32),
            pltpu.VMEM((DOCS, WIDTH), BF16),
            pltpu.VMEM((8, DOCS), jnp.int32),
            pltpu.VMEM((ROWS, 128), F32),
            pltpu.SemaphoreType.DMA((2 + PARTS,)),
        ],
        compiler_params=pltpu.CompilerParams(vmem_limit_bytes=28 * MIB),
        cost_estimate=pl.CostEstimate(flops=2 * 10**9, bytes_accessed=9 * 2**20, transcendentals=256),
        name="place_documents",
    )(*operands)


def tail_rows(y_ref):
    to = iota((TAIL, ROWS), 0)
    at = iota((TAIL, ROWS), 1)
    want = (to % CHIPS) * HEAD + to // CHIPS
    left = dot(onehot(at == want), y_ref[:, WIDTH:META]).astype(BF16)
    right = dot(onehot(at == want + 4), y_ref[:, WIDTH:META]).astype(BF16)
    return left, right


def lane_counts(y_ref):
    meta = y_ref[:, META:].astype(F32).T[:8, :]
    pick = onehot(iota((ROWS, TAIL), 0) == (iota((ROWS, TAIL), 1) % CHIPS) * HEAD)
    tail = dot(meta.astype(BF16), pick)
    return meta[0:1, :], meta[1:2, :], tail[0:1, :], tail[1:2, :]


def pack_kernel(y_ref, v_ref):
    room = v_ref.shape[0]
    counts = y_ref[:, META:].astype(F32).T[:8, :]
    first = CAP - counts[1:2, :]
    row = (iota((1, ROWS), 1) % HEAD).astype(F32)
    low = row < 4
    over = [row >= first, low & (row + HEAD >= first), ~low & (row + HEAD - 4 >= first)]
    flags = [jnp.where(mask, 1.0, 0.0) for mask in over]
    before = onehot(iota((ROWS, ROWS), 0) < iota((ROWS, ROWS), 1))
    place = dot(jnp.concatenate(flags + [jnp.zeros((5, ROWS), F32)], axis=0).astype(BF16), before)
    count = jnp.sum(flags[0], axis=1, keepdims=True)
    full = jnp.where(count + jnp.sum(flags[1], axis=1, keepdims=True) > room, 1.0, 0.0)
    places = [place[0:1, :], place[1:2, :] + count, place[2:3, :] + count]
    take = [onehot((iota((room, ROWS), 0) == at.astype(jnp.int32)) & mask) for at, mask in zip(places, over)]
    tail = y_ref[:, WIDTH:META]
    v_ref[:, :HALFW] = (dot(take[0], y_ref[:, :HALFW]) + dot(take[1], tail)).astype(BF16)
    v_ref[:, HALFW:WIDTH] = (dot(take[0], y_ref[:, HALFW:WIDTH]) + dot(take[2], tail)).astype(BF16)
    lane = iota((ROWS, 128), 1)
    at = iota((ROWS, 128), 0)

    def about(row):
        return jnp.where(lane == 0, at // HEAD, jnp.where(lane == 1, CAP - 1 - row, jnp.where(lane == 2, 1, 0))).astype(F32).astype(BF16)

    info = dot(take[0], about(at % HEAD)) + dot(take[1], about(at % HEAD + HEAD))
    v_ref[:, WIDTH:] = jnp.where(iota((room, 128), 1) == 3, full, info).astype(BF16)


def slots(tops):
    lane = iota((256, 128), 1)
    at = iota((256, 128), 0)
    head = [jnp.max(jnp.where(lane == at % HEAD, top, -2.0).reshape(32, HEAD, 128), axis=1) for top in tops[:2]]
    tail = jnp.max(jnp.where(lane == at // CHIPS + HEAD, tops[2], -2.0).reshape(4, CHIPS, 128), axis=0)
    return jnp.maximum(jnp.concatenate(head, axis=0), tail)


def own_valid(y_ref):
    own1, _, own2, _ = lane_counts(y_ref)
    ok1 = (iota((1, ROWS), 1) % HEAD).astype(F32) < own1
    ok2 = (iota((1, TAIL), 1) // CHIPS + HEAD).astype(F32) < own2
    return [ok1[:, :256], ok1[:, 256:], ok2]


def row_block(y_ref, x2_ref, block):
    return y_ref[256 * block : 256 * (block + 1), :WIDTH] if block < 2 else x2_ref[...]


def row_max(mine, other, keep):
    return jnp.max(jnp.where(keep, dot_t(mine, other), -2.0), axis=1, keepdims=True)


def off_diagonal(n):
    return iota((n, n), 0) != iota((n, n), 1)


def call(kernel, name, out_shape, flops, *args, mib=28, scratch=()):
    return pl.pallas_call(
        kernel,
        out_shape=out_shape,
        scratch_shapes=list(scratch),
        compiler_params=pltpu.CompilerParams(vmem_limit_bytes=mib * MIB),
        cost_estimate=pl.CostEstimate(flops=int(flops), bytes_accessed=2**20, transcendentals=0),
        name=name,
    )(*args)


def own_kernel(y_ref, best_ref, x2_ref):
    left, right = tail_rows(y_ref)
    x2_ref[:, :HALFW] = left
    x2_ref[:, HALFW:] = right
    ok = own_valid(y_ref)
    tops = []
    for a in range(3):
        mine = row_block(y_ref, x2_ref, a)
        top = jnp.full((256, 1), -2.0, F32)
        for b in range(3):
            keep = ok[b] & off_diagonal(256) if a == b else ok[b]
            top = jnp.maximum(top, row_max(mine, row_block(y_ref, x2_ref, b), keep))
        tops.append(top)
    best_ref[...] = slots(tops)


def cross_kernel(y_ref, x2_ref, s_ref, so_far_ref, best_ref, s2_ref):
    left, right = tail_rows(s_ref)
    s2_ref[:, :HALFW] = left
    s2_ref[:, HALFW:] = right
    ok = own_valid(s_ref)
    tops = []
    for a in range(3):
        mine = row_block(y_ref, x2_ref, a)
        top = jnp.full((256, 1), -2.0, F32)
        for b in range(3):
            top = jnp.maximum(top, row_max(mine, row_block(s_ref, s2_ref, b), ok[b]))
        tops.append(top)
    best_ref[...] = jnp.maximum(so_far_ref[...], slots(tops))


def valid_rows(y_ref):
    counts = y_ref[:, META:].astype(F32)
    head = (iota((ROWS, 1), 0) % HEAD).astype(F32) < counts[:, 0:1]
    source = jnp.max(counts.reshape(CHIPS, HEAD, 128), axis=1)
    tail = (iota((TAIL, 1), 0) // CHIPS + HEAD).astype(F32) < jnp.concatenate([source] * 4, axis=0)[:, 0:1]
    return [head[:256], head[256:], tail]


def tiles(room):
    size = min(room, 256)
    return [slice(start, start + size) for start in range(0, room, size)]


def column_max(scores, keep):
    return jnp.max(jnp.where(keep, scores, -2.0), axis=0, keepdims=True)


def received_kernel(s_ref, s2_ref, v_ref, so_far_ref, top_ref):
    room = v_ref.shape[0]

    def step(i, carry):
        start = pl.multiple_of(i * 256, 256)
        mine = v_ref[pl.ds(start, 256), :WIDTH]
        ok_s = valid_rows(s_ref)
        used = v_ref[:, WIDTH:].astype(F32)[:, 2:3] > 0.5
        top = jnp.full((1, 256), -2.0, F32)
        for b in range(3):
            top = jnp.maximum(top, column_max(dot_t(row_block(s_ref, s2_ref, b), mine), ok_s[b]))
        for at in tiles(room):
            keep = used[at] & (iota((256, 256), 0) + at.start != iota((256, 256), 1) + start)
            top = jnp.maximum(top, column_max(dot_t(v_ref[at, :WIDTH], mine), keep))
        top_ref[:, pl.ds(start, 256)] = jnp.broadcast_to(top, (8, 256))
        return carry

    lax.fori_loop(0, room // 256, step, 0)


def sibling_kernel(y_ref, x2_ref, v_ref, w_ref, so_far_ref, so_far_top_ref, out_ref, top_ref, best_ref, lane_ref):
    room = v_ref.shape[0]
    about_v = v_ref[:, WIDTH:].astype(F32)
    about_w = w_ref[:, WIDTH:].astype(F32)
    lanes = jnp.concatenate([about_v, about_w], axis=0).T[:8, :]
    lane_ref[...] = lanes
    used = lanes[2:3, :] > 0.5
    top_ref[...] = so_far_top_ref[...]
    best_ref[...] = jnp.full(best_ref.shape, -2.0, F32)

    def step(i, carry):
        start = pl.multiple_of(i * 256, 256)
        ok_y = valid_rows(y_ref)
        for ref, first in ((v_ref, 0), (w_ref, room)):
            rows = ref[pl.ds(start, 256), :WIDTH]
            ok = lane_ref[2:3, pl.ds(start + first, 256)] > 0.5
            top = top_ref[:, pl.ds(start, 256)]
            for a in range(3):
                scores = dot_t(row_block(y_ref, x2_ref, a), rows)
                best = jnp.max(jnp.where(ok, scores, -2.0), axis=1, keepdims=True)
                span = slice(256 * a, 256 * (a + 1))
                best_ref[span, :] = jnp.maximum(best_ref[span, :], best)
                top = jnp.maximum(top, column_max(scores, ok_y[a]))
            if first == 0:
                for at in tiles(room):
                    theirs = w_ref[at, WIDTH:].astype(F32)[:, 2:3] > 0.5
                    top = jnp.maximum(top, column_max(dot_t(w_ref[at, :WIDTH], rows), theirs))
                top_ref[:, pl.ds(start, 256)] = top
        return carry

    lax.fori_loop(0, room // 256, step, 0)
    best = jnp.maximum(so_far_ref[...], slots([best_ref[256 * a : 256 * (a + 1), 0:1] for a in range(3)]))
    source = lanes[0:1, :room].astype(jnp.int32)
    here = (iota((CHIPS, room), 0) == source) & used[:, :room]
    rank = onehot((iota((room, 128), 1) == about_v[:, 1:2].astype(jnp.int32)) & (about_v[:, 2:3] > 0.5))
    placed = jnp.zeros((CHIPS, 128), F32)
    for piece in split3(jnp.where(here, top_ref[0:1, :], 0.0)):
        placed = placed + dot(piece, rank)
    filled = dot(onehot(here), rank)
    full = jnp.maximum(about_v[0:1, 3:4], about_w[0:1, 3:4])
    out = jnp.where(filled > 0.5, placed, best)
    out_ref[...] = jnp.where(iota((CHIPS, 128), 1) == 127, full, out)


def after_kernel(v_ref, best_ref, out_ref):
    pass


def after(v, best):
    anywhere = pl.BlockSpec(memory_space=pl.ANY)
    return pl.pallas_call(
        after_kernel,
        in_specs=[anywhere, anywhere],
        out_specs=anywhere,
        out_shape=jax.ShapeDtypeStruct(v.shape, v.dtype),
        input_output_aliases={0: 0},
        compiler_params=pltpu.CompilerParams(vmem_limit_bytes=MIB),
        name="overflow_after_own",
    )(v, best)


def owner_side(y, room):
    swap = [(0, 1), (1, 0)]
    mib = 28 if room <= 256 else 52
    slot_shape = jax.ShapeDtypeStruct((CHIPS, 128), F32)
    top_shape = jax.ShapeDtypeStruct((8, room), F32)
    tail_shape = jax.ShapeDtypeStruct((TAIL, WIDTH), BF16)
    packed_shape = jax.ShapeDtypeStruct((room, WIDTH + 128), BF16)
    s = lax.ppermute(y, "core", swap)
    v = call(pack_kernel, "pack_overflow", packed_shape, 3e9, y, mib=mib)
    v = lax.ppermute(v, "y", [(0, 1), (1, 0), (2, 3), (3, 2)])
    best, x2 = call(own_kernel, "own_pairs", [slot_shape, tail_shape], 5e9, y)
    best, s2 = call(cross_kernel, "cross_pairs", [slot_shape, tail_shape], 6e9, y, x2, s, best)
    v = after(v, best)
    w = lax.ppermute(v, "core", swap)
    top = call(received_kernel, "received_pairs", top_shape, 3e9, s, s2, v, best, mib=mib)
    scratch = [pltpu.VMEM((8, room), F32), pltpu.VMEM((ROWS + TAIL, 128), F32), pltpu.VMEM((8, 2 * room), F32)]
    return call(sibling_kernel, "sibling_pairs", slot_shape, 1e9, y, x2, v, w, best, top, mib=mib, scratch=scratch)


def pick_kernel(back_ref, rank_ref, out_ref, full_ref):
    rank = rank_ref[0:1, :]
    cluster = rank_ref[1:2, :]
    at_rank = onehot(iota((128, DOCS), 0) == rank)
    back = back_ref[...]
    found = jnp.zeros((CHIPS, DOCS), F32)
    for piece in split3(back):
        found = found + dot(piece, at_rank)
    out_ref[...] = jnp.sum(jnp.where(iota((CHIPS, DOCS), 0) == cluster, found, 0.0), axis=0, keepdims=True)
    full_ref[0, 0] = jnp.max(back[:, 127:128])


def return_to_source(best, rank):
    back = lax.all_to_all(best, CHIP_AXES, split_axis=0, concat_axis=0, tiled=True)
    return pl.pallas_call(
        pick_kernel,
        out_specs=[pl.BlockSpec(memory_space=pltpu.VMEM), pl.BlockSpec(memory_space=pltpu.SMEM)],
        out_shape=[jax.ShapeDtypeStruct((1, DOCS), F32), jax.ShapeDtypeStruct((1, 1), F32)],
        compiler_params=pltpu.CompilerParams(vmem_limit_bytes=4 * MIB),
        name="pick_documents",
    )(back, rank)


def next_chip(x, way, core):
    bits = 4 * core if way < 2 else 2
    unit = 1 << bits
    place = (iota(x.shape, 1) >> bits) & 3
    if way % 2 == 0:
        return jnp.where(place == 3, pltpu.roll(x, 3 * unit, axis=1), pltpu.roll(x, 128 - unit, axis=1))
    return jnp.where(place == 0, pltpu.roll(x, 128 - 3 * unit, axis=1), pltpu.roll(x, unit, axis=1))


def neighbour(z, x, y, way, core):
    step = 1 if way % 2 == 0 else 3
    if way < 2:
        y, z = jnp.where(core == 0, (y + step) & 3, y), jnp.where(core == 0, z, (z + step) & 3)
    else:
        x = (x + step) & 3
    return 16 * z + 4 * x + y


def spread_kernel(embed_hbm, group_hbm, half_hbm, out_ref, rank_ref, embed_ref, group_ref, half_ref, unit_ref, note_ref, slot_ref, sems):
    names = [pltpu.make_async_copy(group_hbm, group_ref, sems.at[0]), pltpu.make_async_copy(half_hbm, half_ref, sems.at[1])]
    size = DOCS // PARTS
    spans = [pl.ds(size * part, size) for part in range(PARTS)]
    parts = [pltpu.make_async_copy(embed_hbm.at[span, :], embed_ref.at[span, :], sems.at[2 + i]) for i, span in enumerate(spans)]
    for copy in names + parts:
        copy.start()
    for copy in names:
        copy.wait()
    group, half = group_ref[...], half_ref[...]
    z, x, y = ((group >> 4) + 2 * half) & 3, ((group >> 2) + 2 * half) & 3, (group + 2 * half) & 3
    home = 16 * z + 4 * x + y
    member = onehot((iota((2 * CHIPS, DOCS), 0) & (CHIPS - 1)) == home)
    earlier = onehot(iota((DOCS, DOCS), 0) < iota((DOCS, DOCS), 1))
    before = dot(member[:CHIPS], earlier)
    rank = jnp.sum(before * member[:CHIPS].astype(F32), axis=0, keepdims=True)
    counts = dot_t(jnp.ones((8, DOCS), BF16), member)
    left = jnp.maximum(counts - SLOTS, 0.0)
    free = SLOTS - jnp.minimum(counts, float(SLOTS))
    given = [jnp.zeros((8, 2 * CHIPS), F32) for _ in range(WAYS)]
    core = lax.axis_index("core")
    turn = (21 * lax.axis_index("z") + 5 * lax.axis_index("x") + lax.axis_index("y")) % 6
    early = jnp.where(turn < 3, 1.0, 0.0)
    plan = [(0, early), (1, 1.0), (0, 1.0 - early), (2, early), (3, 1.0), (2, 1.0 - early), (0, 1.0), (1, 1.0)]
    plan += [(d, 24.0) for d in range(WAYS)]
    for part, (copy, span) in enumerate(zip(parts, spans)):
        copy.wait()
        floats = embed_ref[span, :].astype(F32)
        scale = lax.rsqrt(jnp.sum(floats * floats, axis=1, keepdims=True) + 1e-06)
        unit_ref[span, :] = (floats * scale).astype(BF16)
        for d, most in plan[3 * part : 3 * part + 3]:
            take = jnp.minimum(jnp.minimum(left, next_chip(free, d, core)), most)
            given[d] = given[d] + take
            left = left - take
            free = free - next_chip(take, d ^ 1, core)
    ends, offsets = [], []
    total, used = jnp.zeros_like(left), jnp.zeros_like(left)
    for d in range(WAYS):
        total = total + given[d]
        ends.append(total)
        offsets.append(next_chip(used, d, core))
        used = used + next_chip(given[d], d ^ 1, core)
    table = jnp.concatenate([row[0:1] for row in ends + offsets] + [jnp.zeros((8, 2 * CHIPS), F32)], axis=0)
    table = jnp.where(iota(table.shape, 1) < CHIPS, table, 0.0)
    found = dot(table.astype(BF16), member)
    beyond = rank - SLOTS
    own = beyond < 0.0
    chip = home
    row = jnp.where(own, rank.astype(jnp.int32), -1)
    came = jnp.zeros((1, DOCS), F32)
    for d in range(WAYS):
        start = found[d - 1 : d] if d else jnp.zeros((1, DOCS), F32)
        this = (beyond >= start) & (beyond < found[d : d + 1])
        offset = found[WAYS + d : WAYS + d + 1]
        row = jnp.where(this, SLOTS - 1 - (offset + beyond - start).astype(jnp.int32), row)
        chip = jnp.where(this, neighbour(z, x, y, d, core), chip)
        came = jnp.where(this, d + 1.0, came)
    slot_ref[0:1, :] = jnp.where((row >= 0) & (row < HEAD), chip * HEAD + row, -1)
    slot_ref[1:2, :] = jnp.where(row >= HEAD, chip * HEAD + 4 * (row - HEAD), -8)
    rank_ref[0:1, :] = rank.astype(jnp.int32)
    rank_ref[1:2, :] = home
    lost = jnp.max(jnp.where(row < 0, 1.0, 0.0), axis=1, keepdims=True)
    line = iota((128, DOCS), 0)
    for part in range(2):
        at = line - 8 * part
        notes = jnp.where(at == 0, jnp.where(own, 1.0, 0.0), jnp.where(at == 1, came, jnp.where(at == 2, rank, 0.0)))
        note_ref[part] = jnp.where(at == 3, lost, notes).T.astype(BF16)

    at = iota((ROWS, DOCS), 0)
    whole = onehot(at == slot_ref[0:1, :])
    quarters = jnp.zeros((ROWS, QUARTER), F32)
    notes = dot(whole, note_ref[0])
    for q in range(4):
        span = slice(QUARTER * q, QUARTER * (q + 1))
        out_ref[:, span] = dot(whole, unit_ref[:, span]).astype(BF16)
        this = onehot(at == slot_ref[1:2, :] + q)
        quarters = quarters + dot(this, unit_ref[:, span])
        notes = notes + dot(this, note_ref[1])
    out_ref[:, WIDTH:NOTES] = quarters.astype(BF16)
    out_ref[:, NOTES:] = notes.astype(BF16)


def spread_documents(embed, group, half):
    far = pl.BlockSpec(memory_space=pltpu.HBM)
    operands = [pltpu.with_memory_space_constraint(x, pltpu.HBM) for x in (embed, group, half)]
    return pl.pallas_call(
        spread_kernel,
        in_specs=[far, far, far],
        out_shape=[jax.ShapeDtypeStruct((ROWS, FIRST), BF16), jax.ShapeDtypeStruct((8, DOCS), jnp.int32)],
        scratch_shapes=[
            pltpu.VMEM((DOCS, WIDTH), BF16),
            pltpu.VMEM((1, DOCS), jnp.int32),
            pltpu.VMEM((1, DOCS), jnp.int32),
            pltpu.VMEM((DOCS, WIDTH), BF16),
            pltpu.VMEM((2, DOCS, 128), BF16),
            pltpu.VMEM((8, DOCS), jnp.int32),
            pltpu.SemaphoreType.DMA((2 + PARTS,)),
        ],
        compiler_params=pltpu.CompilerParams(vmem_limit_bytes=28 * MIB),
        cost_estimate=pl.CostEstimate(flops=2 * 10**9, bytes_accessed=9 * 2**20, transcendentals=256),
        name="spread_documents",
    )(*operands)


def quarter_rows(y_ref, out_ref, first):
    to, at = iota((4 * REST, ROWS), 0), iota((4 * REST, ROWS), 1)
    row = to % REST
    want = (row % CHIPS) * HEAD + 4 * (row // CHIPS) + to // REST
    rows = dot(onehot(at == want), y_ref[:, WIDTH:NOTES]).astype(BF16)
    for q in range(4):
        out_ref[first : first + REST, QUARTER * q : QUARTER * (q + 1)] = rows[REST * q : REST * (q + 1)]


def at_home(y_ref):
    notes = y_ref[:, NOTES:].astype(F32).T[:16, :]
    at, to = iota((ROWS, REST), 0), iota((ROWS, REST), 1)
    pick = onehot(at == (to % CHIPS) * HEAD + 4 * (to // CHIPS))
    return notes[0:1, :] > 0.5, dot(notes[8:16, :].astype(BF16), pick)[0:1, :] > 0.5


def sort_kernel(y_ref, *v_refs):
    notes = y_ref[:, NOTES:].astype(F32).T[:16, :]
    quarter = iota((1, ROWS), 1) % 4
    ways = [notes[1:2, :] == d + 1.0 for d in range(WAYS)]
    ways += [(notes[9:10, :] == d + 1.0) & (quarter == q) for q in range(4) for d in range(WAYS)]
    flags = jnp.concatenate([jnp.where(way, 1.0, 0.0) for way in ways] + [jnp.zeros((4, ROWS), F32)], axis=0)
    before = onehot(iota((ROWS, ROWS), 0) < iota((ROWS, ROWS), 1))
    place = dot(flags.astype(BF16), before)
    sums = jnp.sum(flags, axis=1, keepdims=True)
    loads = [sums[d : d + 1] + sums[WAYS + d : WAYS + d + 1] - ROOMS[d] for d in range(WAYS)]
    most = functools.reduce(jnp.maximum, loads)
    lost = jnp.max(jnp.maximum(notes[3:4, :], notes[11:12, :]), axis=1, keepdims=True)
    full = jnp.where((most > 0.5) | (lost > 0.5), 1.0, 0.0)

    def take(first, shift):
        rows = []
        for d in range(WAYS):
            slot = iota((ROOMS[d], ROWS), 0)
            to = place[first + d : first + d + 1, :] + (sums[d : d + 1, :] if shift else 0.0)
            rows.append(jnp.where((slot == to.astype(jnp.int32)) & ways[first + d], 1.0, 0.0))
        return jnp.concatenate(rows, axis=0).astype(BF16)

    whole = take(0, False)
    lane = iota((ROWS, 128), 1)
    source = (iota((ROWS, 128), 0) // HEAD).astype(F32)
    extra = jnp.where(lane == 4, source, jnp.where(lane == 5, 1.0, 0.0))
    given = y_ref[:, NOTES:].astype(F32)
    info = dot(whole, jnp.where(lane == 2, given, extra).astype(BF16))
    some = jnp.concatenate([take(WAYS * (1 + q), True) for q in range(4)], axis=0)
    quarters = dot(some, y_ref[:, WIDTH:NOTES])
    for q in range(4):
        span = slice(QUARTER * q, QUARTER * (q + 1))
        rows = (dot(whole, y_ref[:, span]) + quarters[OVER * q : OVER * (q + 1)]).astype(BF16)
        for d in range(WAYS):
            v_refs[d][:, span] = rows[STARTS[d] : STARTS[d] + ROOMS[d]]
        if q == 0:
            moved = jnp.where(lane == 2, pltpu.roll(given, 128 - 8, axis=1), extra)
            info = info + dot(some[:OVER], moved.astype(BF16))
    info = jnp.where(iota((OVER, 128), 1) == 3, full, info).astype(BF16)
    for d in range(WAYS):
        v_refs[d][:, WIDTH:] = info[STARTS[d] : STARTS[d] + ROOMS[d]]


def to_slots(top, rest):
    keep = iota((ROWS, 128), 1) == iota((ROWS, 128), 0) % HEAD
    head = jnp.max(jnp.where(keep, top, -2.0).reshape(CHIPS, HEAD, 128), axis=1)
    keep = iota((REST, 128), 1) == iota((REST, 128), 0) // CHIPS + HEAD
    return jnp.maximum(head, jnp.max(jnp.where(keep, rest, -2.0).reshape(2, CHIPS, 128), axis=0))


def upright(line):
    return jnp.broadcast_to(line, (8, line.shape[1])).T[:, 0:1]


def lane_max(scores, keep):
    return jnp.max(jnp.where(keep, scores, -2.0), axis=1, keepdims=True)


def home_kernel(y_ref, s_ref, best_ref, rest_ref):
    quarter_rows(y_ref, rest_ref, 0)
    quarter_rows(s_ref, rest_ref, REST)
    (ok, ok2), (ok_s, ok_s2) = at_home(y_ref), at_home(s_ref)
    here = y_ref[:, NOTES:].astype(F32)[:, 0:1] > 0.5
    low, high, theirs = y_ref[:256, :WIDTH], y_ref[256:, :WIDTH], s_ref[:, :WIDTH]
    both = dot_t(low, high)
    top0 = jnp.maximum(row_max(low, low, ok[:, :256] & off_diagonal(256)), lane_max(both, ok[:, 256:]))
    top1 = row_max(high, high, ok[:, 256:] & off_diagonal(256))
    top0 = jnp.maximum(top0, row_max(low, theirs, ok_s))
    top1 = jnp.maximum(top1, row_max(high, theirs, ok_s))
    beside1 = column_max(both, here[:256])
    ok_rest = jnp.concatenate([jnp.where(ok2, 1.0, 0.0), jnp.where(ok_s2, 1.0, 0.0)], axis=1)
    scores = dot_t(rest_ref[...], y_ref[:, :WIDTH])
    beside = column_max(scores, upright(ok_rest) > 0.5)
    beside = jnp.concatenate([beside[:, :256], jnp.maximum(beside[:, 256:], beside1)], axis=1)
    top = jnp.maximum(jnp.concatenate([top0, top1], axis=0), upright(beside))
    mine = rest_ref[:REST]
    keep = (ok_rest > 0.5) & (iota((REST, 2 * REST), 0) != iota((REST, 2 * REST), 1))
    rest = jnp.maximum(lane_max(scores[:REST], ok), row_max(mine, rest_ref[...], keep))
    best_ref[...] = to_slots(top, jnp.maximum(rest, row_max(mine, theirs, ok_s)))


def join_kernel(*refs):
    out_ref = refs[-1]
    for d in range(WAYS):
        out_ref[STARTS[d] : STARTS[d] + ROOMS[d], :] = refs[d][...]


def notes_of(v_ref):
    return v_ref[:, WIDTH:].astype(F32).T[:8, :]


def guests_kernel(y_ref, s_ref, rest_ref, v_ref, so_far_ref, top_ref, own_ref):
    mine = v_ref[:, :WIDTH]
    used = v_ref[:, WIDTH:].astype(F32)[:, 5:6] > 0.5
    ok_v = notes_of(v_ref)[5:6, :] > 0.5
    top = row_max(mine, mine, ok_v & off_diagonal(OVER))
    (ok, ok2), (ok_s, ok_s2) = at_home(y_ref), at_home(s_ref)
    scores = dot_t(mine, y_ref[:, :WIDTH])
    own_ref[:, :ROWS] = jnp.broadcast_to(column_max(scores, used), (8, ROWS))
    top = jnp.maximum(top, lane_max(scores, ok))
    top = jnp.maximum(top, row_max(mine, s_ref[:, :WIDTH], ok_s))
    scores = dot_t(mine, rest_ref[...])
    own_ref[:, ROWS:] = jnp.broadcast_to(column_max(scores[:, :REST], used), (8, REST))
    top = jnp.maximum(top, jnp.maximum(lane_max(scores[:, :REST], ok2), lane_max(scores[:, REST:], ok_s2)))
    top_ref[...] = jnp.broadcast_to(top, (OVER, 128))


def finish_kernel(y_ref, rest_ref, v_ref, w_ref, so_far_ref, top_ref, own_ref, out_ref):
    about = v_ref[:, WIDTH:].astype(F32)
    about_w = w_ref[:, WIDTH:].astype(F32)
    lanes = notes_of(v_ref)
    theirs = w_ref[:, :WIDTH]
    used = about_w[:, 5:6] > 0.5
    head = jnp.maximum(own_ref[:, :ROWS], column_max(dot_t(theirs, y_ref[:, :WIDTH]), used))
    rest = jnp.maximum(own_ref[:, ROWS:], column_max(dot_t(theirs, rest_ref[:REST]), used))
    best = jnp.maximum(so_far_ref[...], to_slots(head.T[:, 0:1], rest.T[:, 0:1]))
    top = row_max(v_ref[:, :WIDTH], theirs, notes_of(w_ref)[5:6, :] > 0.5)
    top = jnp.maximum(top_ref[...], top)
    here = onehot((iota((CHIPS, OVER), 0) == lanes[4:5, :].astype(jnp.int32)) & (lanes[5:6, :] > 0.5))
    rank = (iota((OVER, 128), 1) == about[:, 2:3].astype(jnp.int32)) & (about[:, 5:6] > 0.5)
    pieces = dot(here, jnp.concatenate([*split3(jnp.where(rank, top, 0.0)), onehot(rank)], axis=1))
    placed = pieces[:, :128] + pieces[:, 128:256] + pieces[:, 256:384]
    filled = pieces[:, 384:]
    full = jnp.maximum(about[0:1, 3:4], about_w[0:1, 3:4])
    out = jnp.where(filled > 0.5, placed, best)
    out_ref[...] = jnp.where(iota((CHIPS, 128), 1) == 127, full, out)


def way_home(way):
    pairs = []
    for z, x, y, core in itertools.product(range(4), range(4), range(4), range(2)):
        to = [z, x, y]
        axis = 1 if way >= 2 else 2 if core == 0 else 0
        to[axis] = (to[axis] + (3 if way % 2 == 0 else 1)) % 4
        pairs.append((32 * z + 8 * x + 2 * y + core, 32 * to[0] + 8 * to[1] + 2 * to[2] + core))
    return pairs


def owner_short(y):
    swap = [(0, 1), (1, 0)]
    slot_shape = jax.ShapeDtypeStruct((CHIPS, 128), F32)
    rest_shape = jax.ShapeDtypeStruct((2 * REST, WIDTH), BF16)
    way_shapes = [jax.ShapeDtypeStruct((room, SHORT), BF16) for room in ROOMS]
    s = lax.ppermute(y, "core", swap)
    ways = call(sort_kernel, "sort_overflow", way_shapes, 3e9, y, mib=20)
    came = []
    for d, v in enumerate(ways):
        came.append(lax.ppermute(v, ALL_AXES, way_home(d)))
    best, rest = call(home_kernel, "home_pairs", [slot_shape, rest_shape], 4e10, y, s, mib=24)
    v = call(join_kernel, "join_overflow", jax.ShapeDtypeStruct((OVER, SHORT), BF16), 1e8, *came, best, mib=8)
    w = lax.ppermute(v, "core", swap)
    shapes = [jax.ShapeDtypeStruct((OVER, 128), F32), jax.ShapeDtypeStruct((8, OWN), F32)]
    top, own = call(guests_kernel, "guest_pairs", shapes, 6e9, y, s, rest, v, best, mib=24)
    return call(finish_kernel, "finish_pairs", slot_shape, 3e9, y, rest, v, w, best, top, own, mib=24)


def wide_form(embed, group, half):
    sent, rank = place_documents(embed, group, half)
    y = lax.all_to_all(sent, CHIP_AXES, split_axis=0, concat_axis=0, tiled=True)
    return return_to_source(owner_side(y, ROWS + TAIL), rank)[0]


def on_device(embed, group, half):
    group, half = group.reshape(1, DOCS), half.reshape(1, DOCS)
    sent, rank = spread_documents(embed, group, half)
    y = lax.all_to_all(sent, CHIP_AXES, split_axis=0, concat_axis=0, tiled=True)
    nearest, full = return_to_source(owner_short(y), rank)
    nearest = lax.cond(
        full[0, 0] > 0.5,
        lambda embed, group, half, nearest: wide_form(embed, group, half),
        lambda embed, group, half, nearest: nearest,
        embed,
        group,
        half,
        nearest,
    )
    return nearest.reshape(DOCS)


def solution(mesh):
    devices = mesh.devices.reshape(4, 4, 4, 2)
    fine = Mesh(devices, ALL_AXES)
    return jax.shard_map(
        on_device,
        mesh=fine,
        in_specs=(P(ALL_AXES, None), P(ALL_AXES, None), P(ALL_AXES)),
        out_specs=P(ALL_AXES),
        check_vma=False,
    )
```

```python
import functools
import itertools

import jax
import jax.numpy as jnp
from jax import lax
from jax.experimental import pallas as pl
from jax.experimental.pallas import tpu as pltpu
from jax.sharding import Mesh, PartitionSpec as P

WIDTH = 4096
HALFW = WIDTH // 2
CHIPS = 64
DOCS = 256
CAP = 24
SIDE = 12
HEAD = 8
PARTS = 4
ROWS = CHIPS * HEAD
TAIL = CHIPS * (SIDE - HEAD)
META = WIDTH + HALFW
SENT = META + 128
CHIP_AXES = ("z", "x", "y")
SHORT = WIDTH + 128
SLOTS = 10
ROOMS = (64, 64, 32, 32)
WAYS = len(ROOMS)
STARTS = (0, 64, 128, 160)
OVER = sum(ROOMS)
QUARTER = WIDTH // 4
NOTES = WIDTH + QUARTER
FIRST = NOTES + 128
REST = CHIPS * (SLOTS - HEAD)
OWN = ROWS + REST
ALL_AXES = CHIP_AXES + ("core",)
F32 = jnp.float32
BF16 = jnp.bfloat16
MIB = 1024 * 1024


def iota(shape, axis):
    return lax.broadcasted_iota(jnp.int32, shape, axis)


def dot(a, b):
    return jnp.dot(a, b, preferred_element_type=F32)


def dot_t(a, b):
    return lax.dot_general(a, b, (((1,), (1,)), ((), ())), preferred_element_type=F32)


def onehot(mask):
    return jnp.where(mask, 1.0, 0.0).astype(BF16)


def split3(x):
    a = x.astype(BF16)
    rest = x - a.astype(F32)
    b = rest.astype(BF16)
    c = (rest - b.astype(F32)).astype(BF16)
    return a, b, c


def send_kernel(embed_hbm, group_hbm, half_hbm, out_ref, rank_ref, embed_ref, group_ref, half_ref, unit_ref, slot_ref, meta_ref, sems):
    step = pl.program_id(0)

    @pl.when(step == 0)
    def _():
        names = [pltpu.make_async_copy(group_hbm, group_ref, sems.at[0]), pltpu.make_async_copy(half_hbm, half_ref, sems.at[1])]
        size = DOCS // PARTS
        spans = [pl.ds(size * part, size) for part in range(PARTS)]
        parts = [pltpu.make_async_copy(embed_hbm.at[span, :], embed_ref.at[span, :], sems.at[2 + i]) for i, span in enumerate(spans)]
        for copy in names + parts:
            copy.start()
        for copy in names:
            copy.wait()
        cluster = 2 * group_ref[...] + half_ref[...]
        other = cluster + 1 - 2 * half_ref[...]
        member = iota((CHIPS, DOCS), 0) == cluster
        earlier = onehot(iota((DOCS, DOCS), 0) < iota((DOCS, DOCS), 1))
        before = dot(onehot(member), earlier)
        rank = jnp.sum(jnp.where(member, before, 0.0), axis=0, keepdims=True).astype(jnp.int32)
        over = rank >= SIDE
        chip = jnp.where(over, other, cluster)
        row = jnp.where(over, CAP - 1 - rank, rank)
        slot_ref[0:1, :] = jnp.where(row < HEAD, chip * HEAD + row, -1)
        slot_ref[1:2, :] = jnp.where(row >= HEAD, chip * HEAD + row - HEAD, -1)
        slot_ref[2:3, :] = jnp.where(row >= HEAD, chip * HEAD + row - HEAD + 4, -1)
        rank_ref[0:1, :] = rank
        rank_ref[1:2, :] = cluster
        own = jnp.sum(jnp.where(member, 1.0, 0.0), axis=1, keepdims=True)
        oth = jnp.sum(jnp.where(iota((CHIPS, DOCS), 0) == other, 1.0, 0.0), axis=1, keepdims=True)
        lane = iota((CHIPS, 128), 1)
        meta = jnp.where(lane == 0, own, jnp.where(lane == 1, oth, 0.0))
        meta_ref[...] = jnp.broadcast_to(meta[:, None, :], (CHIPS, HEAD, 128)).reshape(ROWS, 128)
        for copy, span in zip(parts, spans):
            copy.wait()
            floats = embed_ref[span, :].astype(F32)
            scale = lax.rsqrt(jnp.sum(floats * floats, axis=1, keepdims=True) + 1e-06)
            unit_ref[span, :] = (floats * scale).astype(BF16)

    rows = out_ref.shape[0]
    base = step * rows
    here = iota((rows, DOCS), 0) + base
    head = onehot(here == slot_ref[0:1, :])
    left = onehot(here == slot_ref[1:2, :])
    right = onehot(here == slot_ref[2:3, :])
    out_ref[:, :WIDTH] = dot(head, unit_ref[...]).astype(BF16)
    out_ref[:, WIDTH:META] = (dot(left, unit_ref[:, :HALFW]) + dot(right, unit_ref[:, HALFW:])).astype(BF16)
    out_ref[:, META:] = meta_ref[pl.ds(pl.multiple_of(base, rows), rows), :].astype(BF16)


def place_documents(embed, group, half):
    steps = 4
    far = pl.BlockSpec(memory_space=pltpu.HBM)
    operands = [pltpu.with_memory_space_constraint(x, pltpu.HBM) for x in (embed, group, half)]
    return pl.pallas_call(
        send_kernel,
        grid=(steps,),
        in_specs=[far, far, far],
        out_specs=[pl.BlockSpec((ROWS // steps, SENT), lambda i: (i, 0)), pl.BlockSpec((8, DOCS), lambda i: (0, 0))],
        out_shape=[jax.ShapeDtypeStruct((ROWS, SENT), BF16), jax.ShapeDtypeStruct((8, DOCS), jnp.int32)],
        scratch_shapes=[
            pltpu.VMEM((DOCS, WIDTH), BF16),
            pltpu.VMEM((1, DOCS), jnp.int32),
            pltpu.VMEM((1, DOCS), jnp.int32),
            pltpu.VMEM((DOCS, WIDTH), BF16),
            pltpu.VMEM((8, DOCS), jnp.int32),
            pltpu.VMEM((ROWS, 128), F32),
            pltpu.SemaphoreType.DMA((2 + PARTS,)),
        ],
        compiler_params=pltpu.CompilerParams(vmem_limit_bytes=28 * MIB),
        cost_estimate=pl.CostEstimate(flops=2 * 10**9, bytes_accessed=9 * 2**20, transcendentals=256),
        name="place_documents",
    )(*operands)


def tail_rows(y_ref):
    to = iota((TAIL, ROWS), 0)
    at = iota((TAIL, ROWS), 1)
    want = (to % CHIPS) * HEAD + to // CHIPS
    left = dot(onehot(at == want), y_ref[:, WIDTH:META]).astype(BF16)
    right = dot(onehot(at == want + 4), y_ref[:, WIDTH:META]).astype(BF16)
    return left, right


def lane_counts(y_ref):
    meta = y_ref[:, META:].astype(F32).T[:8, :]
    pick = onehot(iota((ROWS, TAIL), 0) == (iota((ROWS, TAIL), 1) % CHIPS) * HEAD)
    tail = dot(meta.astype(BF16), pick)
    return meta[0:1, :], meta[1:2, :], tail[0:1, :], tail[1:2, :]


def pack_kernel(y_ref, v_ref):
    room = v_ref.shape[0]
    counts = y_ref[:, META:].astype(F32).T[:8, :]
    first = CAP - counts[1:2, :]
    row = (iota((1, ROWS), 1) % HEAD).astype(F32)
    low = row < 4
    over = [row >= first, low & (row + HEAD >= first), ~low & (row + HEAD - 4 >= first)]
    flags = [jnp.where(mask, 1.0, 0.0) for mask in over]
    before = onehot(iota((ROWS, ROWS), 0) < iota((ROWS, ROWS), 1))
    place = dot(jnp.concatenate(flags + [jnp.zeros((5, ROWS), F32)], axis=0).astype(BF16), before)
    count = jnp.sum(flags[0], axis=1, keepdims=True)
    full = jnp.where(count + jnp.sum(flags[1], axis=1, keepdims=True) > room, 1.0, 0.0)
    places = [place[0:1, :], place[1:2, :] + count, place[2:3, :] + count]
    take = [onehot((iota((room, ROWS), 0) == at.astype(jnp.int32)) & mask) for at, mask in zip(places, over)]
    tail = y_ref[:, WIDTH:META]
    v_ref[:, :HALFW] = (dot(take[0], y_ref[:, :HALFW]) + dot(take[1], tail)).astype(BF16)
    v_ref[:, HALFW:WIDTH] = (dot(take[0], y_ref[:, HALFW:WIDTH]) + dot(take[2], tail)).astype(BF16)
    lane = iota((ROWS, 128), 1)
    at = iota((ROWS, 128), 0)

    def about(row):
        return jnp.where(lane == 0, at // HEAD, jnp.where(lane == 1, CAP - 1 - row, jnp.where(lane == 2, 1, 0))).astype(F32).astype(BF16)

    info = dot(take[0], about(at % HEAD)) + dot(take[1], about(at % HEAD + HEAD))
    v_ref[:, WIDTH:] = jnp.where(iota((room, 128), 1) == 3, full, info).astype(BF16)


def slots(tops):
    lane = iota((256, 128), 1)
    at = iota((256, 128), 0)
    head = [jnp.max(jnp.where(lane == at % HEAD, top, -2.0).reshape(32, HEAD, 128), axis=1) for top in tops[:2]]
    tail = jnp.max(jnp.where(lane == at // CHIPS + HEAD, tops[2], -2.0).reshape(4, CHIPS, 128), axis=0)
    return jnp.maximum(jnp.concatenate(head, axis=0), tail)


def own_valid(y_ref):
    own1, _, own2, _ = lane_counts(y_ref)
    ok1 = (iota((1, ROWS), 1) % HEAD).astype(F32) < own1
    ok2 = (iota((1, TAIL), 1) // CHIPS + HEAD).astype(F32) < own2
    return [ok1[:, :256], ok1[:, 256:], ok2]


def row_block(y_ref, x2_ref, block):
    return y_ref[256 * block : 256 * (block + 1), :WIDTH] if block < 2 else x2_ref[...]


def row_max(mine, other, keep):
    return jnp.max(jnp.where(keep, dot_t(mine, other), -2.0), axis=1, keepdims=True)


def off_diagonal(n):
    return iota((n, n), 0) != iota((n, n), 1)


def call(kernel, name, out_shape, flops, *args, mib=28, scratch=()):
    return pl.pallas_call(
        kernel,
        out_shape=out_shape,
        scratch_shapes=list(scratch),
        compiler_params=pltpu.CompilerParams(vmem_limit_bytes=mib * MIB),
        cost_estimate=pl.CostEstimate(flops=int(flops), bytes_accessed=2**20, transcendentals=0),
        name=name,
    )(*args)


def own_kernel(y_ref, best_ref, x2_ref):
    left, right = tail_rows(y_ref)
    x2_ref[:, :HALFW] = left
    x2_ref[:, HALFW:] = right
    ok = own_valid(y_ref)
    tops = []
    for a in range(3):
        mine = row_block(y_ref, x2_ref, a)
        top = jnp.full((256, 1), -2.0, F32)
        for b in range(3):
            keep = ok[b] & off_diagonal(256) if a == b else ok[b]
            top = jnp.maximum(top, row_max(mine, row_block(y_ref, x2_ref, b), keep))
        tops.append(top)
    best_ref[...] = slots(tops)


def cross_kernel(y_ref, x2_ref, s_ref, so_far_ref, best_ref, s2_ref):
    left, right = tail_rows(s_ref)
    s2_ref[:, :HALFW] = left
    s2_ref[:, HALFW:] = right
    ok = own_valid(s_ref)
    tops = []
    for a in range(3):
        mine = row_block(y_ref, x2_ref, a)
        top = jnp.full((256, 1), -2.0, F32)
        for b in range(3):
            top = jnp.maximum(top, row_max(mine, row_block(s_ref, s2_ref, b), ok[b]))
        tops.append(top)
    best_ref[...] = jnp.maximum(so_far_ref[...], slots(tops))


def valid_rows(y_ref):
    counts = y_ref[:, META:].astype(F32)
    head = (iota((ROWS, 1), 0) % HEAD).astype(F32) < counts[:, 0:1]
    source = jnp.max(counts.reshape(CHIPS, HEAD, 128), axis=1)
    tail = (iota((TAIL, 1), 0) // CHIPS + HEAD).astype(F32) < jnp.concatenate([source] * 4, axis=0)[:, 0:1]
    return [head[:256], head[256:], tail]


def tiles(room):
    size = min(room, 256)
    return [slice(start, start + size) for start in range(0, room, size)]


def column_max(scores, keep):
    return jnp.max(jnp.where(keep, scores, -2.0), axis=0, keepdims=True)


def received_kernel(s_ref, s2_ref, v_ref, so_far_ref, top_ref):
    room = v_ref.shape[0]

    def step(i, carry):
        start = pl.multiple_of(i * 256, 256)
        mine = v_ref[pl.ds(start, 256), :WIDTH]
        ok_s = valid_rows(s_ref)
        used = v_ref[:, WIDTH:].astype(F32)[:, 2:3] > 0.5
        top = jnp.full((1, 256), -2.0, F32)
        for b in range(3):
            top = jnp.maximum(top, column_max(dot_t(row_block(s_ref, s2_ref, b), mine), ok_s[b]))
        for at in tiles(room):
            keep = used[at] & (iota((256, 256), 0) + at.start != iota((256, 256), 1) + start)
            top = jnp.maximum(top, column_max(dot_t(v_ref[at, :WIDTH], mine), keep))
        top_ref[:, pl.ds(start, 256)] = jnp.broadcast_to(top, (8, 256))
        return carry

    lax.fori_loop(0, room // 256, step, 0)


def sibling_kernel(y_ref, x2_ref, v_ref, w_ref, so_far_ref, so_far_top_ref, out_ref, top_ref, best_ref, lane_ref):
    room = v_ref.shape[0]
    about_v = v_ref[:, WIDTH:].astype(F32)
    about_w = w_ref[:, WIDTH:].astype(F32)
    lanes = jnp.concatenate([about_v, about_w], axis=0).T[:8, :]
    lane_ref[...] = lanes
    used = lanes[2:3, :] > 0.5
    top_ref[...] = so_far_top_ref[...]
    best_ref[...] = jnp.full(best_ref.shape, -2.0, F32)

    def step(i, carry):
        start = pl.multiple_of(i * 256, 256)
        ok_y = valid_rows(y_ref)
        for ref, first in ((v_ref, 0), (w_ref, room)):
            rows = ref[pl.ds(start, 256), :WIDTH]
            ok = lane_ref[2:3, pl.ds(start + first, 256)] > 0.5
            top = top_ref[:, pl.ds(start, 256)]
            for a in range(3):
                scores = dot_t(row_block(y_ref, x2_ref, a), rows)
                best = jnp.max(jnp.where(ok, scores, -2.0), axis=1, keepdims=True)
                span = slice(256 * a, 256 * (a + 1))
                best_ref[span, :] = jnp.maximum(best_ref[span, :], best)
                top = jnp.maximum(top, column_max(scores, ok_y[a]))
            if first == 0:
                for at in tiles(room):
                    theirs = w_ref[at, WIDTH:].astype(F32)[:, 2:3] > 0.5
                    top = jnp.maximum(top, column_max(dot_t(w_ref[at, :WIDTH], rows), theirs))
                top_ref[:, pl.ds(start, 256)] = top
        return carry

    lax.fori_loop(0, room // 256, step, 0)
    best = jnp.maximum(so_far_ref[...], slots([best_ref[256 * a : 256 * (a + 1), 0:1] for a in range(3)]))
    source = lanes[0:1, :room].astype(jnp.int32)
    here = (iota((CHIPS, room), 0) == source) & used[:, :room]
    rank = onehot((iota((room, 128), 1) == about_v[:, 1:2].astype(jnp.int32)) & (about_v[:, 2:3] > 0.5))
    placed = jnp.zeros((CHIPS, 128), F32)
    for piece in split3(jnp.where(here, top_ref[0:1, :], 0.0)):
        placed = placed + dot(piece, rank)
    filled = dot(onehot(here), rank)
    full = jnp.maximum(about_v[0:1, 3:4], about_w[0:1, 3:4])
    out = jnp.where(filled > 0.5, placed, best)
    out_ref[...] = jnp.where(iota((CHIPS, 128), 1) == 127, full, out)


def after_kernel(v_ref, best_ref, out_ref):
    pass


def after(v, best):
    anywhere = pl.BlockSpec(memory_space=pl.ANY)
    return pl.pallas_call(
        after_kernel,
        in_specs=[anywhere, anywhere],
        out_specs=anywhere,
        out_shape=jax.ShapeDtypeStruct(v.shape, v.dtype),
        input_output_aliases={0: 0},
        compiler_params=pltpu.CompilerParams(vmem_limit_bytes=MIB),
        name="overflow_after_own",
    )(v, best)


def owner_side(y, room):
    swap = [(0, 1), (1, 0)]
    mib = 28 if room <= 256 else 52
    slot_shape = jax.ShapeDtypeStruct((CHIPS, 128), F32)
    top_shape = jax.ShapeDtypeStruct((8, room), F32)
    tail_shape = jax.ShapeDtypeStruct((TAIL, WIDTH), BF16)
    packed_shape = jax.ShapeDtypeStruct((room, WIDTH + 128), BF16)
    s = lax.ppermute(y, "core", swap)
    v = call(pack_kernel, "pack_overflow", packed_shape, 3e9, y, mib=mib)
    v = lax.ppermute(v, "y", [(0, 1), (1, 0), (2, 3), (3, 2)])
    best, x2 = call(own_kernel, "own_pairs", [slot_shape, tail_shape], 5e9, y)
    best, s2 = call(cross_kernel, "cross_pairs", [slot_shape, tail_shape], 6e9, y, x2, s, best)
    v = after(v, best)
    w = lax.ppermute(v, "core", swap)
    top = call(received_kernel, "received_pairs", top_shape, 3e9, s, s2, v, best, mib=mib)
    scratch = [pltpu.VMEM((8, room), F32), pltpu.VMEM((ROWS + TAIL, 128), F32), pltpu.VMEM((8, 2 * room), F32)]
    return call(sibling_kernel, "sibling_pairs", slot_shape, 1e9, y, x2, v, w, best, top, mib=mib, scratch=scratch)


def pick_kernel(back_ref, rank_ref, out_ref, full_ref):
    rank = rank_ref[0:1, :]
    cluster = rank_ref[1:2, :]
    at_rank = onehot(iota((128, DOCS), 0) == rank)
    back = back_ref[...]
    found = jnp.zeros((CHIPS, DOCS), F32)
    for piece in split3(back):
        found = found + dot(piece, at_rank)
    out_ref[...] = jnp.sum(jnp.where(iota((CHIPS, DOCS), 0) == cluster, found, 0.0), axis=0, keepdims=True)
    full_ref[0, 0] = jnp.max(back[:, 127:128])


def return_to_source(best, rank):
    back = lax.all_to_all(best, CHIP_AXES, split_axis=0, concat_axis=0, tiled=True)
    return pl.pallas_call(
        pick_kernel,
        out_specs=[pl.BlockSpec(memory_space=pltpu.VMEM), pl.BlockSpec(memory_space=pltpu.SMEM)],
        out_shape=[jax.ShapeDtypeStruct((1, DOCS), F32), jax.ShapeDtypeStruct((1, 1), F32)],
        compiler_params=pltpu.CompilerParams(vmem_limit_bytes=4 * MIB),
        name="pick_documents",
    )(back, rank)


def next_chip(x, way, core):
    bits = 4 * core if way < 2 else 2
    unit = 1 << bits
    place = (iota(x.shape, 1) >> bits) & 3
    if way % 2 == 0:
        return jnp.where(place == 3, pltpu.roll(x, 3 * unit, axis=1), pltpu.roll(x, 128 - unit, axis=1))
    return jnp.where(place == 0, pltpu.roll(x, 128 - 3 * unit, axis=1), pltpu.roll(x, unit, axis=1))


def neighbour(z, x, y, way, core):
    step = 1 if way % 2 == 0 else 3
    if way < 2:
        y, z = jnp.where(core == 0, (y + step) & 3, y), jnp.where(core == 0, z, (z + step) & 3)
    else:
        x = (x + step) & 3
    return 16 * z + 4 * x + y


def spread_kernel(embed_hbm, group_hbm, half_hbm, out_ref, rank_ref, embed_ref, group_ref, half_ref, unit_ref, note_ref, slot_ref, sems):
    names = [pltpu.make_async_copy(group_hbm, group_ref, sems.at[0]), pltpu.make_async_copy(half_hbm, half_ref, sems.at[1])]
    size = DOCS // PARTS
    spans = [pl.ds(size * part, size) for part in range(PARTS)]
    parts = [pltpu.make_async_copy(embed_hbm.at[span, :], embed_ref.at[span, :], sems.at[2 + i]) for i, span in enumerate(spans)]
    for copy in names + parts:
        copy.start()
    for copy in names:
        copy.wait()
    group, half = group_ref[...], half_ref[...]
    z, x, y = ((group >> 4) + 2 * half) & 3, ((group >> 2) + 2 * half) & 3, (group + 2 * half) & 3
    home = 16 * z + 4 * x + y
    member = onehot((iota((2 * CHIPS, DOCS), 0) & (CHIPS - 1)) == home)
    earlier = onehot(iota((DOCS, DOCS), 0) < iota((DOCS, DOCS), 1))
    before = dot(member[:CHIPS], earlier)
    rank = jnp.sum(before * member[:CHIPS].astype(F32), axis=0, keepdims=True)
    counts = dot_t(jnp.ones((8, DOCS), BF16), member)
    left = jnp.maximum(counts - SLOTS, 0.0)
    free = SLOTS - jnp.minimum(counts, float(SLOTS))
    given = [jnp.zeros((8, 2 * CHIPS), F32) for _ in range(WAYS)]
    core = lax.axis_index("core")
    turn = (21 * lax.axis_index("z") + 5 * lax.axis_index("x") + lax.axis_index("y")) % 6
    early = jnp.where(turn < 3, 1.0, 0.0)
    plan = [(0, early), (1, 1.0), (0, 1.0 - early), (2, early), (3, 1.0), (2, 1.0 - early), (0, 1.0), (1, 1.0)]
    plan += [(d, 24.0) for d in range(WAYS)]
    for part, (copy, span) in enumerate(zip(parts, spans)):
        copy.wait()
        floats = embed_ref[span, :].astype(F32)
        scale = lax.rsqrt(jnp.sum(floats * floats, axis=1, keepdims=True) + 1e-06)
        unit_ref[span, :] = (floats * scale).astype(BF16)
        for d, most in plan[3 * part : 3 * part + 3]:
            take = jnp.minimum(jnp.minimum(left, next_chip(free, d, core)), most)
            given[d] = given[d] + take
            left = left - take
            free = free - next_chip(take, d ^ 1, core)
    ends, offsets = [], []
    total, used = jnp.zeros_like(left), jnp.zeros_like(left)
    for d in range(WAYS):
        total = total + given[d]
        ends.append(total)
        offsets.append(next_chip(used, d, core))
        used = used + next_chip(given[d], d ^ 1, core)
    table = jnp.concatenate([row[0:1] for row in ends + offsets] + [jnp.zeros((8, 2 * CHIPS), F32)], axis=0)
    table = jnp.where(iota(table.shape, 1) < CHIPS, table, 0.0)
    found = dot(table.astype(BF16), member)
    beyond = rank - SLOTS
    own = beyond < 0.0
    chip = home
    row = jnp.where(own, rank.astype(jnp.int32), -1)
    came = jnp.zeros((1, DOCS), F32)
    for d in range(WAYS):
        start = found[d - 1 : d] if d else jnp.zeros((1, DOCS), F32)
        this = (beyond >= start) & (beyond < found[d : d + 1])
        offset = found[WAYS + d : WAYS + d + 1]
        row = jnp.where(this, SLOTS - 1 - (offset + beyond - start).astype(jnp.int32), row)
        chip = jnp.where(this, neighbour(z, x, y, d, core), chip)
        came = jnp.where(this, d + 1.0, came)
    slot_ref[0:1, :] = jnp.where((row >= 0) & (row < HEAD), chip * HEAD + row, -1)
    slot_ref[1:2, :] = jnp.where(row >= HEAD, chip * HEAD + 4 * (row - HEAD), -8)
    rank_ref[0:1, :] = rank.astype(jnp.int32)
    rank_ref[1:2, :] = home
    lost = jnp.max(jnp.where(row < 0, 1.0, 0.0), axis=1, keepdims=True)
    line = iota((128, DOCS), 0)
    for part in range(2):
        at = line - 8 * part
        notes = jnp.where(at == 0, jnp.where(own, 1.0, 0.0), jnp.where(at == 1, came, jnp.where(at == 2, rank, 0.0)))
        note_ref[part] = jnp.where(at == 3, lost, notes).T.astype(BF16)

    at = iota((ROWS, DOCS), 0)
    whole = onehot(at == slot_ref[0:1, :])
    quarters = jnp.zeros((ROWS, QUARTER), F32)
    notes = dot(whole, note_ref[0])
    for q in range(4):
        span = slice(QUARTER * q, QUARTER * (q + 1))
        out_ref[:, span] = dot(whole, unit_ref[:, span]).astype(BF16)
        this = onehot(at == slot_ref[1:2, :] + q)
        quarters = quarters + dot(this, unit_ref[:, span])
        notes = notes + dot(this, note_ref[1])
    out_ref[:, WIDTH:NOTES] = quarters.astype(BF16)
    out_ref[:, NOTES:] = notes.astype(BF16)


def spread_documents(embed, group, half):
    far = pl.BlockSpec(memory_space=pltpu.HBM)
    operands = [pltpu.with_memory_space_constraint(x, pltpu.HBM) for x in (embed, group, half)]
    return pl.pallas_call(
        spread_kernel,
        in_specs=[far, far, far],
        out_shape=[jax.ShapeDtypeStruct((ROWS, FIRST), BF16), jax.ShapeDtypeStruct((8, DOCS), jnp.int32)],
        scratch_shapes=[
            pltpu.VMEM((DOCS, WIDTH), BF16),
            pltpu.VMEM((1, DOCS), jnp.int32),
            pltpu.VMEM((1, DOCS), jnp.int32),
            pltpu.VMEM((DOCS, WIDTH), BF16),
            pltpu.VMEM((2, DOCS, 128), BF16),
            pltpu.VMEM((8, DOCS), jnp.int32),
            pltpu.SemaphoreType.DMA((2 + PARTS,)),
        ],
        compiler_params=pltpu.CompilerParams(vmem_limit_bytes=28 * MIB),
        cost_estimate=pl.CostEstimate(flops=2 * 10**9, bytes_accessed=9 * 2**20, transcendentals=256),
        name="spread_documents",
    )(*operands)


def quarter_rows(y_ref, out_ref, first):
    to, at = iota((4 * REST, ROWS), 0), iota((4 * REST, ROWS), 1)
    row = to % REST
    want = (row % CHIPS) * HEAD + 4 * (row // CHIPS) + to // REST
    rows = dot(onehot(at == want), y_ref[:, WIDTH:NOTES]).astype(BF16)
    for q in range(4):
        out_ref[first : first + REST, QUARTER * q : QUARTER * (q + 1)] = rows[REST * q : REST * (q + 1)]


def at_home(y_ref):
    notes = y_ref[:, NOTES:].astype(F32).T[:16, :]
    at, to = iota((ROWS, REST), 0), iota((ROWS, REST), 1)
    pick = onehot(at == (to % CHIPS) * HEAD + 4 * (to // CHIPS))
    return notes[0:1, :] > 0.5, dot(notes[8:16, :].astype(BF16), pick)[0:1, :] > 0.5


def sort_kernel(y_ref, *v_refs):
    notes = y_ref[:, NOTES:].astype(F32).T[:16, :]
    quarter = iota((1, ROWS), 1) % 4
    ways = [notes[1:2, :] == d + 1.0 for d in range(WAYS)]
    ways += [(notes[9:10, :] == d + 1.0) & (quarter == q) for q in range(4) for d in range(WAYS)]
    flags = jnp.concatenate([jnp.where(way, 1.0, 0.0) for way in ways] + [jnp.zeros((4, ROWS), F32)], axis=0)
    before = onehot(iota((ROWS, ROWS), 0) < iota((ROWS, ROWS), 1))
    place = dot(flags.astype(BF16), before)
    sums = jnp.sum(flags, axis=1, keepdims=True)
    loads = [sums[d : d + 1] + sums[WAYS + d : WAYS + d + 1] - ROOMS[d] for d in range(WAYS)]
    most = functools.reduce(jnp.maximum, loads)
    lost = jnp.max(jnp.maximum(notes[3:4, :], notes[11:12, :]), axis=1, keepdims=True)
    full = jnp.where((most > 0.5) | (lost > 0.5), 1.0, 0.0)

    def take(first, shift):
        rows = []
        for d in range(WAYS):
            slot = iota((ROOMS[d], ROWS), 0)
            to = place[first + d : first + d + 1, :] + (sums[d : d + 1, :] if shift else 0.0)
            rows.append(jnp.where((slot == to.astype(jnp.int32)) & ways[first + d], 1.0, 0.0))
        return jnp.concatenate(rows, axis=0).astype(BF16)

    whole = take(0, False)
    lane = iota((ROWS, 128), 1)
    source = (iota((ROWS, 128), 0) // HEAD).astype(F32)
    extra = jnp.where(lane == 4, source, jnp.where(lane == 5, 1.0, 0.0))
    given = y_ref[:, NOTES:].astype(F32)
    info = dot(whole, jnp.where(lane == 2, given, extra).astype(BF16))
    some = jnp.concatenate([take(WAYS * (1 + q), True) for q in range(4)], axis=0)
    quarters = dot(some, y_ref[:, WIDTH:NOTES])
    for q in range(4):
        span = slice(QUARTER * q, QUARTER * (q + 1))
        rows = (dot(whole, y_ref[:, span]) + quarters[OVER * q : OVER * (q + 1)]).astype(BF16)
        for d in range(WAYS):
            v_refs[d][:, span] = rows[STARTS[d] : STARTS[d] + ROOMS[d]]
        if q == 0:
            moved = jnp.where(lane == 2, pltpu.roll(given, 128 - 8, axis=1), extra)
            info = info + dot(some[:OVER], moved.astype(BF16))
    info = jnp.where(iota((OVER, 128), 1) == 3, full, info).astype(BF16)
    for d in range(WAYS):
        v_refs[d][:, WIDTH:] = info[STARTS[d] : STARTS[d] + ROOMS[d]]


def to_slots(top, rest):
    keep = iota((ROWS, 128), 1) == iota((ROWS, 128), 0) % HEAD
    head = jnp.max(jnp.where(keep, top, -2.0).reshape(CHIPS, HEAD, 128), axis=1)
    keep = iota((REST, 128), 1) == iota((REST, 128), 0) // CHIPS + HEAD
    return jnp.maximum(head, jnp.max(jnp.where(keep, rest, -2.0).reshape(2, CHIPS, 128), axis=0))


def upright(line):
    return jnp.broadcast_to(line, (8, line.shape[1])).T[:, 0:1]


def lane_max(scores, keep):
    return jnp.max(jnp.where(keep, scores, -2.0), axis=1, keepdims=True)


def home_kernel(y_ref, best_ref):
    ok = y_ref[:, NOTES:].astype(F32).T[0:1, :] > 0.5
    here = y_ref[:, NOTES:].astype(F32)[:, 0:1] > 0.5
    low, high = y_ref[:256, :WIDTH], y_ref[256:, :WIDTH]
    both = dot_t(low, high)
    top0 = jnp.maximum(row_max(low, low, ok[:, :256] & off_diagonal(256)), lane_max(both, ok[:, 256:]))
    top1 = row_max(high, high, ok[:, 256:] & off_diagonal(256))
    top1 = jnp.maximum(top1, upright(column_max(both, here[:256])))
    best_ref[...] = jnp.broadcast_to(jnp.concatenate([top0, top1], axis=0), (ROWS, 128))


def other_core_kernel(y_ref, s_ref, so_far_ref, best_ref, rest_ref):
    quarter_rows(y_ref, rest_ref, 0)
    quarter_rows(s_ref, rest_ref, REST)
    (ok, ok2), (ok_s, ok_s2) = at_home(y_ref), at_home(s_ref)
    theirs = s_ref[:, :WIDTH]
    tops = [row_max(y_ref[256 * a : 256 * (a + 1), :WIDTH], theirs, ok_s) for a in range(2)]
    ok_rest = jnp.concatenate([jnp.where(ok2, 1.0, 0.0), jnp.where(ok_s2, 1.0, 0.0)], axis=1)
    scores = dot_t(rest_ref[...], y_ref[:, :WIDTH])
    beside = column_max(scores, upright(ok_rest) > 0.5)
    top = jnp.maximum(jnp.maximum(jnp.concatenate(tops, axis=0), upright(beside)), so_far_ref[:, 0:1])
    mine = rest_ref[:REST]
    keep = (ok_rest > 0.5) & (iota((REST, 2 * REST), 0) != iota((REST, 2 * REST), 1))
    rest = jnp.maximum(lane_max(scores[:REST], ok), row_max(mine, rest_ref[...], keep))
    best_ref[...] = to_slots(top, jnp.maximum(rest, row_max(mine, theirs, ok_s)))


def join_kernel(*refs):
    out_ref = refs[-1]
    for d in range(WAYS):
        out_ref[STARTS[d] : STARTS[d] + ROOMS[d], :] = refs[d][...]


def notes_of(v_ref):
    return v_ref[:, WIDTH:].astype(F32).T[:8, :]


def guests_kernel(y_ref, s_ref, rest_ref, v_ref, so_far_ref, top_ref, own_ref):
    mine = v_ref[:, :WIDTH]
    used = v_ref[:, WIDTH:].astype(F32)[:, 5:6] > 0.5
    ok_v = notes_of(v_ref)[5:6, :] > 0.5
    top = row_max(mine, mine, ok_v & off_diagonal(OVER))
    (ok, ok2), (ok_s, ok_s2) = at_home(y_ref), at_home(s_ref)
    scores = dot_t(mine, y_ref[:, :WIDTH])
    own_ref[:, :ROWS] = jnp.broadcast_to(column_max(scores, used), (8, ROWS))
    top = jnp.maximum(top, lane_max(scores, ok))
    top = jnp.maximum(top, row_max(mine, s_ref[:, :WIDTH], ok_s))
    scores = dot_t(mine, rest_ref[...])
    own_ref[:, ROWS:] = jnp.broadcast_to(column_max(scores[:, :REST], used), (8, REST))
    top = jnp.maximum(top, jnp.maximum(lane_max(scores[:, :REST], ok2), lane_max(scores[:, REST:], ok_s2)))
    top_ref[...] = jnp.broadcast_to(top, (OVER, 128))


def finish_kernel(y_ref, rest_ref, v_ref, w_ref, so_far_ref, top_ref, own_ref, out_ref):
    about = v_ref[:, WIDTH:].astype(F32)
    about_w = w_ref[:, WIDTH:].astype(F32)
    lanes = notes_of(v_ref)
    theirs = w_ref[:, :WIDTH]
    used = about_w[:, 5:6] > 0.5
    head = jnp.maximum(own_ref[:, :ROWS], column_max(dot_t(theirs, y_ref[:, :WIDTH]), used))
    rest = jnp.maximum(own_ref[:, ROWS:], column_max(dot_t(theirs, rest_ref[:REST]), used))
    best = jnp.maximum(so_far_ref[...], to_slots(head.T[:, 0:1], rest.T[:, 0:1]))
    top = row_max(v_ref[:, :WIDTH], theirs, notes_of(w_ref)[5:6, :] > 0.5)
    top = jnp.maximum(top_ref[...], top)
    here = onehot((iota((CHIPS, OVER), 0) == lanes[4:5, :].astype(jnp.int32)) & (lanes[5:6, :] > 0.5))
    rank = (iota((OVER, 128), 1) == about[:, 2:3].astype(jnp.int32)) & (about[:, 5:6] > 0.5)
    pieces = dot(here, jnp.concatenate([*split3(jnp.where(rank, top, 0.0)), onehot(rank)], axis=1))
    placed = pieces[:, :128] + pieces[:, 128:256] + pieces[:, 256:384]
    filled = pieces[:, 384:]
    full = jnp.maximum(about[0:1, 3:4], about_w[0:1, 3:4])
    out = jnp.where(filled > 0.5, placed, best)
    out_ref[...] = jnp.where(iota((CHIPS, 128), 1) == 127, full, out)


def way_home(way):
    pairs = []
    for z, x, y, core in itertools.product(range(4), range(4), range(4), range(2)):
        to = [z, x, y]
        axis = 1 if way >= 2 else 2 if core == 0 else 0
        to[axis] = (to[axis] + (3 if way % 2 == 0 else 1)) % 4
        pairs.append((32 * z + 8 * x + 2 * y + core, 32 * to[0] + 8 * to[1] + 2 * to[2] + core))
    return pairs


def owner_short(y):
    swap = [(0, 1), (1, 0)]
    slot_shape = jax.ShapeDtypeStruct((CHIPS, 128), F32)
    rest_shape = jax.ShapeDtypeStruct((2 * REST, WIDTH), BF16)
    way_shapes = [jax.ShapeDtypeStruct((room, SHORT), BF16) for room in ROOMS]
    s = lax.ppermute(y, "core", swap)
    ways = call(sort_kernel, "sort_overflow", way_shapes, 3e9, y, mib=20)
    came = []
    for d, v in enumerate(ways):
        came.append(lax.ppermute(v, ALL_AXES, way_home(d)))
    best = call(home_kernel, "home_pairs", jax.ShapeDtypeStruct((ROWS, 128), F32), 1e10, y, mib=24)
    best, rest = call(other_core_kernel, "other_core_pairs", [slot_shape, rest_shape], 4e10, y, s, best, mib=24)
    v = call(join_kernel, "join_overflow", jax.ShapeDtypeStruct((OVER, SHORT), BF16), 1e8, *came, best, mib=8)
    w = lax.ppermute(v, "core", swap)
    shapes = [jax.ShapeDtypeStruct((OVER, 128), F32), jax.ShapeDtypeStruct((8, OWN), F32)]
    top, own = call(guests_kernel, "guest_pairs", shapes, 6e9, y, s, rest, v, best, mib=24)
    return call(finish_kernel, "finish_pairs", slot_shape, 3e9, y, rest, v, w, best, top, own, mib=24)


def wide_form(embed, group, half):
    sent, rank = place_documents(embed, group, half)
    y = lax.all_to_all(sent, CHIP_AXES, split_axis=0, concat_axis=0, tiled=True)
    return return_to_source(owner_side(y, ROWS + TAIL), rank)[0]


def on_device(embed, group, half):
    group, half = group.reshape(1, DOCS), half.reshape(1, DOCS)
    sent, rank = spread_documents(embed, group, half)
    y = lax.all_to_all(sent, CHIP_AXES, split_axis=0, concat_axis=0, tiled=True)
    nearest, full = return_to_source(owner_short(y), rank)
    nearest = lax.cond(
        full[0, 0] > 0.5,
        lambda embed, group, half, nearest: wide_form(embed, group, half),
        lambda embed, group, half, nearest: nearest,
        embed,
        group,
        half,
        nearest,
    )
    return nearest.reshape(DOCS)


def solution(mesh):
    devices = mesh.devices.reshape(4, 4, 4, 2)
    fine = Mesh(devices, ALL_AXES)
    return jax.shard_map(
        on_device,
        mesh=fine,
        in_specs=(P(ALL_AXES, None), P(ALL_AXES, None), P(ALL_AXES)),
        out_specs=P(ALL_AXES),
        check_vma=False,
    )
```

```python
import functools
import itertools

import jax
import jax.numpy as jnp
from jax import lax
from jax.experimental import pallas as pl
from jax.experimental.pallas import tpu as pltpu
from jax.sharding import Mesh, PartitionSpec as P

WIDTH = 4096
HALFW = WIDTH // 2
CHIPS = 64
DOCS = 256
CAP = 24
SIDE = 12
HEAD = 8
PARTS = 4
ROWS = CHIPS * HEAD
TAIL = CHIPS * (SIDE - HEAD)
META = WIDTH + HALFW
SENT = META + 128
CHIP_AXES = ("z", "x", "y")
SHORT = WIDTH + 128
SLOTS = 10
ROOMS = (64, 64, 32, 32)
WAYS = len(ROOMS)
STARTS = (0, 64, 128, 160)
OVER = sum(ROOMS)
QUARTER = WIDTH // 4
NOTES = WIDTH + QUARTER
FIRST = NOTES + 128
REST = CHIPS * (SLOTS - HEAD)
OWN = ROWS + REST
ALL_AXES = CHIP_AXES + ("core",)
F32 = jnp.float32
BF16 = jnp.bfloat16
MIB = 1024 * 1024


def iota(shape, axis):
    return lax.broadcasted_iota(jnp.int32, shape, axis)


def dot(a, b):
    return jnp.dot(a, b, preferred_element_type=F32)


def dot_t(a, b):
    return lax.dot_general(a, b, (((1,), (1,)), ((), ())), preferred_element_type=F32)


def onehot(mask):
    return jnp.where(mask, 1.0, 0.0).astype(BF16)


def split3(x):
    a = x.astype(BF16)
    rest = x - a.astype(F32)
    b = rest.astype(BF16)
    c = (rest - b.astype(F32)).astype(BF16)
    return a, b, c


def send_kernel(embed_hbm, group_hbm, half_hbm, out_ref, rank_ref, embed_ref, group_ref, half_ref, unit_ref, slot_ref, meta_ref, sems):
    step = pl.program_id(0)

    @pl.when(step == 0)
    def _():
        names = [pltpu.make_async_copy(group_hbm, group_ref, sems.at[0]), pltpu.make_async_copy(half_hbm, half_ref, sems.at[1])]
        size = DOCS // PARTS
        spans = [pl.ds(size * part, size) for part in range(PARTS)]
        parts = [pltpu.make_async_copy(embed_hbm.at[span, :], embed_ref.at[span, :], sems.at[2 + i]) for i, span in enumerate(spans)]
        for copy in names + parts:
            copy.start()
        for copy in names:
            copy.wait()
        cluster = 2 * group_ref[...] + half_ref[...]
        other = cluster + 1 - 2 * half_ref[...]
        member = iota((CHIPS, DOCS), 0) == cluster
        earlier = onehot(iota((DOCS, DOCS), 0) < iota((DOCS, DOCS), 1))
        before = dot(onehot(member), earlier)
        rank = jnp.sum(jnp.where(member, before, 0.0), axis=0, keepdims=True).astype(jnp.int32)
        over = rank >= SIDE
        chip = jnp.where(over, other, cluster)
        row = jnp.where(over, CAP - 1 - rank, rank)
        slot_ref[0:1, :] = jnp.where(row < HEAD, chip * HEAD + row, -1)
        slot_ref[1:2, :] = jnp.where(row >= HEAD, chip * HEAD + row - HEAD, -1)
        slot_ref[2:3, :] = jnp.where(row >= HEAD, chip * HEAD + row - HEAD + 4, -1)
        rank_ref[0:1, :] = rank
        rank_ref[1:2, :] = cluster
        own = jnp.sum(jnp.where(member, 1.0, 0.0), axis=1, keepdims=True)
        oth = jnp.sum(jnp.where(iota((CHIPS, DOCS), 0) == other, 1.0, 0.0), axis=1, keepdims=True)
        lane = iota((CHIPS, 128), 1)
        meta = jnp.where(lane == 0, own, jnp.where(lane == 1, oth, 0.0))
        meta_ref[...] = jnp.broadcast_to(meta[:, None, :], (CHIPS, HEAD, 128)).reshape(ROWS, 128)
        for copy, span in zip(parts, spans):
            copy.wait()
            floats = embed_ref[span, :].astype(F32)
            scale = lax.rsqrt(jnp.sum(floats * floats, axis=1, keepdims=True) + 1e-06)
            unit_ref[span, :] = (floats * scale).astype(BF16)

    rows = out_ref.shape[0]
    base = step * rows
    here = iota((rows, DOCS), 0) + base
    head = onehot(here == slot_ref[0:1, :])
    left = onehot(here == slot_ref[1:2, :])
    right = onehot(here == slot_ref[2:3, :])
    out_ref[:, :WIDTH] = dot(head, unit_ref[...]).astype(BF16)
    out_ref[:, WIDTH:META] = (dot(left, unit_ref[:, :HALFW]) + dot(right, unit_ref[:, HALFW:])).astype(BF16)
    out_ref[:, META:] = meta_ref[pl.ds(pl.multiple_of(base, rows), rows), :].astype(BF16)


def place_documents(embed, group, half):
    steps = 4
    far = pl.BlockSpec(memory_space=pltpu.HBM)
    operands = [pltpu.with_memory_space_constraint(x, pltpu.HBM) for x in (embed, group, half)]
    return pl.pallas_call(
        send_kernel,
        grid=(steps,),
        in_specs=[far, far, far],
        out_specs=[pl.BlockSpec((ROWS // steps, SENT), lambda i: (i, 0)), pl.BlockSpec((8, DOCS), lambda i: (0, 0))],
        out_shape=[jax.ShapeDtypeStruct((ROWS, SENT), BF16), jax.ShapeDtypeStruct((8, DOCS), jnp.int32)],
        scratch_shapes=[
            pltpu.VMEM((DOCS, WIDTH), BF16),
            pltpu.VMEM((1, DOCS), jnp.int32),
            pltpu.VMEM((1, DOCS), jnp.int32),
            pltpu.VMEM((DOCS, WIDTH), BF16),
            pltpu.VMEM((8, DOCS), jnp.int32),
            pltpu.VMEM((ROWS, 128), F32),
            pltpu.SemaphoreType.DMA((2 + PARTS,)),
        ],
        compiler_params=pltpu.CompilerParams(vmem_limit_bytes=28 * MIB),
        cost_estimate=pl.CostEstimate(flops=2 * 10**9, bytes_accessed=9 * 2**20, transcendentals=256),
        name="place_documents",
    )(*operands)


def tail_rows(y_ref):
    to = iota((TAIL, ROWS), 0)
    at = iota((TAIL, ROWS), 1)
    want = (to % CHIPS) * HEAD + to // CHIPS
    left = dot(onehot(at == want), y_ref[:, WIDTH:META]).astype(BF16)
    right = dot(onehot(at == want + 4), y_ref[:, WIDTH:META]).astype(BF16)
    return left, right


def lane_counts(y_ref):
    meta = y_ref[:, META:].astype(F32).T[:8, :]
    pick = onehot(iota((ROWS, TAIL), 0) == (iota((ROWS, TAIL), 1) % CHIPS) * HEAD)
    tail = dot(meta.astype(BF16), pick)
    return meta[0:1, :], meta[1:2, :], tail[0:1, :], tail[1:2, :]


def pack_kernel(y_ref, v_ref):
    room = v_ref.shape[0]
    counts = y_ref[:, META:].astype(F32).T[:8, :]
    first = CAP - counts[1:2, :]
    row = (iota((1, ROWS), 1) % HEAD).astype(F32)
    low = row < 4
    over = [row >= first, low & (row + HEAD >= first), ~low & (row + HEAD - 4 >= first)]
    flags = [jnp.where(mask, 1.0, 0.0) for mask in over]
    before = onehot(iota((ROWS, ROWS), 0) < iota((ROWS, ROWS), 1))
    place = dot(jnp.concatenate(flags + [jnp.zeros((5, ROWS), F32)], axis=0).astype(BF16), before)
    count = jnp.sum(flags[0], axis=1, keepdims=True)
    full = jnp.where(count + jnp.sum(flags[1], axis=1, keepdims=True) > room, 1.0, 0.0)
    places = [place[0:1, :], place[1:2, :] + count, place[2:3, :] + count]
    take = [onehot((iota((room, ROWS), 0) == at.astype(jnp.int32)) & mask) for at, mask in zip(places, over)]
    tail = y_ref[:, WIDTH:META]
    v_ref[:, :HALFW] = (dot(take[0], y_ref[:, :HALFW]) + dot(take[1], tail)).astype(BF16)
    v_ref[:, HALFW:WIDTH] = (dot(take[0], y_ref[:, HALFW:WIDTH]) + dot(take[2], tail)).astype(BF16)
    lane = iota((ROWS, 128), 1)
    at = iota((ROWS, 128), 0)

    def about(row):
        return jnp.where(lane == 0, at // HEAD, jnp.where(lane == 1, CAP - 1 - row, jnp.where(lane == 2, 1, 0))).astype(F32).astype(BF16)

    info = dot(take[0], about(at % HEAD)) + dot(take[1], about(at % HEAD + HEAD))
    v_ref[:, WIDTH:] = jnp.where(iota((room, 128), 1) == 3, full, info).astype(BF16)


def slots(tops):
    lane = iota((256, 128), 1)
    at = iota((256, 128), 0)
    head = [jnp.max(jnp.where(lane == at % HEAD, top, -2.0).reshape(32, HEAD, 128), axis=1) for top in tops[:2]]
    tail = jnp.max(jnp.where(lane == at // CHIPS + HEAD, tops[2], -2.0).reshape(4, CHIPS, 128), axis=0)
    return jnp.maximum(jnp.concatenate(head, axis=0), tail)


def own_valid(y_ref):
    own1, _, own2, _ = lane_counts(y_ref)
    ok1 = (iota((1, ROWS), 1) % HEAD).astype(F32) < own1
    ok2 = (iota((1, TAIL), 1) // CHIPS + HEAD).astype(F32) < own2
    return [ok1[:, :256], ok1[:, 256:], ok2]


def row_block(y_ref, x2_ref, block):
    return y_ref[256 * block : 256 * (block + 1), :WIDTH] if block < 2 else x2_ref[...]


def row_max(mine, other, keep):
    return jnp.max(jnp.where(keep, dot_t(mine, other), -2.0), axis=1, keepdims=True)


def off_diagonal(n):
    return iota((n, n), 0) != iota((n, n), 1)


def call(kernel, name, out_shape, flops, *args, mib=28, scratch=()):
    return pl.pallas_call(
        kernel,
        out_shape=out_shape,
        scratch_shapes=list(scratch),
        compiler_params=pltpu.CompilerParams(vmem_limit_bytes=mib * MIB),
        cost_estimate=pl.CostEstimate(flops=int(flops), bytes_accessed=2**20, transcendentals=0),
        name=name,
    )(*args)


def own_kernel(y_ref, best_ref, x2_ref):
    left, right = tail_rows(y_ref)
    x2_ref[:, :HALFW] = left
    x2_ref[:, HALFW:] = right
    ok = own_valid(y_ref)
    tops = []
    for a in range(3):
        mine = row_block(y_ref, x2_ref, a)
        top = jnp.full((256, 1), -2.0, F32)
        for b in range(3):
            keep = ok[b] & off_diagonal(256) if a == b else ok[b]
            top = jnp.maximum(top, row_max(mine, row_block(y_ref, x2_ref, b), keep))
        tops.append(top)
    best_ref[...] = slots(tops)


def cross_kernel(y_ref, x2_ref, s_ref, so_far_ref, best_ref, s2_ref):
    left, right = tail_rows(s_ref)
    s2_ref[:, :HALFW] = left
    s2_ref[:, HALFW:] = right
    ok = own_valid(s_ref)
    tops = []
    for a in range(3):
        mine = row_block(y_ref, x2_ref, a)
        top = jnp.full((256, 1), -2.0, F32)
        for b in range(3):
            top = jnp.maximum(top, row_max(mine, row_block(s_ref, s2_ref, b), ok[b]))
        tops.append(top)
    best_ref[...] = jnp.maximum(so_far_ref[...], slots(tops))


def valid_rows(y_ref):
    counts = y_ref[:, META:].astype(F32)
    head = (iota((ROWS, 1), 0) % HEAD).astype(F32) < counts[:, 0:1]
    source = jnp.max(counts.reshape(CHIPS, HEAD, 128), axis=1)
    tail = (iota((TAIL, 1), 0) // CHIPS + HEAD).astype(F32) < jnp.concatenate([source] * 4, axis=0)[:, 0:1]
    return [head[:256], head[256:], tail]


def tiles(room):
    size = min(room, 256)
    return [slice(start, start + size) for start in range(0, room, size)]


def column_max(scores, keep):
    return jnp.max(jnp.where(keep, scores, -2.0), axis=0, keepdims=True)


def received_kernel(s_ref, s2_ref, v_ref, so_far_ref, top_ref):
    room = v_ref.shape[0]

    def step(i, carry):
        start = pl.multiple_of(i * 256, 256)
        mine = v_ref[pl.ds(start, 256), :WIDTH]
        ok_s = valid_rows(s_ref)
        used = v_ref[:, WIDTH:].astype(F32)[:, 2:3] > 0.5
        top = jnp.full((1, 256), -2.0, F32)
        for b in range(3):
            top = jnp.maximum(top, column_max(dot_t(row_block(s_ref, s2_ref, b), mine), ok_s[b]))
        for at in tiles(room):
            keep = used[at] & (iota((256, 256), 0) + at.start != iota((256, 256), 1) + start)
            top = jnp.maximum(top, column_max(dot_t(v_ref[at, :WIDTH], mine), keep))
        top_ref[:, pl.ds(start, 256)] = jnp.broadcast_to(top, (8, 256))
        return carry

    lax.fori_loop(0, room // 256, step, 0)


def sibling_kernel(y_ref, x2_ref, v_ref, w_ref, so_far_ref, so_far_top_ref, out_ref, top_ref, best_ref, lane_ref):
    room = v_ref.shape[0]
    about_v = v_ref[:, WIDTH:].astype(F32)
    about_w = w_ref[:, WIDTH:].astype(F32)
    lanes = jnp.concatenate([about_v, about_w], axis=0).T[:8, :]
    lane_ref[...] = lanes
    used = lanes[2:3, :] > 0.5
    top_ref[...] = so_far_top_ref[...]
    best_ref[...] = jnp.full(best_ref.shape, -2.0, F32)

    def step(i, carry):
        start = pl.multiple_of(i * 256, 256)
        ok_y = valid_rows(y_ref)
        for ref, first in ((v_ref, 0), (w_ref, room)):
            rows = ref[pl.ds(start, 256), :WIDTH]
            ok = lane_ref[2:3, pl.ds(start + first, 256)] > 0.5
            top = top_ref[:, pl.ds(start, 256)]
            for a in range(3):
                scores = dot_t(row_block(y_ref, x2_ref, a), rows)
                best = jnp.max(jnp.where(ok, scores, -2.0), axis=1, keepdims=True)
                span = slice(256 * a, 256 * (a + 1))
                best_ref[span, :] = jnp.maximum(best_ref[span, :], best)
                top = jnp.maximum(top, column_max(scores, ok_y[a]))
            if first == 0:
                for at in tiles(room):
                    theirs = w_ref[at, WIDTH:].astype(F32)[:, 2:3] > 0.5
                    top = jnp.maximum(top, column_max(dot_t(w_ref[at, :WIDTH], rows), theirs))
                top_ref[:, pl.ds(start, 256)] = top
        return carry

    lax.fori_loop(0, room // 256, step, 0)
    best = jnp.maximum(so_far_ref[...], slots([best_ref[256 * a : 256 * (a + 1), 0:1] for a in range(3)]))
    source = lanes[0:1, :room].astype(jnp.int32)
    here = (iota((CHIPS, room), 0) == source) & used[:, :room]
    rank = onehot((iota((room, 128), 1) == about_v[:, 1:2].astype(jnp.int32)) & (about_v[:, 2:3] > 0.5))
    placed = jnp.zeros((CHIPS, 128), F32)
    for piece in split3(jnp.where(here, top_ref[0:1, :], 0.0)):
        placed = placed + dot(piece, rank)
    filled = dot(onehot(here), rank)
    full = jnp.maximum(about_v[0:1, 3:4], about_w[0:1, 3:4])
    out = jnp.where(filled > 0.5, placed, best)
    out_ref[...] = jnp.where(iota((CHIPS, 128), 1) == 127, full, out)


def after_kernel(v_ref, best_ref, out_ref):
    pass


def after(v, best):
    anywhere = pl.BlockSpec(memory_space=pl.ANY)
    return pl.pallas_call(
        after_kernel,
        in_specs=[anywhere, anywhere],
        out_specs=anywhere,
        out_shape=jax.ShapeDtypeStruct(v.shape, v.dtype),
        input_output_aliases={0: 0},
        compiler_params=pltpu.CompilerParams(vmem_limit_bytes=MIB),
        name="overflow_after_own",
    )(v, best)


def owner_side(y, room):
    swap = [(0, 1), (1, 0)]
    mib = 28 if room <= 256 else 52
    slot_shape = jax.ShapeDtypeStruct((CHIPS, 128), F32)
    top_shape = jax.ShapeDtypeStruct((8, room), F32)
    tail_shape = jax.ShapeDtypeStruct((TAIL, WIDTH), BF16)
    packed_shape = jax.ShapeDtypeStruct((room, WIDTH + 128), BF16)
    s = lax.ppermute(y, "core", swap)
    v = call(pack_kernel, "pack_overflow", packed_shape, 3e9, y, mib=mib)
    v = lax.ppermute(v, "y", [(0, 1), (1, 0), (2, 3), (3, 2)])
    best, x2 = call(own_kernel, "own_pairs", [slot_shape, tail_shape], 5e9, y)
    best, s2 = call(cross_kernel, "cross_pairs", [slot_shape, tail_shape], 6e9, y, x2, s, best)
    v = after(v, best)
    w = lax.ppermute(v, "core", swap)
    top = call(received_kernel, "received_pairs", top_shape, 3e9, s, s2, v, best, mib=mib)
    scratch = [pltpu.VMEM((8, room), F32), pltpu.VMEM((ROWS + TAIL, 128), F32), pltpu.VMEM((8, 2 * room), F32)]
    return call(sibling_kernel, "sibling_pairs", slot_shape, 1e9, y, x2, v, w, best, top, mib=mib, scratch=scratch)


def pick_kernel(back_ref, rank_ref, out_ref, full_ref):
    rank = rank_ref[0:1, :]
    cluster = rank_ref[1:2, :]
    at_rank = onehot(iota((128, DOCS), 0) == rank)
    back = back_ref[...]
    found = jnp.zeros((CHIPS, DOCS), F32)
    for piece in split3(back):
        found = found + dot(piece, at_rank)
    out_ref[...] = jnp.sum(jnp.where(iota((CHIPS, DOCS), 0) == cluster, found, 0.0), axis=0, keepdims=True)
    full_ref[0, 0] = jnp.max(back[:, 127:128])


def return_to_source(best, rank):
    back = lax.all_to_all(best, CHIP_AXES, split_axis=0, concat_axis=0, tiled=True)
    return pl.pallas_call(
        pick_kernel,
        out_specs=[pl.BlockSpec(memory_space=pltpu.VMEM), pl.BlockSpec(memory_space=pltpu.SMEM)],
        out_shape=[jax.ShapeDtypeStruct((1, DOCS), F32), jax.ShapeDtypeStruct((1, 1), F32)],
        compiler_params=pltpu.CompilerParams(vmem_limit_bytes=4 * MIB),
        name="pick_documents",
    )(back, rank)


def next_chip(x, way, core):
    bits = 4 * core if way < 2 else 2
    unit = 1 << bits
    place = (iota(x.shape, 1) >> bits) & 3
    if way % 2 == 0:
        return jnp.where(place == 3, pltpu.roll(x, 3 * unit, axis=1), pltpu.roll(x, 128 - unit, axis=1))
    return jnp.where(place == 0, pltpu.roll(x, 128 - 3 * unit, axis=1), pltpu.roll(x, unit, axis=1))


def neighbour(z, x, y, way, core):
    step = 1 if way % 2 == 0 else 3
    if way < 2:
        y, z = jnp.where(core == 0, (y + step) & 3, y), jnp.where(core == 0, z, (z + step) & 3)
    else:
        x = (x + step) & 3
    return 16 * z + 4 * x + y


def spread_kernel(embed_hbm, group_hbm, half_hbm, out_ref, rank_ref, embed_ref, group_ref, half_ref, unit_ref, note_ref, slot_ref, sems):
    names = [pltpu.make_async_copy(group_hbm, group_ref, sems.at[0]), pltpu.make_async_copy(half_hbm, half_ref, sems.at[1])]
    size = DOCS // PARTS
    spans = [pl.ds(size * part, size) for part in range(PARTS)]
    parts = [pltpu.make_async_copy(embed_hbm.at[span, :], embed_ref.at[span, :], sems.at[2 + i]) for i, span in enumerate(spans)]
    for copy in names + parts:
        copy.start()
    for copy in names:
        copy.wait()
    group, half = group_ref[...], half_ref[...]
    z, x, y = ((group >> 4) + 2 * half) & 3, ((group >> 2) + 2 * half) & 3, (group + 2 * half) & 3
    home = 16 * z + 4 * x + y
    member = onehot((iota((2 * CHIPS, DOCS), 0) & (CHIPS - 1)) == home)
    earlier = onehot(iota((DOCS, DOCS), 0) < iota((DOCS, DOCS), 1))
    before = dot(member[:CHIPS], earlier)
    rank = jnp.sum(before * member[:CHIPS].astype(F32), axis=0, keepdims=True)
    counts = dot_t(jnp.ones((8, DOCS), BF16), member)
    left = jnp.maximum(counts - SLOTS, 0.0)
    free = SLOTS - jnp.minimum(counts, float(SLOTS))
    given = [jnp.zeros((8, 2 * CHIPS), F32) for _ in range(WAYS)]
    core = lax.axis_index("core")
    turn = (21 * lax.axis_index("z") + 5 * lax.axis_index("x") + lax.axis_index("y")) % 6
    early = jnp.where(turn < 3, 1.0, 0.0)
    plan = [(0, early), (1, 1.0), (0, 1.0 - early), (2, early), (3, 1.0), (2, 1.0 - early), (0, 1.0), (1, 1.0)]
    plan += [(d, 24.0) for d in range(WAYS)]
    for part, (copy, span) in enumerate(zip(parts, spans)):
        copy.wait()
        floats = embed_ref[span, :].astype(F32)
        scale = lax.rsqrt(jnp.sum(floats * floats, axis=1, keepdims=True) + 1e-06)
        unit_ref[span, :] = (floats * scale).astype(BF16)
        for d, most in plan[3 * part : 3 * part + 3]:
            take = jnp.minimum(jnp.minimum(left, next_chip(free, d, core)), most)
            given[d] = given[d] + take
            left = left - take
            free = free - next_chip(take, d ^ 1, core)
    ends, offsets = [], []
    total, used = jnp.zeros_like(left), jnp.zeros_like(left)
    for d in range(WAYS):
        total = total + given[d]
        ends.append(total)
        offsets.append(next_chip(used, d, core))
        used = used + next_chip(given[d], d ^ 1, core)
    table = jnp.concatenate([row[0:1] for row in ends + offsets] + [jnp.zeros((8, 2 * CHIPS), F32)], axis=0)
    table = jnp.where(iota(table.shape, 1) < CHIPS, table, 0.0)
    found = dot(table.astype(BF16), member)
    beyond = rank - SLOTS
    own = beyond < 0.0
    chip = home
    row = jnp.where(own, rank.astype(jnp.int32), -1)
    came = jnp.zeros((1, DOCS), F32)
    for d in range(WAYS):
        start = found[d - 1 : d] if d else jnp.zeros((1, DOCS), F32)
        this = (beyond >= start) & (beyond < found[d : d + 1])
        offset = found[WAYS + d : WAYS + d + 1]
        row = jnp.where(this, SLOTS - 1 - (offset + beyond - start).astype(jnp.int32), row)
        chip = jnp.where(this, neighbour(z, x, y, d, core), chip)
        came = jnp.where(this, d + 1.0, came)
    slot_ref[0:1, :] = jnp.where((row >= 0) & (row < HEAD), chip * HEAD + row, -1)
    slot_ref[1:2, :] = jnp.where(row >= HEAD, chip * HEAD + 4 * (row - HEAD), -8)
    rank_ref[0:1, :] = rank.astype(jnp.int32)
    rank_ref[1:2, :] = home
    lost = jnp.max(jnp.where(row < 0, 1.0, 0.0), axis=1, keepdims=True)
    line = iota((128, DOCS), 0)
    for part in range(2):
        at = line - 8 * part
        notes = jnp.where(at == 0, jnp.where(own, 1.0, 0.0), jnp.where(at == 1, came, jnp.where(at == 2, rank, 0.0)))
        note_ref[part] = jnp.where(at == 3, lost, notes).T.astype(BF16)

    at = iota((ROWS, DOCS), 0)
    whole = onehot(at == slot_ref[0:1, :])
    quarters = jnp.zeros((ROWS, QUARTER), F32)
    notes = dot(whole, note_ref[0])
    for q in range(4):
        span = slice(QUARTER * q, QUARTER * (q + 1))
        out_ref[:, span] = dot(whole, unit_ref[:, span]).astype(BF16)
        this = onehot(at == slot_ref[1:2, :] + q)
        quarters = quarters + dot(this, unit_ref[:, span])
        notes = notes + dot(this, note_ref[1])
    out_ref[:, WIDTH:NOTES] = quarters.astype(BF16)
    out_ref[:, NOTES:] = notes.astype(BF16)


def spread_documents(embed, group, half):
    far = pl.BlockSpec(memory_space=pltpu.HBM)
    operands = [pltpu.with_memory_space_constraint(x, pltpu.HBM) for x in (embed, group, half)]
    return pl.pallas_call(
        spread_kernel,
        in_specs=[far, far, far],
        out_shape=[jax.ShapeDtypeStruct((ROWS, FIRST), BF16), jax.ShapeDtypeStruct((8, DOCS), jnp.int32)],
        scratch_shapes=[
            pltpu.VMEM((DOCS, WIDTH), BF16),
            pltpu.VMEM((1, DOCS), jnp.int32),
            pltpu.VMEM((1, DOCS), jnp.int32),
            pltpu.VMEM((DOCS, WIDTH), BF16),
            pltpu.VMEM((2, DOCS, 128), BF16),
            pltpu.VMEM((8, DOCS), jnp.int32),
            pltpu.SemaphoreType.DMA((2 + PARTS,)),
        ],
        compiler_params=pltpu.CompilerParams(vmem_limit_bytes=28 * MIB),
        cost_estimate=pl.CostEstimate(flops=2 * 10**9, bytes_accessed=9 * 2**20, transcendentals=256),
        name="spread_documents",
    )(*operands)


def quarter_rows(y_ref, out_ref, first):
    to, at = iota((4 * REST, ROWS), 0), iota((4 * REST, ROWS), 1)
    row = to % REST
    want = (row % CHIPS) * HEAD + 4 * (row // CHIPS) + to // REST
    rows = dot(onehot(at == want), y_ref[:, WIDTH:NOTES]).astype(BF16)
    for q in range(4):
        out_ref[first : first + REST, QUARTER * q : QUARTER * (q + 1)] = rows[REST * q : REST * (q + 1)]


def at_home(y_ref):
    notes = y_ref[:, NOTES:].astype(F32).T[:16, :]
    at, to = iota((ROWS, REST), 0), iota((ROWS, REST), 1)
    pick = onehot(at == (to % CHIPS) * HEAD + 4 * (to // CHIPS))
    return notes[0:1, :] > 0.5, dot(notes[8:16, :].astype(BF16), pick)[0:1, :] > 0.5


def sort_kernel(y_ref, *v_refs):
    notes = y_ref[:, NOTES:].astype(F32).T[:16, :]
    quarter = iota((1, ROWS), 1) % 4
    ways = [notes[1:2, :] == d + 1.0 for d in range(WAYS)]
    ways += [(notes[9:10, :] == d + 1.0) & (quarter == q) for q in range(4) for d in range(WAYS)]
    flags = jnp.concatenate([jnp.where(way, 1.0, 0.0) for way in ways] + [jnp.zeros((4, ROWS), F32)], axis=0)
    before = onehot(iota((ROWS, ROWS), 0) < iota((ROWS, ROWS), 1))
    place = dot(flags.astype(BF16), before)
    sums = jnp.sum(flags, axis=1, keepdims=True)
    loads = [sums[d : d + 1] + sums[WAYS + d : WAYS + d + 1] - ROOMS[d] for d in range(WAYS)]
    most = functools.reduce(jnp.maximum, loads)
    lost = jnp.max(jnp.maximum(notes[3:4, :], notes[11:12, :]), axis=1, keepdims=True)
    full = jnp.where((most > 0.5) | (lost > 0.5), 1.0, 0.0)

    def take(first, shift):
        rows = []
        for d in range(WAYS):
            slot = iota((ROOMS[d], ROWS), 0)
            to = place[first + d : first + d + 1, :] + (sums[d : d + 1, :] if shift else 0.0)
            rows.append(jnp.where((slot == to.astype(jnp.int32)) & ways[first + d], 1.0, 0.0))
        return jnp.concatenate(rows, axis=0).astype(BF16)

    whole = take(0, False)
    lane = iota((ROWS, 128), 1)
    source = (iota((ROWS, 128), 0) // HEAD).astype(F32)
    extra = jnp.where(lane == 4, source, jnp.where(lane == 5, 1.0, 0.0))
    given = y_ref[:, NOTES:].astype(F32)
    info = dot(whole, jnp.where(lane == 2, given, extra).astype(BF16))
    some = jnp.concatenate([take(WAYS * (1 + q), True) for q in range(4)], axis=0)
    quarters = dot(some, y_ref[:, WIDTH:NOTES])
    for q in range(4):
        span = slice(QUARTER * q, QUARTER * (q + 1))
        rows = (dot(whole, y_ref[:, span]) + quarters[OVER * q : OVER * (q + 1)]).astype(BF16)
        for d in range(WAYS):
            v_refs[d][:, span] = rows[STARTS[d] : STARTS[d] + ROOMS[d]]
        if q == 0:
            moved = jnp.where(lane == 2, pltpu.roll(given, 128 - 8, axis=1), extra)
            info = info + dot(some[:OVER], moved.astype(BF16))
    info = jnp.where(iota((OVER, 128), 1) == 3, full, info).astype(BF16)
    for d in range(WAYS):
        v_refs[d][:, WIDTH:] = info[STARTS[d] : STARTS[d] + ROOMS[d]]


def to_slots(top, rest):
    keep = iota((ROWS, 128), 1) == iota((ROWS, 128), 0) % HEAD
    head = jnp.max(jnp.where(keep, top, -2.0).reshape(CHIPS, HEAD, 128), axis=1)
    keep = iota((REST, 128), 1) == iota((REST, 128), 0) // CHIPS + HEAD
    return jnp.maximum(head, jnp.max(jnp.where(keep, rest, -2.0).reshape(2, CHIPS, 128), axis=0))


def upright(line):
    return jnp.broadcast_to(line, (8, line.shape[1])).T[:, 0:1]


def lane_max(scores, keep):
    return jnp.max(jnp.where(keep, scores, -2.0), axis=1, keepdims=True)


def home_kernel(y_ref, best_ref):
    ok = y_ref[:, NOTES:].astype(F32).T[0:1, :] > 0.5
    here = y_ref[:, NOTES:].astype(F32)[:, 0:1] > 0.5
    low, high = y_ref[:256, :WIDTH], y_ref[256:, :WIDTH]
    both = dot_t(low, high)
    top0 = jnp.maximum(row_max(low, low, ok[:, :256] & off_diagonal(256)), lane_max(both, ok[:, 256:]))
    top1 = row_max(high, high, ok[:, 256:] & off_diagonal(256))
    top1 = jnp.maximum(top1, upright(column_max(both, here[:256])))
    best_ref[...] = jnp.broadcast_to(jnp.concatenate([top0, top1], axis=0), (ROWS, 128))


def other_core_kernel(y_ref, s_ref, so_far_ref, best_ref, rest_ref):
    quarter_rows(y_ref, rest_ref, 0)
    quarter_rows(s_ref, rest_ref, REST)
    (ok, ok2), (ok_s, ok_s2) = at_home(y_ref), at_home(s_ref)
    theirs = s_ref[:, :WIDTH]
    mine = rest_ref[:REST]
    upper = row_max(jnp.concatenate([y_ref[256:, :WIDTH], mine], axis=0), theirs, ok_s)
    tops = [row_max(y_ref[:256, :WIDTH], theirs, ok_s), upper[:256]]
    ok_rest = jnp.concatenate([jnp.where(ok2, 1.0, 0.0), jnp.where(ok_s2, 1.0, 0.0)], axis=1)
    scores = dot_t(rest_ref[...], y_ref[:, :WIDTH])
    beside = column_max(scores, upright(ok_rest) > 0.5)
    top = jnp.maximum(jnp.maximum(jnp.concatenate(tops, axis=0), upright(beside)), so_far_ref[:, 0:1])
    keep = (ok_rest > 0.5) & (iota((REST, 2 * REST), 0) != iota((REST, 2 * REST), 1))
    rest = jnp.maximum(lane_max(scores[:REST], ok), row_max(mine, rest_ref[...], keep))
    best_ref[...] = to_slots(top, jnp.maximum(rest, upper[256:]))


def join_kernel(*refs):
    out_ref = refs[-1]
    for d in range(WAYS):
        out_ref[STARTS[d] : STARTS[d] + ROOMS[d], :] = refs[d][...]


def notes_of(v_ref):
    return v_ref[:, WIDTH:].astype(F32).T[:8, :]


def guests_kernel(y_ref, s_ref, rest_ref, v_ref, so_far_ref, top_ref, own_ref):
    mine = v_ref[:, :WIDTH]
    used = v_ref[:, WIDTH:].astype(F32)[:, 5:6] > 0.5
    ok_v = notes_of(v_ref)[5:6, :] > 0.5
    top = row_max(mine, mine, ok_v & off_diagonal(OVER))
    (ok, ok2), (ok_s, ok_s2) = at_home(y_ref), at_home(s_ref)
    scores = dot_t(mine, y_ref[:, :WIDTH])
    own_ref[:, :ROWS] = jnp.broadcast_to(column_max(scores, used), (8, ROWS))
    top = jnp.maximum(top, lane_max(scores, ok))
    top = jnp.maximum(top, row_max(mine, s_ref[:, :WIDTH], ok_s))
    scores = dot_t(mine, rest_ref[...])
    own_ref[:, ROWS:] = jnp.broadcast_to(column_max(scores[:, :REST], used), (8, REST))
    top = jnp.maximum(top, jnp.maximum(lane_max(scores[:, :REST], ok2), lane_max(scores[:, REST:], ok_s2)))
    top_ref[...] = jnp.broadcast_to(top, (OVER, 128))


def finish_kernel(y_ref, rest_ref, v_ref, w_ref, so_far_ref, top_ref, own_ref, out_ref):
    about = v_ref[:, WIDTH:].astype(F32)
    about_w = w_ref[:, WIDTH:].astype(F32)
    lanes = notes_of(v_ref)
    theirs = w_ref[:, :WIDTH]
    used = about_w[:, 5:6] > 0.5
    head = jnp.maximum(own_ref[:, :ROWS], column_max(dot_t(theirs, y_ref[:, :WIDTH]), used))
    rest = jnp.maximum(own_ref[:, ROWS:], column_max(dot_t(theirs, rest_ref[:REST]), used))
    best = jnp.maximum(so_far_ref[...], to_slots(head.T[:, 0:1], rest.T[:, 0:1]))
    top = row_max(v_ref[:, :WIDTH], theirs, notes_of(w_ref)[5:6, :] > 0.5)
    top = jnp.maximum(top_ref[...], top)
    here = onehot((iota((CHIPS, OVER), 0) == lanes[4:5, :].astype(jnp.int32)) & (lanes[5:6, :] > 0.5))
    rank = (iota((OVER, 128), 1) == about[:, 2:3].astype(jnp.int32)) & (about[:, 5:6] > 0.5)
    pieces = dot(here, jnp.concatenate([*split3(jnp.where(rank, top, 0.0)), onehot(rank)], axis=1))
    placed = pieces[:, :128] + pieces[:, 128:256] + pieces[:, 256:384]
    filled = pieces[:, 384:]
    full = jnp.maximum(about[0:1, 3:4], about_w[0:1, 3:4])
    out = jnp.where(filled > 0.5, placed, best)
    out_ref[...] = jnp.where(iota((CHIPS, 128), 1) == 127, full, out)


def way_home(way):
    pairs = []
    for z, x, y, core in itertools.product(range(4), range(4), range(4), range(2)):
        to = [z, x, y]
        axis = 1 if way >= 2 else 2 if core == 0 else 0
        to[axis] = (to[axis] + (3 if way % 2 == 0 else 1)) % 4
        pairs.append((32 * z + 8 * x + 2 * y + core, 32 * to[0] + 8 * to[1] + 2 * to[2] + core))
    return pairs


def owner_short(y):
    swap = [(0, 1), (1, 0)]
    slot_shape = jax.ShapeDtypeStruct((CHIPS, 128), F32)
    rest_shape = jax.ShapeDtypeStruct((2 * REST, WIDTH), BF16)
    way_shapes = [jax.ShapeDtypeStruct((room, SHORT), BF16) for room in ROOMS]
    s = lax.ppermute(y, "core", swap)
    ways = call(sort_kernel, "sort_overflow", way_shapes, 3e9, y, mib=20)
    came = []
    for d, v in enumerate(ways):
        came.append(lax.ppermute(v, ALL_AXES, way_home(d)))
    best = call(home_kernel, "home_pairs", jax.ShapeDtypeStruct((ROWS, 128), F32), 1e10, y, mib=24)
    best, rest = call(other_core_kernel, "other_core_pairs", [slot_shape, rest_shape], 4e10, y, s, best, mib=24)
    v = call(join_kernel, "join_overflow", jax.ShapeDtypeStruct((OVER, SHORT), BF16), 1e8, *came, best, mib=8)
    w = lax.ppermute(v, "core", swap)
    shapes = [jax.ShapeDtypeStruct((OVER, 128), F32), jax.ShapeDtypeStruct((8, OWN), F32)]
    top, own = call(guests_kernel, "guest_pairs", shapes, 6e9, y, s, rest, v, best, mib=24)
    return call(finish_kernel, "finish_pairs", slot_shape, 3e9, y, rest, v, w, best, top, own, mib=24)


def wide_form(embed, group, half):
    sent, rank = place_documents(embed, group, half)
    y = lax.all_to_all(sent, CHIP_AXES, split_axis=0, concat_axis=0, tiled=True)
    return return_to_source(owner_side(y, ROWS + TAIL), rank)[0]


def on_device(embed, group, half):
    group, half = group.reshape(1, DOCS), half.reshape(1, DOCS)
    sent, rank = spread_documents(embed, group, half)
    y = lax.all_to_all(sent, CHIP_AXES, split_axis=0, concat_axis=0, tiled=True)
    nearest, full = return_to_source(owner_short(y), rank)
    nearest = lax.cond(
        full[0, 0] > 0.5,
        lambda embed, group, half, nearest: wide_form(embed, group, half),
        lambda embed, group, half, nearest: nearest,
        embed,
        group,
        half,
        nearest,
    )
    return nearest.reshape(DOCS)


def solution(mesh):
    devices = mesh.devices.reshape(4, 4, 4, 2)
    fine = Mesh(devices, ALL_AXES)
    return jax.shard_map(
        on_device,
        mesh=fine,
        in_specs=(P(ALL_AXES, None), P(ALL_AXES, None), P(ALL_AXES)),
        out_specs=P(ALL_AXES),
        check_vma=False,
    )
```

```python
import functools
import itertools

import jax
import jax.numpy as jnp
from jax import lax
from jax.experimental import pallas as pl
from jax.experimental.pallas import tpu as pltpu
from jax.sharding import Mesh, PartitionSpec as P

WIDTH = 4096
HALFW = WIDTH // 2
CHIPS = 64
DOCS = 256
CAP = 24
SIDE = 12
HEAD = 8
PARTS = 4
ROWS = CHIPS * HEAD
TAIL = CHIPS * (SIDE - HEAD)
META = WIDTH + HALFW
SENT = META + 128
CHIP_AXES = ("z", "x", "y")
SHORT = WIDTH + 128
SLOTS = 10
ROOMS = (64, 64, 32, 32)
WAYS = len(ROOMS)
STARTS = (0, 64, 128, 160)
OVER = sum(ROOMS)
QUARTER = WIDTH // 4
NOTES = WIDTH + QUARTER
FIRST = NOTES + 128
REST = CHIPS * (SLOTS - HEAD)
OWN = ROWS + REST
ALL_AXES = CHIP_AXES + ("core",)
F32 = jnp.float32
BF16 = jnp.bfloat16
MIB = 1024 * 1024


def iota(shape, axis):
    return lax.broadcasted_iota(jnp.int32, shape, axis)


def dot(a, b):
    return jnp.dot(a, b, preferred_element_type=F32)


def dot_t(a, b):
    return lax.dot_general(a, b, (((1,), (1,)), ((), ())), preferred_element_type=F32)


def onehot(mask):
    return jnp.where(mask, 1.0, 0.0).astype(BF16)


def split3(x):
    a = x.astype(BF16)
    rest = x - a.astype(F32)
    b = rest.astype(BF16)
    c = (rest - b.astype(F32)).astype(BF16)
    return a, b, c


def send_kernel(embed_hbm, group_hbm, half_hbm, out_ref, rank_ref, embed_ref, group_ref, half_ref, unit_ref, slot_ref, meta_ref, sems):
    step = pl.program_id(0)

    @pl.when(step == 0)
    def _():
        names = [pltpu.make_async_copy(group_hbm, group_ref, sems.at[0]), pltpu.make_async_copy(half_hbm, half_ref, sems.at[1])]
        size = DOCS // PARTS
        spans = [pl.ds(size * part, size) for part in range(PARTS)]
        parts = [pltpu.make_async_copy(embed_hbm.at[span, :], embed_ref.at[span, :], sems.at[2 + i]) for i, span in enumerate(spans)]
        for copy in names + parts:
            copy.start()
        for copy in names:
            copy.wait()
        cluster = 2 * group_ref[...] + half_ref[...]
        other = cluster + 1 - 2 * half_ref[...]
        member = iota((CHIPS, DOCS), 0) == cluster
        earlier = onehot(iota((DOCS, DOCS), 0) < iota((DOCS, DOCS), 1))
        before = dot(onehot(member), earlier)
        rank = jnp.sum(jnp.where(member, before, 0.0), axis=0, keepdims=True).astype(jnp.int32)
        over = rank >= SIDE
        chip = jnp.where(over, other, cluster)
        row = jnp.where(over, CAP - 1 - rank, rank)
        slot_ref[0:1, :] = jnp.where(row < HEAD, chip * HEAD + row, -1)
        slot_ref[1:2, :] = jnp.where(row >= HEAD, chip * HEAD + row - HEAD, -1)
        slot_ref[2:3, :] = jnp.where(row >= HEAD, chip * HEAD + row - HEAD + 4, -1)
        rank_ref[0:1, :] = rank
        rank_ref[1:2, :] = cluster
        own = jnp.sum(jnp.where(member, 1.0, 0.0), axis=1, keepdims=True)
        oth = jnp.sum(jnp.where(iota((CHIPS, DOCS), 0) == other, 1.0, 0.0), axis=1, keepdims=True)
        lane = iota((CHIPS, 128), 1)
        meta = jnp.where(lane == 0, own, jnp.where(lane == 1, oth, 0.0))
        meta_ref[...] = jnp.broadcast_to(meta[:, None, :], (CHIPS, HEAD, 128)).reshape(ROWS, 128)
        for copy, span in zip(parts, spans):
            copy.wait()
            floats = embed_ref[span, :].astype(F32)
            scale = lax.rsqrt(jnp.sum(floats * floats, axis=1, keepdims=True) + 1e-06)
            unit_ref[span, :] = (floats * scale).astype(BF16)

    rows = out_ref.shape[0]
    base = step * rows
    here = iota((rows, DOCS), 0) + base
    head = onehot(here == slot_ref[0:1, :])
    left = onehot(here == slot_ref[1:2, :])
    right = onehot(here == slot_ref[2:3, :])
    out_ref[:, :WIDTH] = dot(head, unit_ref[...]).astype(BF16)
    out_ref[:, WIDTH:META] = (dot(left, unit_ref[:, :HALFW]) + dot(right, unit_ref[:, HALFW:])).astype(BF16)
    out_ref[:, META:] = meta_ref[pl.ds(pl.multiple_of(base, rows), rows), :].astype(BF16)


def place_documents(embed, group, half):
    steps = 4
    far = pl.BlockSpec(memory_space=pltpu.HBM)
    operands = [pltpu.with_memory_space_constraint(x, pltpu.HBM) for x in (embed, group, half)]
    return pl.pallas_call(
        send_kernel,
        grid=(steps,),
        in_specs=[far, far, far],
        out_specs=[pl.BlockSpec((ROWS // steps, SENT), lambda i: (i, 0)), pl.BlockSpec((8, DOCS), lambda i: (0, 0))],
        out_shape=[jax.ShapeDtypeStruct((ROWS, SENT), BF16), jax.ShapeDtypeStruct((8, DOCS), jnp.int32)],
        scratch_shapes=[
            pltpu.VMEM((DOCS, WIDTH), BF16),
            pltpu.VMEM((1, DOCS), jnp.int32),
            pltpu.VMEM((1, DOCS), jnp.int32),
            pltpu.VMEM((DOCS, WIDTH), BF16),
            pltpu.VMEM((8, DOCS), jnp.int32),
            pltpu.VMEM((ROWS, 128), F32),
            pltpu.SemaphoreType.DMA((2 + PARTS,)),
        ],
        compiler_params=pltpu.CompilerParams(vmem_limit_bytes=28 * MIB),
        cost_estimate=pl.CostEstimate(flops=2 * 10**9, bytes_accessed=9 * 2**20, transcendentals=256),
        name="place_documents",
    )(*operands)


def tail_rows(y_ref):
    to = iota((TAIL, ROWS), 0)
    at = iota((TAIL, ROWS), 1)
    want = (to % CHIPS) * HEAD + to // CHIPS
    left = dot(onehot(at == want), y_ref[:, WIDTH:META]).astype(BF16)
    right = dot(onehot(at == want + 4), y_ref[:, WIDTH:META]).astype(BF16)
    return left, right


def lane_counts(y_ref):
    meta = y_ref[:, META:].astype(F32).T[:8, :]
    pick = onehot(iota((ROWS, TAIL), 0) == (iota((ROWS, TAIL), 1) % CHIPS) * HEAD)
    tail = dot(meta.astype(BF16), pick)
    return meta[0:1, :], meta[1:2, :], tail[0:1, :], tail[1:2, :]


def pack_kernel(y_ref, v_ref):
    room = v_ref.shape[0]
    counts = y_ref[:, META:].astype(F32).T[:8, :]
    first = CAP - counts[1:2, :]
    row = (iota((1, ROWS), 1) % HEAD).astype(F32)
    low = row < 4
    over = [row >= first, low & (row + HEAD >= first), ~low & (row + HEAD - 4 >= first)]
    flags = [jnp.where(mask, 1.0, 0.0) for mask in over]
    before = onehot(iota((ROWS, ROWS), 0) < iota((ROWS, ROWS), 1))
    place = dot(jnp.concatenate(flags + [jnp.zeros((5, ROWS), F32)], axis=0).astype(BF16), before)
    count = jnp.sum(flags[0], axis=1, keepdims=True)
    full = jnp.where(count + jnp.sum(flags[1], axis=1, keepdims=True) > room, 1.0, 0.0)
    places = [place[0:1, :], place[1:2, :] + count, place[2:3, :] + count]
    take = [onehot((iota((room, ROWS), 0) == at.astype(jnp.int32)) & mask) for at, mask in zip(places, over)]
    tail = y_ref[:, WIDTH:META]
    v_ref[:, :HALFW] = (dot(take[0], y_ref[:, :HALFW]) + dot(take[1], tail)).astype(BF16)
    v_ref[:, HALFW:WIDTH] = (dot(take[0], y_ref[:, HALFW:WIDTH]) + dot(take[2], tail)).astype(BF16)
    lane = iota((ROWS, 128), 1)
    at = iota((ROWS, 128), 0)

    def about(row):
        return jnp.where(lane == 0, at // HEAD, jnp.where(lane == 1, CAP - 1 - row, jnp.where(lane == 2, 1, 0))).astype(F32).astype(BF16)

    info = dot(take[0], about(at % HEAD)) + dot(take[1], about(at % HEAD + HEAD))
    v_ref[:, WIDTH:] = jnp.where(iota((room, 128), 1) == 3, full, info).astype(BF16)


def slots(tops):
    lane = iota((256, 128), 1)
    at = iota((256, 128), 0)
    head = [jnp.max(jnp.where(lane == at % HEAD, top, -2.0).reshape(32, HEAD, 128), axis=1) for top in tops[:2]]
    tail = jnp.max(jnp.where(lane == at // CHIPS + HEAD, tops[2], -2.0).reshape(4, CHIPS, 128), axis=0)
    return jnp.maximum(jnp.concatenate(head, axis=0), tail)


def own_valid(y_ref):
    own1, _, own2, _ = lane_counts(y_ref)
    ok1 = (iota((1, ROWS), 1) % HEAD).astype(F32) < own1
    ok2 = (iota((1, TAIL), 1) // CHIPS + HEAD).astype(F32) < own2
    return [ok1[:, :256], ok1[:, 256:], ok2]


def row_block(y_ref, x2_ref, block):
    return y_ref[256 * block : 256 * (block + 1), :WIDTH] if block < 2 else x2_ref[...]


def row_max(mine, other, keep):
    return jnp.max(jnp.where(keep, dot_t(mine, other), -2.0), axis=1, keepdims=True)


def off_diagonal(n):
    return iota((n, n), 0) != iota((n, n), 1)


def call(kernel, name, out_shape, flops, *args, mib=28, scratch=()):
    return pl.pallas_call(
        kernel,
        out_shape=out_shape,
        scratch_shapes=list(scratch),
        compiler_params=pltpu.CompilerParams(vmem_limit_bytes=mib * MIB),
        cost_estimate=pl.CostEstimate(flops=int(flops), bytes_accessed=2**20, transcendentals=0),
        name=name,
    )(*args)


def own_kernel(y_ref, best_ref, x2_ref):
    left, right = tail_rows(y_ref)
    x2_ref[:, :HALFW] = left
    x2_ref[:, HALFW:] = right
    ok = own_valid(y_ref)
    tops = []
    for a in range(3):
        mine = row_block(y_ref, x2_ref, a)
        top = jnp.full((256, 1), -2.0, F32)
        for b in range(3):
            keep = ok[b] & off_diagonal(256) if a == b else ok[b]
            top = jnp.maximum(top, row_max(mine, row_block(y_ref, x2_ref, b), keep))
        tops.append(top)
    best_ref[...] = slots(tops)


def cross_kernel(y_ref, x2_ref, s_ref, so_far_ref, best_ref, s2_ref):
    left, right = tail_rows(s_ref)
    s2_ref[:, :HALFW] = left
    s2_ref[:, HALFW:] = right
    ok = own_valid(s_ref)
    tops = []
    for a in range(3):
        mine = row_block(y_ref, x2_ref, a)
        top = jnp.full((256, 1), -2.0, F32)
        for b in range(3):
            top = jnp.maximum(top, row_max(mine, row_block(s_ref, s2_ref, b), ok[b]))
        tops.append(top)
    best_ref[...] = jnp.maximum(so_far_ref[...], slots(tops))


def valid_rows(y_ref):
    counts = y_ref[:, META:].astype(F32)
    head = (iota((ROWS, 1), 0) % HEAD).astype(F32) < counts[:, 0:1]
    source = jnp.max(counts.reshape(CHIPS, HEAD, 128), axis=1)
    tail = (iota((TAIL, 1), 0) // CHIPS + HEAD).astype(F32) < jnp.concatenate([source] * 4, axis=0)[:, 0:1]
    return [head[:256], head[256:], tail]


def tiles(room):
    size = min(room, 256)
    return [slice(start, start + size) for start in range(0, room, size)]


def column_max(scores, keep):
    return jnp.max(jnp.where(keep, scores, -2.0), axis=0, keepdims=True)


def received_kernel(s_ref, s2_ref, v_ref, so_far_ref, top_ref):
    room = v_ref.shape[0]

    def step(i, carry):
        start = pl.multiple_of(i * 256, 256)
        mine = v_ref[pl.ds(start, 256), :WIDTH]
        ok_s = valid_rows(s_ref)
        used = v_ref[:, WIDTH:].astype(F32)[:, 2:3] > 0.5
        top = jnp.full((1, 256), -2.0, F32)
        for b in range(3):
            top = jnp.maximum(top, column_max(dot_t(row_block(s_ref, s2_ref, b), mine), ok_s[b]))
        for at in tiles(room):
            keep = used[at] & (iota((256, 256), 0) + at.start != iota((256, 256), 1) + start)
            top = jnp.maximum(top, column_max(dot_t(v_ref[at, :WIDTH], mine), keep))
        top_ref[:, pl.ds(start, 256)] = jnp.broadcast_to(top, (8, 256))
        return carry

    lax.fori_loop(0, room // 256, step, 0)


def sibling_kernel(y_ref, x2_ref, v_ref, w_ref, so_far_ref, so_far_top_ref, out_ref, top_ref, best_ref, lane_ref):
    room = v_ref.shape[0]
    about_v = v_ref[:, WIDTH:].astype(F32)
    about_w = w_ref[:, WIDTH:].astype(F32)
    lanes = jnp.concatenate([about_v, about_w], axis=0).T[:8, :]
    lane_ref[...] = lanes
    used = lanes[2:3, :] > 0.5
    top_ref[...] = so_far_top_ref[...]
    best_ref[...] = jnp.full(best_ref.shape, -2.0, F32)

    def step(i, carry):
        start = pl.multiple_of(i * 256, 256)
        ok_y = valid_rows(y_ref)
        for ref, first in ((v_ref, 0), (w_ref, room)):
            rows = ref[pl.ds(start, 256), :WIDTH]
            ok = lane_ref[2:3, pl.ds(start + first, 256)] > 0.5
            top = top_ref[:, pl.ds(start, 256)]
            for a in range(3):
                scores = dot_t(row_block(y_ref, x2_ref, a), rows)
                best = jnp.max(jnp.where(ok, scores, -2.0), axis=1, keepdims=True)
                span = slice(256 * a, 256 * (a + 1))
                best_ref[span, :] = jnp.maximum(best_ref[span, :], best)
                top = jnp.maximum(top, column_max(scores, ok_y[a]))
            if first == 0:
                for at in tiles(room):
                    theirs = w_ref[at, WIDTH:].astype(F32)[:, 2:3] > 0.5
                    top = jnp.maximum(top, column_max(dot_t(w_ref[at, :WIDTH], rows), theirs))
                top_ref[:, pl.ds(start, 256)] = top
        return carry

    lax.fori_loop(0, room // 256, step, 0)
    best = jnp.maximum(so_far_ref[...], slots([best_ref[256 * a : 256 * (a + 1), 0:1] for a in range(3)]))
    source = lanes[0:1, :room].astype(jnp.int32)
    here = (iota((CHIPS, room), 0) == source) & used[:, :room]
    rank = onehot((iota((room, 128), 1) == about_v[:, 1:2].astype(jnp.int32)) & (about_v[:, 2:3] > 0.5))
    placed = jnp.zeros((CHIPS, 128), F32)
    for piece in split3(jnp.where(here, top_ref[0:1, :], 0.0)):
        placed = placed + dot(piece, rank)
    filled = dot(onehot(here), rank)
    full = jnp.maximum(about_v[0:1, 3:4], about_w[0:1, 3:4])
    out = jnp.where(filled > 0.5, placed, best)
    out_ref[...] = jnp.where(iota((CHIPS, 128), 1) == 127, full, out)


def after_kernel(v_ref, best_ref, out_ref):
    pass


def after(v, best):
    anywhere = pl.BlockSpec(memory_space=pl.ANY)
    return pl.pallas_call(
        after_kernel,
        in_specs=[anywhere, anywhere],
        out_specs=anywhere,
        out_shape=jax.ShapeDtypeStruct(v.shape, v.dtype),
        input_output_aliases={0: 0},
        compiler_params=pltpu.CompilerParams(vmem_limit_bytes=MIB),
        name="overflow_after_own",
    )(v, best)


def owner_side(y, room):
    swap = [(0, 1), (1, 0)]
    mib = 28 if room <= 256 else 52
    slot_shape = jax.ShapeDtypeStruct((CHIPS, 128), F32)
    top_shape = jax.ShapeDtypeStruct((8, room), F32)
    tail_shape = jax.ShapeDtypeStruct((TAIL, WIDTH), BF16)
    packed_shape = jax.ShapeDtypeStruct((room, WIDTH + 128), BF16)
    s = lax.ppermute(y, "core", swap)
    v = call(pack_kernel, "pack_overflow", packed_shape, 3e9, y, mib=mib)
    v = lax.ppermute(v, "y", [(0, 1), (1, 0), (2, 3), (3, 2)])
    best, x2 = call(own_kernel, "own_pairs", [slot_shape, tail_shape], 5e9, y)
    best, s2 = call(cross_kernel, "cross_pairs", [slot_shape, tail_shape], 6e9, y, x2, s, best)
    v = after(v, best)
    w = lax.ppermute(v, "core", swap)
    top = call(received_kernel, "received_pairs", top_shape, 3e9, s, s2, v, best, mib=mib)
    scratch = [pltpu.VMEM((8, room), F32), pltpu.VMEM((ROWS + TAIL, 128), F32), pltpu.VMEM((8, 2 * room), F32)]
    return call(sibling_kernel, "sibling_pairs", slot_shape, 1e9, y, x2, v, w, best, top, mib=mib, scratch=scratch)


def pick_kernel(back_ref, rank_ref, out_ref, full_ref):
    rank = rank_ref[0:1, :]
    cluster = rank_ref[1:2, :]
    at_rank = onehot(iota((128, DOCS), 0) == rank)
    back = back_ref[...]
    found = jnp.zeros((CHIPS, DOCS), F32)
    for piece in split3(back):
        found = found + dot(piece, at_rank)
    out_ref[...] = jnp.sum(jnp.where(iota((CHIPS, DOCS), 0) == cluster, found, 0.0), axis=0, keepdims=True)
    full_ref[0, 0] = jnp.max(back[:, 127:128])


def return_to_source(best, rank):
    back = lax.all_to_all(best, CHIP_AXES, split_axis=0, concat_axis=0, tiled=True)
    return pl.pallas_call(
        pick_kernel,
        out_specs=[pl.BlockSpec(memory_space=pltpu.VMEM), pl.BlockSpec(memory_space=pltpu.SMEM)],
        out_shape=[jax.ShapeDtypeStruct((1, DOCS), F32), jax.ShapeDtypeStruct((1, 1), F32)],
        compiler_params=pltpu.CompilerParams(vmem_limit_bytes=4 * MIB),
        name="pick_documents",
    )(back, rank)


def next_chip(x, way, core):
    bits = 4 * core if way < 2 else 2
    unit = 1 << bits
    place = (iota(x.shape, 1) >> bits) & 3
    if way % 2 == 0:
        return jnp.where(place == 3, pltpu.roll(x, 3 * unit, axis=1), pltpu.roll(x, 128 - unit, axis=1))
    return jnp.where(place == 0, pltpu.roll(x, 128 - 3 * unit, axis=1), pltpu.roll(x, unit, axis=1))


def neighbour(z, x, y, way, core):
    step = 1 if way % 2 == 0 else 3
    if way < 2:
        y, z = jnp.where(core == 0, (y + step) & 3, y), jnp.where(core == 0, z, (z + step) & 3)
    else:
        x = (x + step) & 3
    return 16 * z + 4 * x + y


def spread_kernel(embed_hbm, group_hbm, half_hbm, out_ref, rank_ref, embed_ref, group_ref, half_ref, unit_ref, note_ref, slot_ref, sems):
    names = [pltpu.make_async_copy(group_hbm, group_ref, sems.at[0]), pltpu.make_async_copy(half_hbm, half_ref, sems.at[1])]
    size = DOCS // PARTS
    spans = [pl.ds(size * part, size) for part in range(PARTS)]
    parts = [pltpu.make_async_copy(embed_hbm.at[span, :], embed_ref.at[span, :], sems.at[2 + i]) for i, span in enumerate(spans)]
    for copy in names + parts:
        copy.start()
    for copy in names:
        copy.wait()
    group, half = group_ref[...], half_ref[...]
    z, x, y = ((group >> 4) + 2 * half) & 3, ((group >> 2) + 2 * half) & 3, (group + 2 * half) & 3
    home = 16 * z + 4 * x + y
    member = onehot((iota((2 * CHIPS, DOCS), 0) & (CHIPS - 1)) == home)
    earlier = onehot(iota((DOCS, DOCS), 0) < iota((DOCS, DOCS), 1))
    before = dot(member[:CHIPS], earlier)
    rank = jnp.sum(before * member[:CHIPS].astype(F32), axis=0, keepdims=True)
    counts = dot_t(jnp.ones((8, DOCS), BF16), member)
    left = jnp.maximum(counts - SLOTS, 0.0)
    free = SLOTS - jnp.minimum(counts, float(SLOTS))
    given = [jnp.zeros((8, 2 * CHIPS), F32) for _ in range(WAYS)]
    core = lax.axis_index("core")
    turn = (21 * lax.axis_index("z") + 5 * lax.axis_index("x") + lax.axis_index("y")) % 6
    early = jnp.where(turn < 3, 1.0, 0.0)
    plan = [(0, early), (1, 1.0), (0, 1.0 - early), (2, early), (3, 1.0), (2, 1.0 - early), (0, 1.0), (1, 1.0)]
    plan += [(d, 24.0) for d in range(WAYS)]
    for part, (copy, span) in enumerate(zip(parts, spans)):
        copy.wait()
        floats = embed_ref[span, :].astype(F32)
        scale = lax.rsqrt(jnp.sum(floats * floats, axis=1, keepdims=True) + 1e-06)
        unit_ref[span, :] = (floats * scale).astype(BF16)
        for d, most in plan[3 * part : 3 * part + 3]:
            take = jnp.minimum(jnp.minimum(left, next_chip(free, d, core)), most)
            given[d] = given[d] + take
            left = left - take
            free = free - next_chip(take, d ^ 1, core)
    ends, offsets = [], []
    total, used = jnp.zeros_like(left), jnp.zeros_like(left)
    for d in range(WAYS):
        total = total + given[d]
        ends.append(total)
        offsets.append(next_chip(used, d, core))
        used = used + next_chip(given[d], d ^ 1, core)
    table = jnp.concatenate([row[0:1] for row in ends + offsets] + [jnp.zeros((8, 2 * CHIPS), F32)], axis=0)
    table = jnp.where(iota(table.shape, 1) < CHIPS, table, 0.0)
    found = dot(table.astype(BF16), member)
    beyond = rank - SLOTS
    own = beyond < 0.0
    chip = home
    row = jnp.where(own, rank.astype(jnp.int32), -1)
    came = jnp.zeros((1, DOCS), F32)
    for d in range(WAYS):
        start = found[d - 1 : d] if d else jnp.zeros((1, DOCS), F32)
        this = (beyond >= start) & (beyond < found[d : d + 1])
        offset = found[WAYS + d : WAYS + d + 1]
        row = jnp.where(this, SLOTS - 1 - (offset + beyond - start).astype(jnp.int32), row)
        chip = jnp.where(this, neighbour(z, x, y, d, core), chip)
        came = jnp.where(this, d + 1.0, came)
    slot_ref[0:1, :] = jnp.where((row >= 0) & (row < HEAD), chip * HEAD + row, -1)
    slot_ref[1:2, :] = jnp.where(row >= HEAD, chip * HEAD + 4 * (row - HEAD), -8)
    rank_ref[0:1, :] = rank.astype(jnp.int32)
    rank_ref[1:2, :] = home
    lost = jnp.max(jnp.where(row < 0, 1.0, 0.0), axis=1, keepdims=True)
    line = iota((128, DOCS), 0)
    for part in range(2):
        at = line - 8 * part
        notes = jnp.where(at == 0, jnp.where(own, 1.0, 0.0), jnp.where(at == 1, came, jnp.where(at == 2, rank, 0.0)))
        note_ref[part] = jnp.where(at == 3, lost, notes).T.astype(BF16)

    at = iota((ROWS, DOCS), 0)
    whole = onehot(at == slot_ref[0:1, :])
    quarters = jnp.zeros((ROWS, QUARTER), F32)
    notes = dot(whole, note_ref[0])
    for q in range(4):
        span = slice(QUARTER * q, QUARTER * (q + 1))
        out_ref[:, span] = dot(whole, unit_ref[:, span]).astype(BF16)
        this = onehot(at == slot_ref[1:2, :] + q)
        quarters = quarters + dot(this, unit_ref[:, span])
        notes = notes + dot(this, note_ref[1])
    out_ref[:, WIDTH:NOTES] = quarters.astype(BF16)
    out_ref[:, NOTES:] = notes.astype(BF16)


def spread_documents(embed, group, half):
    far = pl.BlockSpec(memory_space=pltpu.HBM)
    operands = [pltpu.with_memory_space_constraint(x, pltpu.HBM) for x in (embed, group, half)]
    return pl.pallas_call(
        spread_kernel,
        in_specs=[far, far, far],
        out_shape=[jax.ShapeDtypeStruct((ROWS, FIRST), BF16), jax.ShapeDtypeStruct((8, DOCS), jnp.int32)],
        scratch_shapes=[
            pltpu.VMEM((DOCS, WIDTH), BF16),
            pltpu.VMEM((1, DOCS), jnp.int32),
            pltpu.VMEM((1, DOCS), jnp.int32),
            pltpu.VMEM((DOCS, WIDTH), BF16),
            pltpu.VMEM((2, DOCS, 128), BF16),
            pltpu.VMEM((8, DOCS), jnp.int32),
            pltpu.SemaphoreType.DMA((2 + PARTS,)),
        ],
        compiler_params=pltpu.CompilerParams(vmem_limit_bytes=28 * MIB),
        cost_estimate=pl.CostEstimate(flops=2 * 10**9, bytes_accessed=9 * 2**20, transcendentals=256),
        name="spread_documents",
    )(*operands)


def quarter_rows(y_ref, out_ref, first):
    to, at = iota((4 * REST, ROWS), 0), iota((4 * REST, ROWS), 1)
    row = to % REST
    want = (row % CHIPS) * HEAD + 4 * (row // CHIPS) + to // REST
    rows = dot(onehot(at == want), y_ref[:, WIDTH:NOTES]).astype(BF16)
    for q in range(4):
        out_ref[first : first + REST, QUARTER * q : QUARTER * (q + 1)] = rows[REST * q : REST * (q + 1)]


def at_home(y_ref):
    notes = y_ref[:, NOTES:].astype(F32).T[:16, :]
    at, to = iota((ROWS, REST), 0), iota((ROWS, REST), 1)
    pick = onehot(at == (to % CHIPS) * HEAD + 4 * (to // CHIPS))
    return notes[0:1, :] > 0.5, dot(notes[8:16, :].astype(BF16), pick)[0:1, :] > 0.5


def sort_kernel(y_ref, *v_refs):
    notes = y_ref[:, NOTES:].astype(F32).T[:16, :]
    quarter = iota((1, ROWS), 1) % 4
    ways = [notes[1:2, :] == d + 1.0 for d in range(WAYS)]
    ways += [(notes[9:10, :] == d + 1.0) & (quarter == q) for q in range(4) for d in range(WAYS)]
    flags = jnp.concatenate([jnp.where(way, 1.0, 0.0) for way in ways] + [jnp.zeros((4, ROWS), F32)], axis=0)
    before = onehot(iota((ROWS, ROWS), 0) < iota((ROWS, ROWS), 1))
    place = dot(flags.astype(BF16), before)
    sums = jnp.sum(flags, axis=1, keepdims=True)
    loads = [sums[d : d + 1] + sums[WAYS + d : WAYS + d + 1] - ROOMS[d] for d in range(WAYS)]
    most = functools.reduce(jnp.maximum, loads)
    lost = jnp.max(jnp.maximum(notes[3:4, :], notes[11:12, :]), axis=1, keepdims=True)
    full = jnp.where((most > 0.5) | (lost > 0.5), 1.0, 0.0)

    def take(first, shift):
        rows = []
        for d in range(WAYS):
            slot = iota((ROOMS[d], ROWS), 0)
            to = place[first + d : first + d + 1, :] + (sums[d : d + 1, :] if shift else 0.0)
            rows.append(jnp.where((slot == to.astype(jnp.int32)) & ways[first + d], 1.0, 0.0))
        return jnp.concatenate(rows, axis=0).astype(BF16)

    whole = take(0, False)
    lane = iota((ROWS, 128), 1)
    source = (iota((ROWS, 128), 0) // HEAD).astype(F32)
    extra = jnp.where(lane == 4, source, jnp.where(lane == 5, 1.0, 0.0))
    given = y_ref[:, NOTES:].astype(F32)
    info = dot(whole, jnp.where(lane == 2, given, extra).astype(BF16))
    some = jnp.concatenate([take(WAYS * (1 + q), True) for q in range(4)], axis=0)
    quarters = dot(some, y_ref[:, WIDTH:NOTES])
    for q in range(4):
        span = slice(QUARTER * q, QUARTER * (q + 1))
        rows = (dot(whole, y_ref[:, span]) + quarters[OVER * q : OVER * (q + 1)]).astype(BF16)
        for d in range(WAYS):
            v_refs[d][:, span] = rows[STARTS[d] : STARTS[d] + ROOMS[d]]
        if q == 0:
            moved = jnp.where(lane == 2, pltpu.roll(given, 128 - 8, axis=1), extra)
            info = info + dot(some[:OVER], moved.astype(BF16))
    info = jnp.where(iota((OVER, 128), 1) == 3, full, info).astype(BF16)
    for d in range(WAYS):
        v_refs[d][:, WIDTH:] = info[STARTS[d] : STARTS[d] + ROOMS[d]]


def to_slots(top, rest):
    keep = iota((ROWS, 128), 1) == iota((ROWS, 128), 0) % HEAD
    head = jnp.max(jnp.where(keep, top, -2.0).reshape(CHIPS, HEAD, 128), axis=1)
    keep = iota((REST, 128), 1) == iota((REST, 128), 0) // CHIPS + HEAD
    return jnp.maximum(head, jnp.max(jnp.where(keep, rest, -2.0).reshape(2, CHIPS, 128), axis=0))


def upright(line):
    return jnp.broadcast_to(line, (8, line.shape[1])).T[:, 0:1]


def lane_max(scores, keep):
    return jnp.max(jnp.where(keep, scores, -2.0), axis=1, keepdims=True)


def home_kernel(y_ref, best_ref):
    ok = y_ref[:, NOTES:].astype(F32).T[0:1, :] > 0.5
    here = y_ref[:, NOTES:].astype(F32)[:, 0:1] > 0.5
    low, high = y_ref[:256, :WIDTH], y_ref[256:, :WIDTH]
    both = dot_t(low, high)
    top0 = jnp.maximum(row_max(low, low, ok[:, :256] & off_diagonal(256)), lane_max(both, ok[:, 256:]))
    top1 = row_max(high, high, ok[:, 256:] & off_diagonal(256))
    top1 = jnp.maximum(top1, upright(column_max(both, here[:256])))
    best_ref[...] = jnp.broadcast_to(jnp.concatenate([top0, top1], axis=0), (ROWS, 128))


def other_core_kernel(y_ref, s_ref, so_far_ref, best_ref, rest_ref):
    quarter_rows(y_ref, rest_ref, 0)
    quarter_rows(s_ref, rest_ref, REST)
    (ok, ok2), (ok_s, ok_s2) = at_home(y_ref), at_home(s_ref)
    theirs = s_ref[:, :WIDTH]
    mine = rest_ref[:REST]
    upper = row_max(jnp.concatenate([y_ref[256:, :WIDTH], mine], axis=0), theirs, ok_s)
    tops = [row_max(y_ref[:256, :WIDTH], theirs, ok_s), upper[:256]]
    ok_rest = jnp.concatenate([jnp.where(ok2, 1.0, 0.0), jnp.where(ok_s2, 1.0, 0.0)], axis=1)
    scores = dot_t(rest_ref[...], y_ref[:, :WIDTH])
    beside = column_max(scores, upright(ok_rest) > 0.5)
    top = jnp.maximum(jnp.maximum(jnp.concatenate(tops, axis=0), upright(beside)), so_far_ref[:, 0:1])
    keep = (ok_rest > 0.5) & (iota((REST, 2 * REST), 0) != iota((REST, 2 * REST), 1))
    rest = jnp.maximum(lane_max(scores[:REST], ok), row_max(mine, rest_ref[...], keep))
    best_ref[...] = to_slots(top, jnp.maximum(rest, upper[256:]))


def join_kernel(*refs):
    out_ref = refs[-1]
    for d in range(WAYS):
        out_ref[STARTS[d] : STARTS[d] + ROOMS[d], :] = refs[d][...]


def notes_of(v_ref):
    return v_ref[:, WIDTH:].astype(F32).T[:8, :]


def guests_kernel(y_ref, s_ref, rest_ref, v_ref, so_far_ref, top_ref, own_ref):
    mine = v_ref[:, :WIDTH]
    used = v_ref[:, WIDTH:].astype(F32)[:, 5:6] > 0.5
    ok_v = notes_of(v_ref)[5:6, :] > 0.5
    top = row_max(mine, mine, ok_v & off_diagonal(OVER))
    (ok, ok2), (ok_s, ok_s2) = at_home(y_ref), at_home(s_ref)
    scores = dot_t(mine, y_ref[:, :WIDTH])
    own_ref[:, :ROWS] = jnp.broadcast_to(column_max(scores, used), (8, ROWS))
    top = jnp.maximum(top, lane_max(scores, ok))
    top = jnp.maximum(top, row_max(mine, s_ref[:, :WIDTH], ok_s))
    scores = dot_t(mine, rest_ref[...])
    own_ref[:, ROWS:] = jnp.broadcast_to(column_max(scores[:, :REST], used), (8, REST))
    top = jnp.maximum(top, jnp.maximum(lane_max(scores[:, :REST], ok2), lane_max(scores[:, REST:], ok_s2)))
    top_ref[...] = jnp.broadcast_to(top, (OVER, 128))


def finish_kernel(y_ref, rest_ref, v_ref, w_ref, so_far_ref, top_ref, own_ref, out_ref):
    about = v_ref[:, WIDTH:].astype(F32)
    about_w = w_ref[:, WIDTH:].astype(F32)
    lanes = notes_of(v_ref)
    theirs = w_ref[:, :WIDTH]
    used = about_w[:, 5:6] > 0.5
    head = jnp.maximum(own_ref[:, :ROWS], column_max(dot_t(theirs, y_ref[:, :WIDTH]), used))
    both = row_max(jnp.concatenate([rest_ref[:REST], v_ref[:, :WIDTH]], axis=0), theirs, notes_of(w_ref)[5:6, :] > 0.5)
    rest = jnp.maximum(own_ref[:, ROWS:].T[:, 0:1], both[:REST])
    best = jnp.maximum(so_far_ref[...], to_slots(head.T[:, 0:1], rest))
    top = jnp.maximum(top_ref[...], both[REST:])
    here = onehot((iota((CHIPS, OVER), 0) == lanes[4:5, :].astype(jnp.int32)) & (lanes[5:6, :] > 0.5))
    rank = (iota((OVER, 128), 1) == about[:, 2:3].astype(jnp.int32)) & (about[:, 5:6] > 0.5)
    pieces = dot(here, jnp.concatenate([*split3(jnp.where(rank, top, 0.0)), onehot(rank)], axis=1))
    placed = pieces[:, :128] + pieces[:, 128:256] + pieces[:, 256:384]
    filled = pieces[:, 384:]
    full = jnp.maximum(about[0:1, 3:4], about_w[0:1, 3:4])
    out = jnp.where(filled > 0.5, placed, best)
    out_ref[...] = jnp.where(iota((CHIPS, 128), 1) == 127, full, out)


def way_home(way):
    pairs = []
    for z, x, y, core in itertools.product(range(4), range(4), range(4), range(2)):
        to = [z, x, y]
        axis = 1 if way >= 2 else 2 if core == 0 else 0
        to[axis] = (to[axis] + (3 if way % 2 == 0 else 1)) % 4
        pairs.append((32 * z + 8 * x + 2 * y + core, 32 * to[0] + 8 * to[1] + 2 * to[2] + core))
    return pairs


def owner_short(y):
    swap = [(0, 1), (1, 0)]
    slot_shape = jax.ShapeDtypeStruct((CHIPS, 128), F32)
    rest_shape = jax.ShapeDtypeStruct((2 * REST, WIDTH), BF16)
    way_shapes = [jax.ShapeDtypeStruct((room, SHORT), BF16) for room in ROOMS]
    s = lax.ppermute(y, "core", swap)
    ways = call(sort_kernel, "sort_overflow", way_shapes, 3e9, y, mib=20)
    came = []
    for d, v in enumerate(ways):
        came.append(lax.ppermute(v, ALL_AXES, way_home(d)))
    best = call(home_kernel, "home_pairs", jax.ShapeDtypeStruct((ROWS, 128), F32), 1e10, y, mib=24)
    best, rest = call(other_core_kernel, "other_core_pairs", [slot_shape, rest_shape], 4e10, y, s, best, mib=24)
    v = call(join_kernel, "join_overflow", jax.ShapeDtypeStruct((OVER, SHORT), BF16), 1e8, *came, best, mib=8)
    w = lax.ppermute(v, "core", swap)
    shapes = [jax.ShapeDtypeStruct((OVER, 128), F32), jax.ShapeDtypeStruct((8, OWN), F32)]
    top, own = call(guests_kernel, "guest_pairs", shapes, 6e9, y, s, rest, v, best, mib=24)
    return call(finish_kernel, "finish_pairs", slot_shape, 3e9, y, rest, v, w, best, top, own, mib=24)


def wide_form(embed, group, half):
    sent, rank = place_documents(embed, group, half)
    y = lax.all_to_all(sent, CHIP_AXES, split_axis=0, concat_axis=0, tiled=True)
    return return_to_source(owner_side(y, ROWS + TAIL), rank)[0]


def on_device(embed, group, half):
    group, half = group.reshape(1, DOCS), half.reshape(1, DOCS)
    sent, rank = spread_documents(embed, group, half)
    y = lax.all_to_all(sent, CHIP_AXES, split_axis=0, concat_axis=0, tiled=True)
    nearest, full = return_to_source(owner_short(y), rank)
    nearest = lax.cond(
        full[0, 0] > 0.5,
        lambda embed, group, half, nearest: wide_form(embed, group, half),
        lambda embed, group, half, nearest: nearest,
        embed,
        group,
        half,
        nearest,
    )
    return nearest.reshape(DOCS)


def solution(mesh):
    devices = mesh.devices.reshape(4, 4, 4, 2)
    fine = Mesh(devices, ALL_AXES)
    return jax.shard_map(
        on_device,
        mesh=fine,
        in_specs=(P(ALL_AXES, None), P(ALL_AXES, None), P(ALL_AXES)),
        out_specs=P(ALL_AXES),
        check_vma=False,
    )
```
